32 devices in a mesh: hash: 4 (over y, core), dp: 8 (over z, x).
Axes of the slice: x: 2, y: 2, z: 4, core: 2. Of those that a mesh axis runs over, the one named last changes fastest.
Arguments:
- histories: bfloat16 [128, 256, 512], P(('hash', 'dp')), may hold values from -6 to 6
- weight_in: bfloat16 [512, 2048], replicated, may hold values from -0.25 to 0.25
- weight_out: bfloat16 [512, 512], replicated, may hold values from -0.25 to 0.25
- candidates: bfloat16 [8192, 512], P(('hash', 'dp')), may hold values from -6 to 6
- cotangent: bfloat16 [8192, 512], P(('hash', 'dp')), may hold values from -6 to 6
- owner_ids: int32 [8192, 1], P(('hash', 'dp')), may hold values from 0 to 31; in each aligned block of 256 rows (0 to 255, 256 to 511, ...) at most 16 rows name the same one
- hist_slot: int32 [8192], P(('hash', 'dp')), may hold values from 0 to 3
- lengths: int32 [8192], P(('hash', 'dp')), may hold values from 1 to 256
Outputs:
- history_grad: bfloat16 [128, 256, 512], P(('hash', 'dp'))
- candidate_grad: bfloat16 [8192, 512], P(('hash', 'dp'))
- weight_in_grad: float32 [512, 2048], P(('hash', 'dp'))
- weight_out_grad: float32 [512, 512], P(('hash', 'dp'))
The draws below stay inside these ranges and needn't reach their ends.
Inputs may be any that keep to these rules, and one draw needn't show every extreme that they name: `owner_ids`: in the rows of one device, at most 16 impressions name the same owner; the bound is reached.
All inputs are finite; a program needn't handle non-finite values.
Results may differ from the reference program's by a relative error of at most 0.012.
Values may be sent and summed in bfloat16 or wider, within the bound.
No kernel may reach another device: no remote copies, remote signals or barrier semaphores. Data moves between devices by JAX's collectives and lax.ppermute only.
A program may use at most 128 MiB of HBM per device.

```python
import math
import jax
import jax.numpy as jnp
import numpy as np
from jax import lax

D = 512
HEADS = 8
HEAD_DIM = 64
L = 256
HIST_DEV = 4
IMP_DEV = 256
CAP = 16
HIST = 128
IMP = 8192
DEVICES = 32


def touch_ends(result, own_key, least, top_value):
    place = [jax.random.randint(jax.random.fold_in(own_key, axis), (), 0, length) for axis, length in enumerate(result.shape)]
    longest = result.shape.index(max(result.shape))
    beside = place[:longest] + [(place[longest] + 1) % result.shape[longest]] + place[longest + 1:]
    return result.at[tuple(place)].set(least).at[tuple(beside)].set(top_value)


def level_of(own_key, extent, cuts, low, largest):
    factor_of = 1.0
    for axis_at, parts in cuts:
        heights = jax.random.uniform(jax.random.fold_in(jax.random.fold_in(own_key, 6), axis_at), (parts,), jnp.float32, low / len(cuts), largest / len(cuts))
        factor_of = factor_of * jnp.repeat(jnp.exp(heights), extent[axis_at] // parts).reshape((-1,) + (1,) * (len(extent) - 1 - axis_at))
    return factor_of


def shared_out(stream_key, own, number, rows, amount, top, most, slope):
    sequence = jax.random.permutation(stream_key, amount)
    heavy_load, usual = load_shares(amount, rows * top, most, slope, True), load_shares(amount, rows * top, most, slope, False)
    places = jnp.arange(amount)

    def named(sizes, turn):
        used = int((sizes > 0).sum())
        fixed = max(1, used // 4)
        passed = fixed + (places - fixed + turn * (used - fixed)) % max(1, amount - fixed)
        return jnp.zeros((amount,), jnp.int32).at[sequence[jnp.where(places < fixed, places, passed)]].set(jnp.asarray(sizes, jnp.int32))

    sizes = jnp.where(number % 4 == 0, named(heavy_load, number // 4), named(usual, number - number // 4 - 1))
    mixed = jax.random.permutation(jax.random.fold_in(own, 3), amount)
    donor, sink = mixed[0:amount // 2 * 2:2], mixed[1:amount // 2 * 2:2]
    margin = jnp.minimum(sizes[donor] - 1, most - sizes[sink]) // 2
    margin = jnp.where((donor == sequence[0]) | (sink == sequence[0]) | (sizes[sink] == 0), 0, jnp.maximum(margin, 0))
    passed = jax.random.randint(jax.random.fold_in(own, 4), (amount // 2,), 0, 1 << 20) % (margin + 1)
    sizes = sizes.at[donor].add(-passed).at[sink].add(passed)
    items = jnp.searchsorted(jnp.cumsum(sizes), jnp.arange(rows * top), side="right").astype(jnp.int32)
    grid = items.reshape(top, rows).T
    grid = grid[jax.random.permutation(jax.random.fold_in(own, 1), rows)]
    turn = jax.random.randint(jax.random.fold_in(own, 2), (rows, 1), 0, top)
    return jnp.take_along_axis(grid, (jnp.arange(top)[None, :] + turn) % top, axis=1)


def load_shares(count, total, reach, skew, full):
    portions = [(1 << 20) // math.isqrt(grade ** skew) + 1 for grade in range(1, count + 1)]
    largest = reach if full else min(reach, max(-(-total // count), total * portions[0] // sum(portions)))
    least = 1 if total - largest >= count - 1 else 0
    given, rest = [largest] + [least] * (count - 1), total - largest - least * (count - 1)
    while rest > 0:
        free = [i for i in range(1, count) if given[i] < largest] or [i for i in range(1, count) if given[i] < reach]
        mass, budget = sum([portions[i] for i in free]), rest
        for i in free:
            addition = min(reach - given[i], max(1, budget * portions[i] // mass), rest)
            given[i] = given[i] + addition
            rest = rest - addition
    return np.array(given)


def normal_values(key, extent, width, reach, shards=(), held_as=jnp.bfloat16):
    values = jax.random.normal(key, extent, jnp.float32) * width
    if len(shards) > 0:
        values = level_of(key, extent, shards, -0.22, 0.18) * values
    return jnp.clip(values, min=-reach, max=reach).astype(held_as)


def setup_inputs(seed: int = 0) -> dict:
    key_list = jax.random.split(jax.random.key(seed), 9)
    histories = normal_values(key_list[0], (HIST, L, D), 1.0, 6.0, ((0, 32),))
    weight_in = normal_values(key_list[1], (D, 4 * D), D ** -0.5, 0.25)
    weight_out = normal_values(key_list[2], (D, D), D ** -0.5, 0.25)
    candidates = normal_values(key_list[3], (IMP, D), 1.0, 6.0, ((0, 32),))
    cotangent = normal_values(key_list[4], (IMP, D), 1.0, 6.0, ((0, 32),))
    owner_ids_keys = jax.random.split(jax.random.fold_in(key_list[5], 1), IMP // IMP_DEV)
    owner_ids_turns = jax.random.permutation(jax.random.fold_in(key_list[5], 3), IMP // IMP_DEV)
    owner_ids = jax.vmap(lambda own, number: shared_out(jax.random.fold_in(key_list[5], 2), own, number, IMP_DEV, DEVICES, 1, CAP, 2))(owner_ids_keys, owner_ids_turns).reshape((IMP, 1))
    hist_slot = touch_ends(jax.random.randint(key_list[6], (IMP,), 0, HIST_DEV), jax.random.fold_in(key_list[6], 1), 0, HIST_DEV - 1).astype(jnp.int32)
    lengths = touch_ends(jax.random.randint(key_list[7], (IMP,), 1, L + 1), jax.random.fold_in(key_list[7], 1), 1, L).astype(jnp.int32)
    return {"histories": histories, "weight_in": weight_in, "weight_out": weight_out, "candidates": candidates, "cotangent": cotangent, "owner_ids": owner_ids, "hist_slot": hist_slot, "lengths": lengths}


norm_eps = 1e-05

def silu_grad(argument):
    sigmoid_v = jax.nn.sigmoid(argument)
    return sigmoid_v * (1.0 + argument * (1.0 - sigmoid_v))

def contract_rows(left_mat, right_mat):
    return lax.dot_general(left_mat, right_mat, (((0,), (0,)), ((), ())), preferred_element_type=jnp.float32)

def contract_cols(left_mat, right_mat):
    return lax.dot_general(left_mat, right_mat, (((1,), (1,)), ((), ())), preferred_element_type=jnp.float32)

def rounded(argument):
    return lax.optimization_barrier(argument.astype(jnp.bfloat16)).astype(jnp.float32)

def causal_table(seq_len):
    positions = jnp.arange(seq_len, dtype=jnp.int32)
    return (positions[:, None] >= positions[None, :]).astype(jnp.float32) / seq_len

def layer_forward(inputs, weight_in, weight_out):
    num_hist, seq_len, model_width = inputs.shape
    head_dim = model_width // HEADS
    flat_rows = inputs.reshape(num_hist * seq_len, model_width)
    pre_act = jnp.dot(flat_rows, weight_in, preferred_element_type=jnp.float32)
    activated = jax.nn.silu(pre_act)
    gate_u = activated[:, :model_width]
    proj_f = rounded(activated[:, model_width:])
    head_shape = (num_hist, seq_len, HEADS, head_dim)
    values = proj_f[:, :model_width].reshape(head_shape)
    queries = proj_f[:, model_width:2 * model_width].reshape(head_shape)
    keys_f = proj_f[:, 2 * model_width:].reshape(head_shape)
    score_scale = head_dim ** (-0.5)
    scores = jnp.einsum('bqhe,bkhe->bhqk', queries, keys_f) * score_scale
    attn_f = rounded(jax.nn.silu(scores) * causal_table(seq_len))
    mixed_rows = jnp.einsum('bhqk,bkhe->bqhe', attn_f, values).reshape(num_hist * seq_len, model_width)
    centred = mixed_rows - lax.optimization_barrier(jnp.mean(mixed_rows, axis=1, keepdims=True))
    inv_std = lax.rsqrt(lax.optimization_barrier(jnp.mean(centred * centred, axis=1, keepdims=True)) + norm_eps)
    normed = centred * inv_std
    merged = (normed * gate_u).astype(jnp.bfloat16)
    output = flat_rows.astype(jnp.float32) + jnp.dot(merged, weight_out, preferred_element_type=jnp.float32)
    saved_state = (pre_act, gate_u, values, queries, keys_f, scores, attn_f, normed, inv_std, merged)
    return (output.astype(jnp.bfloat16).reshape(inputs.shape), saved_state)

def layer_backward(inputs, weight_in, weight_out, saved_state, d_out):
    num_hist, seq_len, model_width = inputs.shape
    head_dim = model_width // HEADS
    flat_count = num_hist * seq_len
    pre_act, gate_u, values, queries, keys_f, scores, attn_f, normed, inv_std, merged = saved_state
    flat_rows = inputs.reshape(flat_count, model_width)
    d_rows = d_out.reshape(flat_count, model_width)
    w_out_part = contract_rows(merged, d_rows)
    d_merged = contract_cols(d_rows, weight_out)
    d_gate = d_merged * normed
    d_norm = d_merged * gate_u
    d_mixed = inv_std * (d_norm - lax.optimization_barrier(jnp.mean(d_norm, axis=1, keepdims=True)) - normed * lax.optimization_barrier(jnp.mean(d_norm * normed, axis=1, keepdims=True)))
    d_mixed_f = rounded(d_mixed).reshape(num_hist, seq_len, HEADS, head_dim)
    d_attn = jnp.einsum('bqhe,bkhe->bhqk', d_mixed_f, values)
    d_values = jnp.einsum('bhqk,bqhe->bkhe', attn_f, d_mixed_f)
    score_scale = head_dim ** (-0.5)
    d_scores = rounded(d_attn * silu_grad(scores) * causal_table(seq_len) * score_scale)
    d_queries = jnp.einsum('bhqk,bkhe->bqhe', d_scores, keys_f)
    d_keys = jnp.einsum('bhqk,bqhe->bkhe', d_scores, queries)
    d_act = jnp.concatenate([d_gate, d_values.reshape(flat_count, model_width), d_queries.reshape(flat_count, model_width), d_keys.reshape(flat_count, model_width)], axis=1)
    d_pre = (d_act * silu_grad(pre_act)).astype(jnp.bfloat16)
    w_in_part = contract_rows(flat_rows, d_pre)
    d_inputs = (d_rows.astype(jnp.float32) + contract_cols(d_pre, weight_in)).astype(jnp.bfloat16)
    return (d_inputs.reshape(inputs.shape), w_in_part, w_out_part)

def reference(histories, weight_in, weight_out, candidates, cotangent, owner_ids, hist_slot, lengths):
    groups = HIST // HIST_DEV
    grouped = histories.reshape(groups, HIST_DEV, L, D)
    encoded = lax.map(lambda block_in: layer_forward(block_in, weight_in, weight_out)[0], grouped)
    encoded = encoded.reshape(HIST, L, D)
    hist_index = (owner_ids[:, 0] * HIST_DEV + hist_slot).astype(jnp.int32)
    block_rows = min(128, IMP)
    block_count = IMP // block_rows
    positions = jnp.arange(L, dtype=jnp.int32)
    score_scale = HEAD_DIM ** (-0.5)

    def target_block(running, block_in):
        index_b, cand_b, cot_b, len_b = block_in
        keys_b = encoded[index_b].astype(jnp.float32).reshape(block_rows, L, HEADS, HEAD_DIM)
        query_b = cand_b.astype(jnp.float32).reshape(block_rows, HEADS, HEAD_DIM)
        grad_b = cot_b.astype(jnp.float32).reshape(block_rows, HEADS, HEAD_DIM)
        inverse = 1.0 / len_b.astype(jnp.float32)
        weight_b = (positions[None, :] < len_b[:, None]).astype(jnp.float32) * inverse[:, None]
        weight_b = weight_b[:, None, :]
        scores_b = jnp.einsum('bhe,blhe->bhl', query_b, keys_b) * score_scale
        attn_b = rounded(jax.nn.silu(scores_b) * weight_b)
        d_attn_b = jnp.einsum('bhe,blhe->bhl', grad_b, keys_b)
        d_scores_b = rounded(d_attn_b * silu_grad(scores_b) * weight_b * score_scale)
        d_query_b = jnp.einsum('bhl,blhe->bhe', d_scores_b, keys_b).reshape(block_rows, D).astype(jnp.bfloat16)
        d_keys_b = jnp.einsum('bhl,bhe->blhe', attn_b, grad_b) + jnp.einsum('bhl,bhe->blhe', d_scores_b, query_b)
        running = running.at[index_b].add(d_keys_b.reshape(block_rows, L, D))
        return (running, d_query_b)
    blocks = (hist_index.reshape(block_count, block_rows), candidates.reshape(block_count, block_rows, D), cotangent.reshape(block_count, block_rows, D), lengths.reshape(block_count, block_rows))
    d_encoded, cand_grads = lax.scan(target_block, jnp.zeros((HIST, L, D), jnp.float32), blocks)
    d_encoded = d_encoded.astype(jnp.bfloat16).reshape(groups, HIST_DEV, L, D)

    def layer_block(running, block_in):
        inputs_b, d_out_b = block_in
        _, saved_state = layer_forward(inputs_b, weight_in, weight_out)
        d_inputs, w_in_part, w_out_part = layer_backward(inputs_b, weight_in, weight_out, saved_state, d_out_b)
        return ((running[0] + w_in_part, running[1] + w_out_part), d_inputs)
    start = (jnp.zeros((D, 4 * D), jnp.float32), jnp.zeros((D, D), jnp.float32))
    (w_in_total, w_out_total), history_grad = lax.scan(layer_block, start, (grouped, d_encoded))
    return (history_grad.reshape(HIST, L, D), cand_grads.reshape(IMP, D), w_in_total, w_out_total)
```

```python
import functools

import jax
import jax.numpy as jnp
from jax import lax
from jax.experimental import pallas as pl
from jax.experimental.pallas import tpu as pltpu
from jax.sharding import PartitionSpec as P

HEADS = 8
TILE = 128
META = 128
AXES = ("hash_hi", "core", "dp_hi", "dp_lo")
norm_eps = 1e-05
f32 = jnp.float32
bf16 = jnp.bfloat16
MIB = 1024 * 1024


def dot_nn(a, b):
    return lax.dot_general(a, b, (((1,), (0,)), ((), ())), preferred_element_type=f32)


def dot_nt(a, b):
    return lax.dot_general(a, b, (((1,), (1,)), ((), ())), preferred_element_type=f32)


def dot_tn(a, b):
    return lax.dot_general(a, b, (((0,), (0,)), ((), ())), preferred_element_type=f32)


def iota(shape, axis):
    return lax.broadcasted_iota(jnp.int32, shape, axis)


def silu_pair(half):
    t = jnp.tanh(half)
    u = 1.0 + t
    act = half * u
    return act, u + act * (1.0 - t)


def lane_masks(width, part):
    lane = iota((1, width), 1)
    return [((lane >= j * part) & (lane < (j + 1) * part)).astype(bf16) for j in range(width // part)]


def both_heads(pair, masks):
    return jnp.concatenate([pair * m for m in masks], axis=0)


def pick_lanes(stacked, head):
    rows = stacked.shape[0] // 2
    lane = iota((1, 2 * head), 1)
    return jnp.where(lane < head, stacked[:rows], stacked[rows:])


def params(mib):
    return pltpu.CompilerParams(dimension_semantics=("arbitrary",), vmem_limit_bytes=mib * MIB)


def whole(shape):
    return pl.BlockSpec(shape, lambda i: (0,) * len(shape))


def cost(flops, nbytes, trans=0):
    return pl.CostEstimate(flops=int(flops), bytes_accessed=int(nbytes), transcendentals=int(trans))


def route_kernel(devices, capacity, own_ref, slot_ref, len_ref, cand_ref, cot_ref, send_ref, pick_ref):
    rows, width = cand_ref.shape
    slots = devices * capacity
    own = own_ref[...]
    hot = (own == iota((devices, rows), 0)).astype(f32)
    before = (iota((rows, rows), 0) < iota((rows, rows), 1)).astype(f32).astype(bf16)
    earlier = dot_nn(hot.astype(bf16), before)
    position = jnp.sum(earlier * hot, axis=0, keepdims=True).astype(jnp.int32)
    target = own * capacity + position
    pick = (target == iota((slots, rows), 0)).astype(f32).astype(bf16)
    pick_ref[...] = pick
    send_ref[:, :width] = dot_nn(pick, cand_ref[...]).astype(bf16)
    send_ref[:, width : 2 * width] = dot_nn(pick, cot_ref[...]).astype(bf16)
    line = iota((META, rows), 0)
    meta = jnp.where(line == 0, slot_ref[...], jnp.where(line == 1, len_ref[...], 0))
    send_ref[:, 2 * width :] = dot_nt(pick, meta.astype(f32).astype(bf16)).astype(bf16)


def route(own, slot, length, cand, cot, devices, capacity):
    rows, width = cand.shape
    slots = devices * capacity
    line = whole((1, rows))
    return pl.pallas_call(
        functools.partial(route_kernel, devices, capacity),
        grid=(1,),
        in_specs=[line, line, line, whole(cand.shape), whole(cot.shape)],
        out_specs=[whole((slots, 2 * width + META)), whole((slots, rows))],
        out_shape=(
            jax.ShapeDtypeStruct((slots, 2 * width + META), bf16),
            jax.ShapeDtypeStruct((slots, rows), bf16),
        ),
        compiler_params=params(60),
        cost_estimate=cost(2e9, 4 * rows * width * 4),
        name="route",
    )(own.reshape(1, rows), slot.reshape(1, rows), length.reshape(1, rows), cand, cot)


def forward_kernel(
    x_ref, win_ref, wout_ref, perm_ref,
    enc_ref, slope_ref, slope_t_ref, v_ref, q_ref, k_ref, q_t_ref, attn_t_ref, grad_ref,
    normed_ref, nu_ref, gi_ref, xt_ref, mt_ref,
    gate_ref, mixed_ref,
):
    seq, width = x_ref.shape[1:]
    head = width // HEADS
    half_seq = seq // 2
    x = x_ref[0]
    for branch in range(4):
        cols = slice(branch * width, (branch + 1) * width)
        act, slope = silu_pair(0.5 * dot_nn(x, win_ref[:, cols]))
        if branch == 3:
            slope_t_ref[0] = jnp.transpose(0.5 * slope).astype(bf16)
        else:
            slope_ref[0, :, cols] = (0.5 * slope).astype(bf16)
        if branch == 0:
            gate_ref[...] = act
        else:
            (v_ref, q_ref, k_ref)[branch - 1][0] = act.astype(bf16)
        if branch == 2:
            q_t_ref[0] = jnp.transpose(act).astype(bf16)
    masks = lane_masks(2 * head, head)
    scale = 0.5 * head**-0.5
    tri = iota((half_seq, half_seq), 0) >= iota((half_seq, half_seq), 1)
    zero = jnp.zeros((half_seq, half_seq), f32)
    for pair in range(HEADS // 2):
        cols = slice(pair * 2 * head, (pair + 1) * 2 * head)
        q_p = q_ref[0, :, cols] * jnp.asarray(scale, bf16)
        half = dot_nt(both_heads(q_p, masks), k_ref[0, :, cols])
        stack = []
        for j in range(2):
            h = 2 * pair + j
            top = silu_pair(half[j * seq : j * seq + half_seq, :half_seq])
            bot = silu_pair(half[j * seq + half_seq : (j + 1) * seq])
            full = []
            for a, b in zip(top, bot):
                a = jnp.concatenate([jnp.where(tri, a, 0.0), zero], axis=1)
                b = jnp.concatenate([b[:, :half_seq], jnp.where(tri, b[:, half_seq:], 0.0)], axis=1)
                full.append(jnp.concatenate([a, b], axis=0))
            stack.append(full[0].astype(bf16))
            attn_t_ref[0, h] = jnp.transpose(full[0]).astype(bf16)
            grad_ref[0, h] = full[1].astype(bf16)
        mixed = dot_nn(jnp.concatenate(stack, axis=0), v_ref[0, :, cols])
        mixed_ref[:, cols] = pick_lanes(mixed, head) * (1.0 / seq)
    mixed = mixed_ref[...]
    centred = mixed - jnp.mean(mixed, axis=1, keepdims=True)
    inv_std = lax.rsqrt(jnp.mean(centred * centred, axis=1, keepdims=True) + norm_eps)
    normed = centred * inv_std
    gate = gate_ref[...]
    merged = (normed * gate).astype(bf16)
    normed_ref[0] = normed.astype(bf16)
    nu_ref[0] = (normed * slope_ref[0, :, :width].astype(f32)).astype(bf16)
    gi_ref[0] = (gate * inv_std).astype(bf16)
    enc_ref[0] = (x.astype(f32) + dot_nn(merged, wout_ref[...])).astype(bf16)
    perm = perm_ref[...]
    xt_ref[...] = dot_nt(perm, x).astype(bf16)
    mt_ref[...] = dot_nt(perm, merged).astype(bf16)


def layer_forward(x, w_in, w_out, perm):
    hist, seq, width = x.shape
    row = pl.BlockSpec((1, seq, width), lambda i: (i, 0, 0))
    wide = pl.BlockSpec((1, seq, 3 * width), lambda i: (i, 0, 0))
    column = pl.BlockSpec((1, width, seq), lambda i: (i, 0, 0))
    square = pl.BlockSpec((1, HEADS, seq, seq), lambda i: (i, 0, 0, 0))
    turned = pl.BlockSpec((width, seq), lambda i: (0, i))
    row_s = jax.ShapeDtypeStruct((hist, seq, width), bf16)
    column_s = jax.ShapeDtypeStruct((hist, width, seq), bf16)
    square_s = jax.ShapeDtypeStruct((hist, HEADS, seq, seq), bf16)
    turned_s = jax.ShapeDtypeStruct((width, hist * seq), bf16)
    return pl.pallas_call(
        forward_kernel,
        grid=(hist,),
        in_specs=[row, whole(w_in.shape), whole(w_out.shape), whole(perm.shape)],
        out_specs=[
            row, wide, column, row, row, row, column, square, square, row, row, row, turned, turned,
        ],
        out_shape=[
            row_s, jax.ShapeDtypeStruct((hist, seq, 3 * width), bf16), column_s, row_s, row_s, row_s,
            column_s, square_s, square_s, row_s, row_s, row_s, turned_s, turned_s,
        ],
        scratch_shapes=[pltpu.VMEM((seq, width), f32), pltpu.VMEM((seq, width), f32)],
        compiler_params=params(60),
        cost_estimate=cost(18e9, 24e6),
        name="forward",
    )(x, w_in, w_out, perm)


def target_kernel(recv_ref, enc_ref, dq_ref, denc_ref, grouped_ref, turned_ref):
    hist, seq, width = enc_ref.shape
    slots = recv_ref.shape[0]
    padded = grouped_ref.shape[0]
    head = width // HEADS
    meta = recv_ref[:, 2 * width :].astype(f32)
    slot_h = meta[:, 0:1]
    valid = meta[:, 1:2] > 0.0
    lane = iota((slots, META), 1).astype(f32)
    hot = jnp.where(valid & (slot_h == lane), 1.0, 0.0)
    lower = (iota((slots, slots), 0) > iota((slots, slots), 1)).astype(f32).astype(bf16)
    rank = jnp.sum(dot_nn(lower, hot.astype(bf16)) * hot, axis=1, keepdims=True)
    starts, start = [], jnp.int32(0)
    begin = jnp.zeros((slots, 1), f32)
    for h in range(hist):
        starts.append(start)
        begin = jnp.where(slot_h == float(h), (start * TILE).astype(f32), begin)
        count = jnp.sum(hot[:, h : h + 1]).astype(jnp.int32)
        start = start + (count + (TILE - 1)) // TILE
    tiles = start
    dest = jnp.where(valid, begin + rank, -1.0)
    eye = iota((slots, slots), 0) == iota((slots, slots), 1)
    dest_row = jnp.sum(jnp.where(eye, dest, 0.0), axis=0, keepdims=True).astype(jnp.int32)
    dest_col = dest.astype(jnp.int32)
    grouped_ref[...] = jnp.zeros_like(grouped_ref)
    turned_ref[...] = jnp.zeros_like(turned_ref)
    masks = lane_masks(2 * head, head)
    scale = 0.5 * head**-0.5
    positions = iota((TILE, seq), 1).astype(f32)

    def one_tile(tile, carry):
        base = pl.multiple_of(tile * TILE, TILE)
        hist_t = jnp.int32(0)
        for h in range(1, hist):
            hist_t = hist_t + (tile >= starts[h]).astype(jnp.int32)
        choose = (iota((TILE, slots), 0) + base == dest_row).astype(f32).astype(bf16)
        rows = dot_nn(choose, recv_ref[...])
        q_all = rows[:, :width] * scale
        g_all = rows[:, width : 2 * width]
        q_t = jnp.transpose(q_all).astype(bf16)
        g_t = jnp.transpose(g_all).astype(bf16)
        q_all = q_all.astype(bf16)
        g_all = g_all.astype(bf16)
        length = rows[:, 2 * width + 1 : 2 * width + 2]
        weight = jnp.where(positions < length, 1.0 / jnp.maximum(length, 1.0), 0.0)
        for pair in range(HEADS // 2):
            cols = slice(pair * 2 * head, (pair + 1) * 2 * head)
            k_p = enc_ref[hist_t, :, cols]
            both = dot_nt(
                jnp.concatenate(
                    [both_heads(q_all[:, cols], masks), both_heads(g_all[:, cols], masks)], axis=0
                ),
                k_p,
            )
            slopes = []
            for j in range(2):
                h = 2 * pair + j
                mine = slice(h * head, (h + 1) * head)
                act, slope = silu_pair(both[j * TILE : (j + 1) * TILE])
                d_attn = both[(2 + j) * TILE : (3 + j) * TILE]
                attn = (act * weight).astype(bf16)
                d_s = (d_attn * weight * slope).astype(bf16)
                turned_ref[hist_t, mine, :] += dot_nn(
                    jnp.concatenate([g_t[mine], q_t[mine]], axis=1),
                    jnp.concatenate([attn, d_s], axis=0),
                )
                slopes.append(d_s)
            d_q = pick_lanes(dot_nn(jnp.concatenate(slopes, axis=0), k_p), head)
            grouped_ref[pl.ds(base, TILE), cols] = (d_q * scale).astype(bf16)
        return carry

    lax.fori_loop(0, tiles, one_tile, 0)
    back = (dest_col == iota((slots, padded), 1)).astype(f32).astype(bf16)
    dq_ref[...] = dot_nn(back, grouped_ref[...]).astype(bf16)
    for h in range(hist):
        denc_ref[h] = jnp.transpose(turned_ref[h]).astype(bf16)


def target_backward(recv, enc):
    hist, seq, width = enc.shape
    slots = recv.shape[0]
    padded = ((slots - hist) // TILE + hist) * TILE
    return pl.pallas_call(
        target_kernel,
        grid=(1,),
        in_specs=[whole(recv.shape), whole(enc.shape)],
        out_specs=[whole((slots, width)), whole(enc.shape)],
        out_shape=(
            jax.ShapeDtypeStruct((slots, width), bf16),
            jax.ShapeDtypeStruct(enc.shape, bf16),
        ),
        scratch_shapes=[pltpu.VMEM((padded, width), bf16), pltpu.VMEM((hist, width, seq), f32)],
        compiler_params=params(60),
        cost_estimate=cost(12e9, 4e6),
        name="target",
    )(recv, enc)


def backward_kernel(
    denc_ref, wout_ref, normed_ref, nu_ref, gi_ref, v_ref, k_ref, q_t_ref, attn_t_ref, grad_ref,
    sv_ref, sq_ref, sk_ref, xt_hbm, mt_hbm,
    dpre_ref, dk_ref, keep_ref, send_ref,
    xt_ref, mt_ref, all_ref, all_k_ref, all_enc_ref, dmix_ref, sem_ref,
):
    step = pl.program_id(0)
    seq, width = denc_ref.shape[1:]
    head = width // HEADS
    kept = keep_ref.shape[0]
    copies = [
        pltpu.make_async_copy(xt_hbm, xt_ref, sem_ref.at[0]),
        pltpu.make_async_copy(mt_hbm, mt_ref, sem_ref.at[1]),
    ]

    @pl.when(step == 0)
    def _():
        for copy in copies:
            copy.start()

    here = pl.ds(pl.multiple_of(step * seq, seq), seq)
    d_enc = denc_ref[0]
    all_enc_ref[here, :] = d_enc
    d_merged = dot_nt(d_enc, wout_ref[...])
    d_pre = (d_merged * nu_ref[0].astype(f32)).astype(bf16)
    dpre_ref[0, :, :width] = d_pre
    all_ref[here, :width] = d_pre
    normed = normed_ref[0].astype(f32)
    d_norm = d_merged * gi_ref[0].astype(f32)
    d_mix = (
        d_norm
        - jnp.mean(d_norm, axis=1, keepdims=True)
        - normed * jnp.mean(d_norm * normed, axis=1, keepdims=True)
    )
    dmix_ref[...] = d_mix.astype(bf16)
    masks = lane_masks(2 * head, head)
    scale = 0.5 * head**-0.5 / seq
    for pair in range(HEADS // 2):
        cols = slice(pair * 2 * head, (pair + 1) * 2 * head)
        d_p = dmix_ref[:, cols]
        d_attn = dot_nt(both_heads(d_p, masks), v_ref[0, :, cols])
        d_s = [
            (d_attn[j * seq : (j + 1) * seq] * grad_ref[0, 2 * pair + j].astype(f32)).astype(bf16)
            for j in range(2)
        ]
        attn_t = jnp.concatenate([attn_t_ref[0, 2 * pair], attn_t_ref[0, 2 * pair + 1]], axis=0)
        d_v = pick_lanes(dot_nn(attn_t, d_p), head) * (1.0 / seq)
        d_q = pick_lanes(dot_nn(jnp.concatenate(d_s, axis=0), k_ref[0, :, cols]), head) * scale
        for branch, grad, slope_ref in ((1, d_v, sv_ref), (2, d_q, sq_ref)):
            at = slice(branch * width + pair * 2 * head, branch * width + (pair + 1) * 2 * head)
            d_pre = (grad * slope_ref[0, :, cols].astype(f32)).astype(bf16)
            dpre_ref[0, :, at] = d_pre
            all_ref[here, at] = d_pre
        for j in range(2):
            mine = slice((2 * pair + j) * head, (2 * pair + j + 1) * head)
            d_k = dot_nn(q_t_ref[0, mine], d_s[j]) * scale
            d_pre = (d_k * sk_ref[0, mine].astype(f32)).astype(bf16)
            dk_ref[0, mine] = d_pre
            all_k_ref[mine, here] = d_pre

    @pl.when(step == pl.num_programs(0) - 1)
    def _():
        for copy in copies:
            copy.wait()
        for block in range(5):
            cols = slice(block * width, (block + 1) * width)
            if block == 0:
                part = dot_nn(mt_ref[...], all_enc_ref[...])
            elif block == 4:
                part = dot_nt(xt_ref[...], all_k_ref[...])
            else:
                part = dot_nn(xt_ref[...], all_ref[:, (block - 1) * width : block * width])
            keep_ref[:, cols] = part[:kept].astype(bf16)
            send_ref[:, cols] = part[kept:].astype(bf16)


def layer_backward(denc, w_out, state, xt, mt, kept):
    hist, seq, width = denc.shape
    normed, nu, gi, v, k, q_t, attn_t, grad, slope, slope_t = state
    row = pl.BlockSpec((1, seq, width), lambda i: (i, 0, 0))
    column = pl.BlockSpec((1, width, seq), lambda i: (i, 0, 0))
    slope_spec = lambda b: pl.BlockSpec((1, seq, width), lambda i: (i, 0, b))
    square = pl.BlockSpec((1, HEADS, seq, seq), lambda i: (i, 0, 0, 0))
    raw = pl.BlockSpec(memory_space=pl.ANY)
    rows = hist * seq
    return pl.pallas_call(
        backward_kernel,
        grid=(hist,),
        in_specs=[
            row, whole(w_out.shape), row, row, row, row, row, column, square, square,
            slope_spec(1), slope_spec(2), column, raw, raw,
        ],
        out_specs=[
            pl.BlockSpec((1, seq, 3 * width), lambda i: (i, 0, 0)),
            column,
            whole((kept, 5 * width)),
            whole((width - kept, 5 * width)),
        ],
        out_shape=[
            jax.ShapeDtypeStruct((hist, seq, 3 * width), bf16),
            jax.ShapeDtypeStruct((hist, width, seq), bf16),
            jax.ShapeDtypeStruct((kept, 5 * width), bf16),
            jax.ShapeDtypeStruct((width - kept, 5 * width), bf16),
        ],
        scratch_shapes=[
            pltpu.VMEM((width, rows), bf16),
            pltpu.VMEM((width, rows), bf16),
            pltpu.VMEM((rows, 3 * width), bf16),
            pltpu.VMEM((width, rows), bf16),
            pltpu.VMEM((rows, width), bf16),
            pltpu.VMEM((seq, width), bf16),
            pltpu.SemaphoreType.DMA((2,)),
        ],
        compiler_params=params(60),
        cost_estimate=cost(22e9, 30e6),
        name="layer_backward",
    )(denc, w_out, normed, nu, gi, v, k, q_t, attn_t, grad, slope, slope, slope_t, xt, mt)


def input_kernel(denc_ref, win_ref, dpre_ref, dk_ref, out_ref):
    width = denc_ref.shape[2]
    total = denc_ref[0].astype(f32) + dot_nt(dpre_ref[0], win_ref[:, : 3 * width])
    total = total + dot_nt(jnp.transpose(dk_ref[0]), win_ref[:, 3 * width :])
    out_ref[0] = total.astype(bf16)


def input_backward(denc, w_in, dpre, dk):
    hist, seq, width = denc.shape
    block = lambda a: pl.BlockSpec((1,) + a.shape[1:], lambda i: (i, 0, 0))
    return pl.pallas_call(
        input_kernel,
        grid=(hist,),
        in_specs=[block(denc), whole(w_in.shape), block(dpre), block(dk)],
        out_specs=block(denc),
        out_shape=jax.ShapeDtypeStruct(denc.shape, bf16),
        compiler_params=params(60),
        cost_estimate=cost(6e9, 8e6),
        name="input_backward",
    )(denc, w_in, dpre, dk)


def owner_order(width):
    n_y, n_core, n_z, n_x = (lax.axis_size(a) for a in AXES)
    rows = width // (n_y * n_core * n_z * n_x)
    place = jnp.arange(width, dtype=jnp.int32)
    inner = place % rows
    place = place // rows
    z, place = place % n_z, place // n_z
    x, place = place % n_x, place // n_x
    y, d_core = place % n_y, place // n_y
    core = (lax.axis_index(AXES[1]) + d_core) % n_core
    y, x = (lax.axis_index(AXES[0]) + y) % n_y, (lax.axis_index(AXES[3]) + x) % n_x
    z = (lax.axis_index(AXES[2]) + z) % n_z
    source = (((y * n_core + core) * n_z + z) * n_x + x) * rows + inner
    return (source[:, None] == jnp.arange(width, dtype=jnp.int32)[None, :]).astype(bf16)


def add_up(blocks):
    total = blocks[0].astype(f32)
    for block in blocks[1:]:
        total = total + block.astype(f32)
    return total


def core_stage(keep, send):
    n_core = lax.axis_size(AXES[1])
    step = keep.shape[0]
    parts = [keep]
    for d in range(1, n_core):
        pairs = [(c, (c + d) % n_core) for c in range(n_core)]
        parts.append(lax.ppermute(send[(d - 1) * step : d * step], AXES[1], pairs))
    return add_up(parts).astype(bf16)


def group_stage(blocks, axes):
    count = len(blocks)
    sizes = [lax.axis_size(a) for a in axes]
    parts = [blocks[0]]
    for d in range(1, count):
        pairs = []
        for c in range(count):
            there, stride, rest_c, rest_d = 0, 1, c, d
            for n in reversed(sizes):
                there += (rest_c + rest_d) % n * stride
                stride, rest_c, rest_d = stride * n, rest_c // n, rest_d // n
            pairs.append((c, there))
        parts.append(lax.ppermute(blocks[d], axes, pairs))
    return add_up(parts)


def scatter_rest(rows):
    plane, line = (AXES[0], AXES[3]), (AXES[2],)
    n_plane, n_line = lax.axis_size(plane), lax.axis_size(line)
    columns = rows.shape[1]
    cut = columns * 13 // 20 // 128 * 128
    each = rows.shape[0] // (n_plane * n_line)
    split = rows.reshape(n_plane, n_line, each, columns)
    one = [split[i, :, :, :cut].reshape(n_line * each, cut) for i in range(n_plane)]
    two = [split[:, i, :, cut:].reshape(n_plane * each, columns - cut) for i in range(n_line)]
    one = group_stage(one, plane).astype(bf16)
    two = group_stage(two, line).astype(bf16)
    one = group_stage([one[i * each : (i + 1) * each] for i in range(n_line)], line)
    two = group_stage([two[i * each : (i + 1) * each] for i in range(n_plane)], plane)
    return jnp.concatenate([one, two], axis=1)


def local(histories, weight_in, weight_out, candidates, cotangent, owner_ids, hist_slot, lengths):
    devices = lax.axis_size(AXES)
    imp_rows, width = candidates.shape
    capacity = max(2, 2 * imp_rows // devices)
    slots = devices * capacity
    kept = width // lax.axis_size(AXES[1])
    after = lax.optimization_barrier

    def exchange(rows):
        shaped = rows.reshape(devices, capacity, rows.shape[1])
        moved = lax.all_to_all(shaped, AXES, split_axis=0, concat_axis=0, tiled=True)
        return moved.reshape(slots, rows.shape[1])

    send, pick = route(owner_ids, hist_slot, lengths, candidates, cotangent, devices, capacity)
    recv = exchange(send)
    perm = owner_order(width)
    enc, slope, slope_t, v, q, k, q_t, attn_t, grad, normed, nu, gi, xt, mt = layer_forward(
        histories, weight_in, weight_out, perm
    )
    d_query, d_enc = target_backward(recv, enc)
    returned = exchange(d_query)

    state = (normed, nu, gi, v, k, q_t, attn_t, grad, slope, slope_t)
    dpre, dk, keep, send = layer_backward(d_enc, weight_out, state, xt, mt, kept)
    send, returned = after((send, returned))
    rows = core_stage(keep, send)
    d_enc, rows = after((d_enc, rows))
    d_inputs = input_backward(d_enc, weight_in, dpre, dk)
    total = scatter_rest(rows)
    candidate_grad = lax.dot_general(
        pick, returned, (((0,), (0,)), ((), ())), preferred_element_type=f32
    ).astype(bf16)
    return d_inputs, candidate_grad, total[:, width:], total[:, :width]


def solution(mesh):
    n_hash, n_dp = mesh.devices.shape
    fine = jax.sharding.Mesh(mesh.devices.reshape(n_hash // 2, 2, n_dp // 2, 2), AXES)
    return jax.shard_map(
        local,
        mesh=fine,
        in_specs=(
            P(AXES, None, None),
            P(),
            P(),
            P(AXES, None),
            P(AXES, None),
            P(AXES, None),
            P(AXES),
            P(AXES),
        ),
        out_specs=(
            P(AXES, None, None),
            P(AXES, None),
            P(AXES, None),
            P(AXES, None),
        ),
        check_vma=False,
    )
```

```python
import functools

import jax
import jax.numpy as jnp
from jax import lax
from jax.experimental import pallas as pl
from jax.experimental.pallas import tpu as pltpu
from jax.sharding import PartitionSpec as P

HEADS = 8
TILE = 128
META = 128
AXES = ("hash_hi", "core", "dp_hi", "dp_lo")
norm_eps = 1e-05
f32 = jnp.float32
bf16 = jnp.bfloat16
MIB = 1024 * 1024


def dot_nn(a, b):
    return lax.dot_general(a, b, (((1,), (0,)), ((), ())), preferred_element_type=f32)


def dot_nt(a, b):
    return lax.dot_general(a, b, (((1,), (1,)), ((), ())), preferred_element_type=f32)


def dot_tn(a, b):
    return lax.dot_general(a, b, (((0,), (0,)), ((), ())), preferred_element_type=f32)


def iota(shape, axis):
    return lax.broadcasted_iota(jnp.int32, shape, axis)


def silu_pair(half):
    t = jnp.tanh(half)
    u = 1.0 + t
    act = half * u
    return act, u + act * (1.0 - t)


def lane_masks(width, part):
    lane = iota((1, width), 1)
    return [((lane >= j * part) & (lane < (j + 1) * part)).astype(bf16) for j in range(width // part)]


def both_heads(pair, masks):
    return jnp.concatenate([pair * m for m in masks], axis=0)


def pick_lanes(stacked, head):
    rows = stacked.shape[0] // 2
    lane = iota((1, 2 * head), 1)
    return jnp.where(lane < head, stacked[:rows], stacked[rows:])


def params(mib):
    return pltpu.CompilerParams(dimension_semantics=("arbitrary",), vmem_limit_bytes=mib * MIB)


def whole(shape):
    return pl.BlockSpec(shape, lambda i: (0,) * len(shape))


def cost(flops, nbytes, trans=0):
    return pl.CostEstimate(flops=int(flops), bytes_accessed=int(nbytes), transcendentals=int(trans))


def route_kernel(devices, capacity, own_ref, slot_ref, len_ref, cand_ref, cot_ref, send_ref, pick_ref):
    rows, width = cand_ref.shape
    slots = devices * capacity
    own = own_ref[...]
    hot = (own == iota((devices, rows), 0)).astype(f32)
    before = (iota((rows, rows), 0) < iota((rows, rows), 1)).astype(f32).astype(bf16)
    earlier = dot_nn(hot.astype(bf16), before)
    position = jnp.sum(earlier * hot, axis=0, keepdims=True).astype(jnp.int32)
    target = own * capacity + position
    pick = (target == iota((slots, rows), 0)).astype(f32).astype(bf16)
    pick_ref[...] = pick
    send_ref[:, :width] = dot_nn(pick, cand_ref[...]).astype(bf16)
    send_ref[:, width : 2 * width] = dot_nn(pick, cot_ref[...]).astype(bf16)
    line = iota((META, rows), 0)
    meta = jnp.where(line == 0, slot_ref[...], jnp.where(line == 1, len_ref[...], 0))
    send_ref[:, 2 * width :] = dot_nt(pick, meta.astype(f32).astype(bf16)).astype(bf16)


def route(own, slot, length, cand, cot, devices, capacity):
    rows, width = cand.shape
    slots = devices * capacity
    line = whole((1, rows))
    return pl.pallas_call(
        functools.partial(route_kernel, devices, capacity),
        grid=(1,),
        in_specs=[line, line, line, whole(cand.shape), whole(cot.shape)],
        out_specs=[whole((slots, 2 * width + META)), whole((slots, rows))],
        out_shape=(
            jax.ShapeDtypeStruct((slots, 2 * width + META), bf16),
            jax.ShapeDtypeStruct((slots, rows), bf16),
        ),
        compiler_params=params(60),
        cost_estimate=cost(2e9, 4 * rows * width * 4),
        name="route",
    )(own.reshape(1, rows), slot.reshape(1, rows), length.reshape(1, rows), cand, cot)


def forward_kernel(
    x_ref, win_ref, wout_ref, perm_ref,
    enc_ref, slope_ref, slope_t_ref, v_ref, q_ref, k_ref, q_t_ref, attn_t_ref, grad_ref,
    normed_ref, nu_ref, gi_ref, xt_ref, mt_ref,
    gate_ref, mixed_ref, slope_u_ref,
):
    seq, width = x_ref.shape[1:]
    head = width // HEADS
    half_seq = seq // 2
    x = x_ref[0]
    for branch in range(4):
        cols = slice(branch * width, (branch + 1) * width)
        act, slope = silu_pair(0.5 * dot_nn(x, win_ref[:, cols]))
        if branch == 3:
            slope_t_ref[0] = jnp.transpose(0.5 * slope).astype(bf16)
        elif branch > 0:
            slope_ref[0, :, (branch - 1) * width : branch * width] = (0.5 * slope).astype(bf16)
        if branch == 0:
            gate_ref[...] = act
            slope_u_ref[...] = 0.5 * slope
        else:
            (v_ref, q_ref, k_ref)[branch - 1][0] = act.astype(bf16)
        if branch == 2:
            q_t_ref[0] = jnp.transpose(act).astype(bf16)
    masks = lane_masks(2 * head, head)
    scale = 0.5 * head**-0.5
    tri = iota((half_seq, half_seq), 0) >= iota((half_seq, half_seq), 1)
    zero = jnp.zeros((half_seq, half_seq), f32)
    for pair in range(HEADS // 2):
        cols = slice(pair * 2 * head, (pair + 1) * 2 * head)
        q_p = q_ref[0, :, cols] * jnp.asarray(scale, bf16)
        half = dot_nt(both_heads(q_p, masks), k_ref[0, :, cols])
        stack = []
        for j in range(2):
            h = 2 * pair + j
            top = silu_pair(half[j * seq : j * seq + half_seq, :half_seq])
            bot = silu_pair(half[j * seq + half_seq : (j + 1) * seq])
            full = []
            for a, b in zip(top, bot):
                a = jnp.concatenate([jnp.where(tri, a, 0.0), zero], axis=1)
                b = jnp.concatenate([b[:, :half_seq], jnp.where(tri, b[:, half_seq:], 0.0)], axis=1)
                full.append(jnp.concatenate([a, b], axis=0))
            stack.append(full[0].astype(bf16))
            attn_t_ref[0, h] = jnp.transpose(full[0]).astype(bf16)
            grad_ref[0, h] = full[1].astype(bf16)
        mixed = dot_nn(jnp.concatenate(stack, axis=0), v_ref[0, :, cols])
        mixed_ref[:, cols] = pick_lanes(mixed, head) * (1.0 / seq)
    mixed = mixed_ref[...]
    centred = mixed - jnp.mean(mixed, axis=1, keepdims=True)
    inv_std = lax.rsqrt(jnp.mean(centred * centred, axis=1, keepdims=True) + norm_eps)
    normed = centred * inv_std
    gate = gate_ref[...]
    merged = (normed * gate).astype(bf16)
    normed_ref[0] = normed.astype(bf16)
    nu_ref[0] = (normed * slope_u_ref[...]).astype(bf16)
    gi_ref[0] = (gate * inv_std).astype(bf16)
    enc_ref[0] = (x.astype(f32) + dot_nn(merged, wout_ref[...])).astype(bf16)
    perm = perm_ref[...]
    xt_ref[...] = dot_nt(perm, x).astype(bf16)
    mt_ref[...] = dot_nt(perm, merged).astype(bf16)


def layer_forward(x, w_in, w_out, perm):
    hist, seq, width = x.shape
    row = pl.BlockSpec((1, seq, width), lambda i: (i, 0, 0))
    wide = pl.BlockSpec((1, seq, 2 * width), lambda i: (i, 0, 0))
    column = pl.BlockSpec((1, width, seq), lambda i: (i, 0, 0))
    square = pl.BlockSpec((1, HEADS, seq, seq), lambda i: (i, 0, 0, 0))
    turned = pl.BlockSpec((width, seq), lambda i: (0, i))
    row_s = jax.ShapeDtypeStruct((hist, seq, width), bf16)
    column_s = jax.ShapeDtypeStruct((hist, width, seq), bf16)
    square_s = jax.ShapeDtypeStruct((hist, HEADS, seq, seq), bf16)
    turned_s = jax.ShapeDtypeStruct((width, hist * seq), bf16)
    return pl.pallas_call(
        forward_kernel,
        grid=(hist,),
        in_specs=[row, whole(w_in.shape), whole(w_out.shape), whole(perm.shape)],
        out_specs=[
            row, wide, column, row, row, row, column, square, square, row, row, row, turned, turned,
        ],
        out_shape=[
            row_s, jax.ShapeDtypeStruct((hist, seq, 2 * width), bf16), column_s, row_s, row_s, row_s,
            column_s, square_s, square_s, row_s, row_s, row_s, turned_s, turned_s,
        ],
        scratch_shapes=[pltpu.VMEM((seq, width), f32)] * 3,
        compiler_params=params(60),
        cost_estimate=cost(18e9, 24e6),
        name="forward",
    )(x, w_in, w_out, perm)


def group_slots(recv_ref, hist):
    slots, width = recv_ref.shape
    meta = recv_ref[:, width - META :].astype(f32)
    slot_h = meta[:, 0:1]
    valid = meta[:, 1:2] > 0.0
    lane = iota((slots, META), 1).astype(f32)
    hot = jnp.where(valid & (slot_h == lane), 1.0, 0.0)
    lower = (iota((slots, slots), 0) > iota((slots, slots), 1)).astype(f32).astype(bf16)
    rank = jnp.sum(dot_nn(lower, hot.astype(bf16)) * hot, axis=1, keepdims=True)
    starts, start = [], jnp.int32(0)
    begin = jnp.zeros((slots, 1), f32)
    for h in range(hist):
        starts.append(start)
        begin = jnp.where(slot_h == float(h), (start * TILE).astype(f32), begin)
        count = jnp.sum(hot[:, h : h + 1]).astype(jnp.int32)
        start = start + (count + (TILE - 1)) // TILE
    dest = jnp.where(valid, begin + rank, -1.0)
    eye = iota((slots, slots), 0) == iota((slots, slots), 1)
    dest_row = jnp.sum(jnp.where(eye, dest, 0.0), axis=0, keepdims=True).astype(jnp.int32)
    return dest.astype(jnp.int32), dest_row, starts, start


def target_tile(tile, starts, dest_row, recv_ref, enc_ref, grouped_ref, turned_ref):
    seq, width = enc_ref.shape[1:]
    head = width // HEADS
    masks = lane_masks(2 * head, head)
    scale = 0.5 * head**-0.5
    base = pl.multiple_of(tile * TILE, TILE)
    hist = jnp.int32(0)
    for start in starts[1:]:
        hist = hist + (tile >= start).astype(jnp.int32)
    choose = (iota((TILE, dest_row.shape[1]), 0) + base == dest_row).astype(f32).astype(bf16)
    rows = dot_nn(choose, recv_ref[...])
    q_all = rows[:, :width] * scale
    g_all = rows[:, width : 2 * width]
    q_t = jnp.transpose(q_all).astype(bf16)
    g_t = jnp.transpose(g_all).astype(bf16)
    q_all = q_all.astype(bf16)
    g_all = g_all.astype(bf16)
    length = rows[:, 2 * width + 1 : 2 * width + 2]
    positions = iota((TILE, seq), 1).astype(f32)
    weight = jnp.where(positions < length, 1.0 / jnp.maximum(length, 1.0), 0.0)
    for pair in range(HEADS // 2):
        cols = slice(pair * 2 * head, (pair + 1) * 2 * head)
        k_p = enc_ref[hist, :, cols]
        both = dot_nt(
            jnp.concatenate(
                [both_heads(q_all[:, cols], masks), both_heads(g_all[:, cols], masks)], axis=0
            ),
            k_p,
        )
        slopes = []
        for j in range(2):
            h = 2 * pair + j
            mine = slice(h * head, (h + 1) * head)
            act, slope = silu_pair(both[j * TILE : (j + 1) * TILE])
            d_attn = both[(2 + j) * TILE : (3 + j) * TILE]
            attn = (act * weight).astype(bf16)
            d_s = (d_attn * weight * slope).astype(bf16)
            turned_ref[hist, mine, :] += dot_nn(
                jnp.concatenate([g_t[mine], q_t[mine]], axis=1),
                jnp.concatenate([attn, d_s], axis=0),
            )
            slopes.append(d_s)
        d_q = pick_lanes(dot_nn(jnp.concatenate(slopes, axis=0), k_p), head)
        grouped_ref[pl.ds(base, TILE), cols] = (d_q * scale).astype(bf16)


def history_backward(
    at, denc_ref, wout_ref, normed_ref, nu_ref, gi_ref, v_ref, k_ref, q_t_ref, attn_t_ref, grad_ref,
    slope_ref, slope_t_ref, dmix_ref, dpre_ref, dk_ref,
):
    seq, width = denc_ref.shape[1:]
    head = width // HEADS
    here = pl.ds(pl.multiple_of(at * seq, seq), seq)
    d_merged = dot_nt(denc_ref[at], wout_ref[...])
    dpre_ref[here, :width] = (d_merged * nu_ref[at].astype(f32)).astype(bf16)
    normed = normed_ref[at].astype(f32)
    d_norm = d_merged * gi_ref[at].astype(f32)
    d_mix = (
        d_norm
        - jnp.mean(d_norm, axis=1, keepdims=True)
        - normed * jnp.mean(d_norm * normed, axis=1, keepdims=True)
    )
    dmix_ref[...] = d_mix.astype(bf16)
    masks = lane_masks(2 * head, head)
    scale = 0.5 * head**-0.5 / seq
    for pair in range(HEADS // 2):
        cols = slice(pair * 2 * head, (pair + 1) * 2 * head)
        d_p = dmix_ref[:, cols]
        d_attn = dot_nt(both_heads(d_p, masks), v_ref[at, :, cols])
        d_s = [
            (d_attn[j * seq : (j + 1) * seq] * grad_ref[at, 2 * pair + j].astype(f32)).astype(bf16)
            for j in range(2)
        ]
        attn_t = jnp.concatenate([attn_t_ref[at, 2 * pair], attn_t_ref[at, 2 * pair + 1]], axis=0)
        d_v = pick_lanes(dot_nn(attn_t, d_p), head) * (1.0 / seq)
        d_q = pick_lanes(dot_nn(jnp.concatenate(d_s, axis=0), k_ref[at, :, cols]), head) * scale
        for branch, grad in ((0, d_v), (1, d_q)):
            old = slice(branch * width + pair * 2 * head, branch * width + (pair + 1) * 2 * head)
            new = slice(old.start + width, old.stop + width)
            dpre_ref[here, new] = (grad * slope_ref[at, :, old].astype(f32)).astype(bf16)
        for j in range(2):
            mine = slice((2 * pair + j) * head, (2 * pair + j + 1) * head)
            d_k = dot_nn(q_t_ref[at, mine], d_s[j]) * scale
            dk_ref[mine, here] = (d_k * slope_t_ref[at, mine].astype(f32)).astype(bf16)


def owner_kernel(*refs):
    n_in, n_out = 15, 6
    sources, outs, refs = refs[:n_in], refs[n_in : n_in + n_out], refs[n_in + n_out :]
    held, refs = refs[:n_in], refs[n_in:]
    (
        recv_ref, enc_ref, wout_ref, normed_ref, nu_ref, gi_ref, v_ref, k_ref, q_t_ref,
        attn_t_ref, grad_ref, slope_ref, slope_t_ref, mt_ref, xt_ref,
    ) = held
    grouped_ref, turned_ref, dmix_ref, dq_ref, denc_ref, dpre_ref, dk_ref, keep_ref, send_ref, sem_in, sem_out = refs
    dq_hbm, denc_hbm, dpre_hbm, dk_hbm, keep_hbm, send_hbm = outs
    hist, seq, width = enc_ref.shape
    slots, padded = recv_ref.shape[0], grouped_ref.shape[0]
    kept = keep_ref.shape[0]
    loads = [
        pltpu.make_async_copy(source, held[i], sem_in.at[i]) for i, source in enumerate(sources)
    ]
    for load in loads:
        load.start()
    grouped_ref[...] = jnp.zeros_like(grouped_ref)
    turned_ref[...] = jnp.zeros_like(turned_ref)
    loads[0].wait()
    dest, dest_row, starts, tiles = group_slots(recv_ref, hist)
    loads[1].wait()

    def one_tile(tile, carry):
        target_tile(tile, starts, dest_row, recv_ref, enc_ref, grouped_ref, turned_ref)
        return carry

    lax.fori_loop(0, tiles, one_tile, 0)
    back = (dest == iota((slots, padded), 1)).astype(f32).astype(bf16)
    dq_ref[...] = dot_nn(back, grouped_ref[...]).astype(bf16)
    for h in range(hist):
        denc_ref[h] = jnp.transpose(turned_ref[h]).astype(bf16)
    stores = [
        pltpu.make_async_copy(dq_ref, dq_hbm, sem_out.at[0]),
        pltpu.make_async_copy(denc_ref, denc_hbm, sem_out.at[1]),
    ]
    for store in stores:
        store.start()
    for load in loads[2:]:
        load.wait()

    def one_history(at, carry):
        history_backward(
            at, denc_ref, wout_ref, normed_ref, nu_ref, gi_ref, v_ref, k_ref, q_t_ref, attn_t_ref,
            grad_ref, slope_ref, slope_t_ref, dmix_ref, dpre_ref, dk_ref,
        )
        return carry

    lax.fori_loop(0, hist, one_history, 0)
    late = [
        pltpu.make_async_copy(dpre_ref, dpre_hbm, sem_out.at[2]),
        pltpu.make_async_copy(dk_ref, dk_hbm, sem_out.at[3]),
    ]
    for store in late:
        store.start()
    stores += late
    for block in range(5):
        cols = slice(block * width, (block + 1) * width)
        if block == 0:
            part = dot_nn(mt_ref[...], denc_ref[...].reshape(hist * seq, width))
        elif block == 4:
            part = dot_nt(xt_ref[...], dk_ref[...])
        else:
            part = dot_nn(xt_ref[...], dpre_ref[:, (block - 1) * width : block * width])
        for half, (ref, hbm) in enumerate(((keep_ref, keep_hbm), (send_ref, send_hbm))):
            ref[:, cols] = (part[:kept] if half == 0 else part[kept:]).astype(bf16)
            store = pltpu.make_async_copy(
                ref.at[:, cols], hbm.at[:, cols], sem_out.at[4 + 2 * block + half]
            )
            store.start()
            stores.append(store)
    for store in stores:
        store.wait()


def owner_backward(recv, enc, w_out, state, mt, xt, kept):
    hist, seq, width = enc.shape
    slots = recv.shape[0]
    rows = hist * seq
    padded = ((slots - hist) // TILE + hist) * TILE
    operands = (recv, enc, w_out) + state + (mt, xt)
    raw = pl.BlockSpec(memory_space=pl.ANY)
    outs = [
        jax.ShapeDtypeStruct((slots, width), bf16),
        jax.ShapeDtypeStruct(enc.shape, bf16),
        jax.ShapeDtypeStruct((rows, 3 * width), bf16),
        jax.ShapeDtypeStruct((width, rows), bf16),
        jax.ShapeDtypeStruct((kept, 5 * width), bf16),
        jax.ShapeDtypeStruct((width - kept, 5 * width), bf16),
    ]
    return pl.pallas_call(
        owner_kernel,
        grid=(1,),
        in_specs=[raw] * len(operands),
        out_specs=[raw] * len(outs),
        out_shape=outs,
        scratch_shapes=[pltpu.VMEM(a.shape, a.dtype) for a in operands]
        + [
            pltpu.VMEM((padded, width), bf16),
            pltpu.VMEM((hist, width, seq), f32),
            pltpu.VMEM((seq, width), bf16),
        ]
        + [pltpu.VMEM(a.shape, a.dtype) for a in outs]
        + [pltpu.SemaphoreType.DMA((len(operands),)), pltpu.SemaphoreType.DMA((14,))],
        compiler_params=params(60),
        cost_estimate=cost(30e9, 30e6),
        name="owner_backward",
    )(*operands)


def input_kernel(denc_ref, win_ref, dpre_ref, dk_ref, out_ref):
    width = denc_ref.shape[2]
    total = denc_ref[0].astype(f32) + dot_nt(dpre_ref[...], win_ref[:, : 3 * width])
    total = total + dot_nt(jnp.transpose(dk_ref[...]), win_ref[:, 3 * width :])
    out_ref[0] = total.astype(bf16)


def input_backward(denc, w_in, dpre, dk):
    hist, seq, width = denc.shape
    block = lambda a: pl.BlockSpec((1,) + a.shape[1:], lambda i: (i, 0, 0))
    return pl.pallas_call(
        input_kernel,
        grid=(hist,),
        in_specs=[
            block(denc),
            whole(w_in.shape),
            pl.BlockSpec((seq, 3 * width), lambda i: (i, 0)),
            pl.BlockSpec((width, seq), lambda i: (0, i)),
        ],
        out_specs=block(denc),
        out_shape=jax.ShapeDtypeStruct(denc.shape, bf16),
        compiler_params=params(60),
        cost_estimate=cost(6e9, 8e6),
        name="input_backward",
    )(denc, w_in, dpre, dk)


def owner_order(width):
    n_y, n_core, n_z, n_x = (lax.axis_size(a) for a in AXES)
    rows = width // (n_y * n_core * n_z * n_x)
    place = jnp.arange(width, dtype=jnp.int32)
    inner = place % rows
    place = place // rows
    z, place = place % n_z, place // n_z
    x, place = place % n_x, place // n_x
    y, d_core = place % n_y, place // n_y
    core = (lax.axis_index(AXES[1]) + d_core) % n_core
    y, x = (lax.axis_index(AXES[0]) + y) % n_y, (lax.axis_index(AXES[3]) + x) % n_x
    z = (lax.axis_index(AXES[2]) + z) % n_z
    source = (((y * n_core + core) * n_z + z) * n_x + x) * rows + inner
    return (source[:, None] == jnp.arange(width, dtype=jnp.int32)[None, :]).astype(bf16)


def add_up(blocks):
    total = blocks[0].astype(f32)
    for block in blocks[1:]:
        total = total + block.astype(f32)
    return total


def core_stage(keep, send):
    n_core = lax.axis_size(AXES[1])
    step = keep.shape[0]
    parts = [keep]
    for d in range(1, n_core):
        pairs = [(c, (c + d) % n_core) for c in range(n_core)]
        parts.append(lax.ppermute(send[(d - 1) * step : d * step], AXES[1], pairs))
    return add_up(parts).astype(bf16)


def send_blocks(rows, axes):
    count = lax.axis_size(axes)
    step = rows.shape[0] // count
    sizes = [lax.axis_size(a) for a in axes]
    parts = [rows[:step]]
    for d in range(1, count):
        pairs = []
        for c in range(count):
            there, stride, rest_c, rest_d = 0, 1, c, d
            for n in reversed(sizes):
                there += (rest_c + rest_d) % n * stride
                stride, rest_c, rest_d = stride * n, rest_c // n, rest_d // n
            pairs.append((c, there))
        parts.append(lax.ppermute(rows[d * step : (d + 1) * step], axes, pairs))
    return parts


def local(histories, weight_in, weight_out, candidates, cotangent, owner_ids, hist_slot, lengths):
    devices = lax.axis_size(AXES)
    imp_rows, width = candidates.shape
    capacity = max(2, 2 * imp_rows // devices)
    slots = devices * capacity
    kept = width // lax.axis_size(AXES[1])
    after = lax.optimization_barrier

    def exchange(rows):
        shaped = rows.reshape(devices, capacity, rows.shape[1])
        moved = lax.all_to_all(shaped, AXES, split_axis=0, concat_axis=0, tiled=True)
        return moved.reshape(slots, rows.shape[1])

    send, pick = route(owner_ids, hist_slot, lengths, candidates, cotangent, devices, capacity)
    recv = exchange(send)
    perm = owner_order(width)
    enc, slope, slope_t, v, q, k, q_t, attn_t, grad, normed, nu, gi, xt, mt = layer_forward(
        histories, weight_in, weight_out, perm
    )
    state = (normed, nu, gi, v, k, q_t, attn_t, grad, slope, slope_t)
    d_query, d_enc, dpre, dk, keep, send = owner_backward(recv, enc, weight_out, state, mt, xt, kept)
    returned = exchange(d_query)
    rows = core_stage(keep, send)
    d_enc, rows = after((d_enc, rows))
    d_inputs = input_backward(d_enc, weight_in, dpre, dk)
    parts = send_blocks(rows, (AXES[0], AXES[3]))
    parts, d_inputs, returned = after((parts, d_inputs, returned))
    total = add_up(send_blocks(add_up(parts).astype(bf16), (AXES[2],)))
    candidate_grad = lax.dot_general(
        pick, returned, (((0,), (0,)), ((), ())), preferred_element_type=f32
    ).astype(bf16)
    return d_inputs, candidate_grad, total[:, width:], total[:, :width]


def solution(mesh):
    n_hash, n_dp = mesh.devices.shape
    fine = jax.sharding.Mesh(mesh.devices.reshape(n_hash // 2, 2, n_dp // 2, 2), AXES)
    return jax.shard_map(
        local,
        mesh=fine,
        in_specs=(
            P(AXES, None, None),
            P(),
            P(),
            P(AXES, None),
            P(AXES, None),
            P(AXES, None),
            P(AXES),
            P(AXES),
        ),
        out_specs=(
            P(AXES, None, None),
            P(AXES, None),
            P(AXES, None),
            P(AXES, None),
        ),
        check_vma=False,
    )
```

```python
import functools

import jax
import jax.numpy as jnp
from jax import lax
from jax.experimental import pallas as pl
from jax.experimental.pallas import tpu as pltpu
from jax.sharding import PartitionSpec as P

HEADS = 8
TILE = 128
META = 128
AXES = ("hash_hi", "core", "dp_hi", "dp_lo")
norm_eps = 1e-05
f32 = jnp.float32
bf16 = jnp.bfloat16
MIB = 1024 * 1024


def dot_nn(a, b):
    return lax.dot_general(a, b, (((1,), (0,)), ((), ())), preferred_element_type=f32)


def dot_nt(a, b):
    return lax.dot_general(a, b, (((1,), (1,)), ((), ())), preferred_element_type=f32)


def dot_tn(a, b):
    return lax.dot_general(a, b, (((0,), (0,)), ((), ())), preferred_element_type=f32)


def iota(shape, axis):
    return lax.broadcasted_iota(jnp.int32, shape, axis)


def silu_pair(half):
    t = jnp.tanh(half)
    u = 1.0 + t
    act = half * u
    return act, u + act * (1.0 - t)


def lane_masks(width, part):
    lane = iota((1, width), 1)
    return [((lane >= j * part) & (lane < (j + 1) * part)).astype(bf16) for j in range(width // part)]


def both_heads(pair, masks):
    return jnp.concatenate([pair * m for m in masks], axis=0)


def pick_lanes(stacked, head):
    rows = stacked.shape[0] // 2
    lane = iota((1, 2 * head), 1)
    return jnp.where(lane < head, stacked[:rows], stacked[rows:])


def params(mib):
    return pltpu.CompilerParams(dimension_semantics=("arbitrary",), vmem_limit_bytes=mib * MIB)


def whole(shape):
    return pl.BlockSpec(shape, lambda i: (0,) * len(shape))


def cost(flops, nbytes, trans=0):
    return pl.CostEstimate(flops=int(flops), bytes_accessed=int(nbytes), transcendentals=int(trans))


def route_kernel(devices, capacity, own_ref, slot_ref, len_ref, cand_ref, cot_ref, send_ref, pick_ref):
    rows, width = cand_ref.shape
    slots = devices * capacity
    own = own_ref[...]
    hot = (own == iota((devices, rows), 0)).astype(f32)
    before = (iota((rows, rows), 0) < iota((rows, rows), 1)).astype(f32).astype(bf16)
    earlier = dot_nn(hot.astype(bf16), before)
    position = jnp.sum(earlier * hot, axis=0, keepdims=True).astype(jnp.int32)
    target = own * capacity + position
    pick = (target == iota((slots, rows), 0)).astype(f32).astype(bf16)
    pick_ref[...] = pick
    send_ref[:, :width] = dot_nn(pick, cand_ref[...]).astype(bf16)
    send_ref[:, width : 2 * width] = dot_nn(pick, cot_ref[...]).astype(bf16)
    line = iota((META, rows), 0)
    meta = jnp.where(line == 0, slot_ref[...], jnp.where(line == 1, len_ref[...], 0))
    send_ref[:, 2 * width :] = dot_nt(pick, meta.astype(f32).astype(bf16)).astype(bf16)


def route(own, slot, length, cand, cot, devices, capacity):
    rows, width = cand.shape
    slots = devices * capacity
    line = whole((1, rows))
    return pl.pallas_call(
        functools.partial(route_kernel, devices, capacity),
        grid=(1,),
        in_specs=[line, line, line, whole(cand.shape), whole(cot.shape)],
        out_specs=[whole((slots, 2 * width + META)), whole((slots, rows))],
        out_shape=(
            jax.ShapeDtypeStruct((slots, 2 * width + META), bf16),
            jax.ShapeDtypeStruct((slots, rows), bf16),
        ),
        compiler_params=params(60),
        cost_estimate=cost(2e9, 4 * rows * width * 4),
        name="route",
    )(own.reshape(1, rows), slot.reshape(1, rows), length.reshape(1, rows), cand, cot)


def forward_kernel(
    x_ref, win_ref, wout_ref, perm_ref,
    enc_ref, slope_ref, slope_t_ref, v_ref, q_ref, k_ref, q_t_ref, attn_t_ref, grad_ref,
    normed_ref, nu_ref, gi_ref, xt_ref, mt_ref,
    gate_ref, mixed_ref, slope_u_ref,
):
    seq, width = x_ref.shape[1:]
    head = width // HEADS
    half_seq = seq // 2
    x = x_ref[0]
    for branch in range(4):
        cols = slice(branch * width, (branch + 1) * width)
        act, slope = silu_pair(0.5 * dot_nn(x, win_ref[:, cols]))
        if branch == 3:
            slope_t_ref[0] = jnp.transpose(0.5 * slope).astype(bf16)
        elif branch > 0:
            slope_ref[0, :, (branch - 1) * width : branch * width] = (0.5 * slope).astype(bf16)
        if branch == 0:
            gate_ref[...] = act
            slope_u_ref[...] = 0.5 * slope
        else:
            (v_ref, q_ref, k_ref)[branch - 1][0] = act.astype(bf16)
        if branch == 2:
            q_t_ref[0] = jnp.transpose(act).astype(bf16)
    masks = lane_masks(2 * head, head)
    scale = 0.5 * head**-0.5
    tri = iota((half_seq, half_seq), 0) >= iota((half_seq, half_seq), 1)
    zero = jnp.zeros((half_seq, half_seq), f32)
    for pair in range(HEADS // 2):
        cols = slice(pair * 2 * head, (pair + 1) * 2 * head)
        q_p = q_ref[0, :, cols] * jnp.asarray(scale, bf16)
        half = dot_nt(both_heads(q_p, masks), k_ref[0, :, cols])
        stack = []
        for j in range(2):
            h = 2 * pair + j
            top = silu_pair(half[j * seq : j * seq + half_seq, :half_seq])
            bot = silu_pair(half[j * seq + half_seq : (j + 1) * seq])
            full = []
            for a, b in zip(top, bot):
                a = jnp.concatenate([jnp.where(tri, a, 0.0), zero], axis=1)
                b = jnp.concatenate([b[:, :half_seq], jnp.where(tri, b[:, half_seq:], 0.0)], axis=1)
                full.append(jnp.concatenate([a, b], axis=0))
            stack.append(full[0].astype(bf16))
            attn_t_ref[0, h] = jnp.transpose(full[0]).astype(bf16)
            grad_ref[0, h] = full[1].astype(bf16)
        mixed = dot_nn(jnp.concatenate(stack, axis=0), v_ref[0, :, cols])
        mixed_ref[:, cols] = pick_lanes(mixed, head) * (1.0 / seq)
    mixed = mixed_ref[...]
    centred = mixed - jnp.mean(mixed, axis=1, keepdims=True)
    inv_std = lax.rsqrt(jnp.mean(centred * centred, axis=1, keepdims=True) + norm_eps)
    normed = centred * inv_std
    gate = gate_ref[...]
    merged = (normed * gate).astype(bf16)
    normed_ref[0] = normed.astype(bf16)
    nu_ref[0] = (normed * slope_u_ref[...]).astype(bf16)
    gi_ref[0] = (gate * inv_std).astype(bf16)
    enc_ref[0] = (x.astype(f32) + dot_nn(merged, wout_ref[...])).astype(bf16)
    perm = perm_ref[...]
    xt_ref[...] = dot_nt(perm, x).astype(bf16)
    mt_ref[...] = dot_nt(perm, merged).astype(bf16)


def layer_forward(x, w_in, w_out, perm):
    hist, seq, width = x.shape
    row = pl.BlockSpec((1, seq, width), lambda i: (i, 0, 0))
    wide = pl.BlockSpec((1, seq, 2 * width), lambda i: (i, 0, 0))
    column = pl.BlockSpec((1, width, seq), lambda i: (i, 0, 0))
    square = pl.BlockSpec((1, HEADS, seq, seq), lambda i: (i, 0, 0, 0))
    turned = pl.BlockSpec((width, seq), lambda i: (0, i))
    row_s = jax.ShapeDtypeStruct((hist, seq, width), bf16)
    column_s = jax.ShapeDtypeStruct((hist, width, seq), bf16)
    square_s = jax.ShapeDtypeStruct((hist, HEADS, seq, seq), bf16)
    turned_s = jax.ShapeDtypeStruct((width, hist * seq), bf16)
    return pl.pallas_call(
        forward_kernel,
        grid=(hist,),
        in_specs=[row, whole(w_in.shape), whole(w_out.shape), whole(perm.shape)],
        out_specs=[
            row, wide, column, row, row, row, column, square, square, row, row, row, turned, turned,
        ],
        out_shape=[
            row_s, jax.ShapeDtypeStruct((hist, seq, 2 * width), bf16), column_s, row_s, row_s, row_s,
            column_s, square_s, square_s, row_s, row_s, row_s, turned_s, turned_s,
        ],
        scratch_shapes=[pltpu.VMEM((seq, width), f32)] * 3,
        compiler_params=params(60),
        cost_estimate=cost(18e9, 24e6),
        name="forward",
    )(x, w_in, w_out, perm)


def group_slots(recv_ref, hist):
    slots, width = recv_ref.shape
    meta = recv_ref[:, width - META :].astype(f32)
    slot_h = meta[:, 0:1]
    valid = meta[:, 1:2] > 0.0
    lane = iota((slots, META), 1).astype(f32)
    hot = jnp.where(valid & (slot_h == lane), 1.0, 0.0)
    lower = (iota((slots, slots), 0) > iota((slots, slots), 1)).astype(f32).astype(bf16)
    rank = jnp.sum(dot_nn(lower, hot.astype(bf16)) * hot, axis=1, keepdims=True)
    starts, start = [], jnp.int32(0)
    begin = jnp.zeros((slots, 1), f32)
    for h in range(hist):
        starts.append(start)
        begin = jnp.where(slot_h == float(h), (start * TILE).astype(f32), begin)
        count = jnp.sum(hot[:, h : h + 1]).astype(jnp.int32)
        start = start + (count + (TILE - 1)) // TILE
    dest = jnp.where(valid, begin + rank, -1.0)
    eye = iota((slots, slots), 0) == iota((slots, slots), 1)
    dest_row = jnp.sum(jnp.where(eye, dest, 0.0), axis=0, keepdims=True).astype(jnp.int32)
    return dest.astype(jnp.int32), dest_row, starts, start


def target_tile(tile, starts, dest_row, recv_ref, enc_ref, grouped_ref, turned_ref):
    seq, width = enc_ref.shape[1:]
    head = width // HEADS
    masks = lane_masks(2 * head, head)
    scale = 0.5 * head**-0.5
    base = pl.multiple_of(tile * TILE, TILE)
    hist = jnp.int32(0)
    for start in starts[1:]:
        hist = hist + (tile >= start).astype(jnp.int32)
    choose = (iota((TILE, dest_row.shape[1]), 0) + base == dest_row).astype(f32).astype(bf16)
    rows = dot_nn(choose, recv_ref[...])
    q_all = rows[:, :width] * scale
    g_all = rows[:, width : 2 * width]
    q_t = jnp.transpose(q_all).astype(bf16)
    g_t = jnp.transpose(g_all).astype(bf16)
    q_all = q_all.astype(bf16)
    g_all = g_all.astype(bf16)
    length = rows[:, 2 * width + 1 : 2 * width + 2]
    positions = iota((TILE, seq), 1).astype(f32)
    weight = jnp.where(positions < length, 1.0 / jnp.maximum(length, 1.0), 0.0)
    for pair in range(HEADS // 2):
        cols = slice(pair * 2 * head, (pair + 1) * 2 * head)
        k_p = enc_ref[hist, :, cols]
        both = dot_nt(
            jnp.concatenate(
                [both_heads(q_all[:, cols], masks), both_heads(g_all[:, cols], masks)], axis=0
            ),
            k_p,
        )
        slopes = []
        for j in range(2):
            h = 2 * pair + j
            mine = slice(h * head, (h + 1) * head)
            act, slope = silu_pair(both[j * TILE : (j + 1) * TILE])
            d_attn = both[(2 + j) * TILE : (3 + j) * TILE]
            attn = (act * weight).astype(bf16)
            d_s = (d_attn * weight * slope).astype(bf16)
            turned_ref[hist, mine, :] += dot_nn(
                jnp.concatenate([g_t[mine], q_t[mine]], axis=1),
                jnp.concatenate([attn, d_s], axis=0),
            )
            slopes.append(d_s)
        d_q = pick_lanes(dot_nn(jnp.concatenate(slopes, axis=0), k_p), head)
        grouped_ref[pl.ds(base, TILE), cols] = (d_q * scale).astype(bf16)


def norm_backward(denc_ref, wout_ref, normed_ref, nu_ref, gi_ref, dmix_ref, dpre_ref):
    hist, seq, width = denc_ref.shape
    for at in range(hist):
        here = slice(at * seq, (at + 1) * seq)
        d_merged = dot_nt(denc_ref[at], wout_ref[...])
        dpre_ref[here, :width] = (d_merged * nu_ref[at].astype(f32)).astype(bf16)
        normed = normed_ref[at].astype(f32)
        d_norm = d_merged * gi_ref[at].astype(f32)
        d_mix = (
            d_norm
            - jnp.mean(d_norm, axis=1, keepdims=True)
            - normed * jnp.mean(d_norm * normed, axis=1, keepdims=True)
        )
        dmix_ref[at] = d_mix.astype(bf16)


def attention_backward(
    at, dmix_ref, v_ref, k_ref, q_t_ref, attn_t_ref, grad_ref, slope_ref, slope_t_ref, dpre_ref, dk_ref
):
    seq, width = dmix_ref.shape[1:]
    head = width // HEADS
    here = slice(at * seq, (at + 1) * seq)
    masks = lane_masks(2 * head, head)
    scale = 0.5 * head**-0.5 / seq
    for pair in range(HEADS // 2):
        cols = slice(pair * 2 * head, (pair + 1) * 2 * head)
        d_p = dmix_ref[at, :, cols]
        d_attn = dot_nt(both_heads(d_p, masks), v_ref[at, :, cols])
        d_s = [
            (d_attn[j * seq : (j + 1) * seq] * grad_ref[at, 2 * pair + j].astype(f32)).astype(bf16)
            for j in range(2)
        ]
        attn_t = jnp.concatenate([attn_t_ref[at, 2 * pair], attn_t_ref[at, 2 * pair + 1]], axis=0)
        d_v = pick_lanes(dot_nn(attn_t, d_p), head) * (1.0 / seq)
        d_q = pick_lanes(dot_nn(jnp.concatenate(d_s, axis=0), k_ref[at, :, cols]), head) * scale
        for branch, grad in ((0, d_v), (1, d_q)):
            old = slice(branch * width + pair * 2 * head, branch * width + (pair + 1) * 2 * head)
            new = slice(old.start + width, old.stop + width)
            dpre_ref[here, new] = (grad * slope_ref[at, :, old].astype(f32)).astype(bf16)
        for j in range(2):
            mine = slice((2 * pair + j) * head, (2 * pair + j + 1) * head)
            d_k = dot_nn(q_t_ref[at, mine], d_s[j]) * scale
            dk_ref[mine, here] = (d_k * slope_t_ref[at, mine].astype(f32)).astype(bf16)


def owner_kernel(*refs):
    n_in, n_out = 15, 6
    sources, outs, refs = refs[:n_in], refs[n_in : n_in + n_out], refs[n_in + n_out :]
    held, refs = refs[:n_in], refs[n_in:]
    (
        recv_ref, enc_ref, wout_ref, normed_ref, nu_ref, gi_ref, v_ref, k_ref, q_t_ref,
        attn_t_ref, grad_ref, slope_ref, slope_t_ref, mt_ref, xt_ref,
    ) = held
    grouped_ref, turned_ref, dmix_ref, dq_ref, denc_ref, dpre_ref, dk_ref, keep_ref, send_ref, sem_in, sem_out = refs
    dq_hbm, denc_hbm, dpre_hbm, dk_hbm, keep_hbm, send_hbm = outs
    hist, seq, width = enc_ref.shape
    slots, padded = recv_ref.shape[0], grouped_ref.shape[0]
    kept = keep_ref.shape[0]

    def load(i, n, at=None):
        source, dest = (sources[i], held[i]) if at is None else (sources[i].at[at], held[i].at[at])
        return pltpu.make_async_copy(source, dest, sem_in.at[n])

    first = [load(i, i) for i in range(6)]
    by_history = [[load(i, i + 7 * at, at) for i in range(6, 13)] for at in range(hist)]
    last = [load(i, 7 * hist + i - 7) for i in (13, 14)]
    for copy in first + sum(by_history, []) + last:
        copy.start()
    grouped_ref[...] = jnp.zeros_like(grouped_ref)
    turned_ref[...] = jnp.zeros_like(turned_ref)
    first[0].wait()
    dest, dest_row, starts, tiles = group_slots(recv_ref, hist)
    first[1].wait()

    def one_tile(tile, carry):
        target_tile(tile, starts, dest_row, recv_ref, enc_ref, grouped_ref, turned_ref)
        return carry

    lax.fori_loop(0, tiles, one_tile, 0)
    for h in range(hist):
        denc_ref[h] = jnp.transpose(turned_ref[h]).astype(bf16)
    back = (dest == iota((slots, padded), 1)).astype(f32).astype(bf16)
    dq_ref[...] = dot_nn(back, grouped_ref[...]).astype(bf16)
    stores = []

    def store(source, dest):
        copy = pltpu.make_async_copy(source, dest, sem_out.at[len(stores)])
        copy.start()
        stores.append(copy)

    store(denc_ref, denc_hbm)
    store(dq_ref, dq_hbm)
    for copy in first[2:]:
        copy.wait()
    norm_backward(denc_ref, wout_ref, normed_ref, nu_ref, gi_ref, dmix_ref, dpre_ref)
    for at in range(hist):
        for copy in by_history[at]:
            copy.wait()
        attention_backward(
            at, dmix_ref, v_ref, k_ref, q_t_ref, attn_t_ref, grad_ref, slope_ref, slope_t_ref,
            dpre_ref, dk_ref,
        )
        here = pl.ds(at * seq, seq)
        store(dpre_ref.at[here, :], dpre_hbm.at[here, :])
        store(dk_ref.at[:, here], dk_hbm.at[:, here])
    for copy in last:
        copy.wait()
    for block in range(5):
        cols = slice(block * width, (block + 1) * width)
        if block == 0:
            part = dot_nn(mt_ref[...], denc_ref[...].reshape(hist * seq, width))
        elif block == 4:
            part = dot_nt(xt_ref[...], dk_ref[...])
        else:
            part = dot_nn(xt_ref[...], dpre_ref[:, (block - 1) * width : block * width])
        keep_ref[:, cols] = part[:kept].astype(bf16)
        send_ref[:, cols] = part[kept:].astype(bf16)
        store(keep_ref.at[:, cols], keep_hbm.at[:, cols])
        store(send_ref.at[:, cols], send_hbm.at[:, cols])
    for copy in stores:
        copy.wait()


def owner_backward(recv, enc, w_out, state, mt, xt, kept):
    hist, seq, width = enc.shape
    slots = recv.shape[0]
    rows = hist * seq
    padded = ((slots - hist) // TILE + hist) * TILE
    operands = (recv, enc, w_out) + state + (mt, xt)
    raw = pl.BlockSpec(memory_space=pl.ANY)
    outs = [
        jax.ShapeDtypeStruct((slots, width), bf16),
        jax.ShapeDtypeStruct(enc.shape, bf16),
        jax.ShapeDtypeStruct((rows, 3 * width), bf16),
        jax.ShapeDtypeStruct((width, rows), bf16),
        jax.ShapeDtypeStruct((kept, 5 * width), bf16),
        jax.ShapeDtypeStruct((width - kept, 5 * width), bf16),
    ]
    return pl.pallas_call(
        owner_kernel,
        grid=(1,),
        in_specs=[raw] * len(operands),
        out_specs=[raw] * len(outs),
        out_shape=outs,
        scratch_shapes=[pltpu.VMEM(a.shape, a.dtype) for a in operands]
        + [
            pltpu.VMEM((padded, width), bf16),
            pltpu.VMEM((hist, width, seq), f32),
            pltpu.VMEM((hist, seq, width), bf16),
        ]
        + [pltpu.VMEM(a.shape, a.dtype) for a in outs]
        + [
            pltpu.SemaphoreType.DMA((7 * hist + 8,)),
            pltpu.SemaphoreType.DMA((2 * hist + 12,)),
        ],
        compiler_params=params(60),
        cost_estimate=cost(30e9, 30e6),
        name="owner_backward",
    )(*operands)


def input_kernel(denc_ref, win_ref, dpre_ref, dk_ref, out_ref):
    width = denc_ref.shape[2]
    total = denc_ref[0].astype(f32) + dot_nt(dpre_ref[...], win_ref[:, : 3 * width])
    total = total + dot_nt(jnp.transpose(dk_ref[...]), win_ref[:, 3 * width :])
    out_ref[0] = total.astype(bf16)


def input_backward(denc, w_in, dpre, dk):
    hist, seq, width = denc.shape
    block = lambda a: pl.BlockSpec((1,) + a.shape[1:], lambda i: (i, 0, 0))
    return pl.pallas_call(
        input_kernel,
        grid=(hist,),
        in_specs=[
            block(denc),
            whole(w_in.shape),
            pl.BlockSpec((seq, 3 * width), lambda i: (i, 0)),
            pl.BlockSpec((width, seq), lambda i: (0, i)),
        ],
        out_specs=block(denc),
        out_shape=jax.ShapeDtypeStruct(denc.shape, bf16),
        compiler_params=params(60),
        cost_estimate=cost(6e9, 8e6),
        name="input_backward",
    )(denc, w_in, dpre, dk)


def owner_order(width):
    n_y, n_core, n_z, n_x = (lax.axis_size(a) for a in AXES)
    rows = width // (n_y * n_core * n_z * n_x)
    place = jnp.arange(width, dtype=jnp.int32)
    inner = place % rows
    place = place // rows
    z, place = place % n_z, place // n_z
    x, place = place % n_x, place // n_x
    y, d_core = place % n_y, place // n_y
    core = (lax.axis_index(AXES[1]) + d_core) % n_core
    y, x = (lax.axis_index(AXES[0]) + y) % n_y, (lax.axis_index(AXES[3]) + x) % n_x
    z = (lax.axis_index(AXES[2]) + z) % n_z
    source = (((y * n_core + core) * n_z + z) * n_x + x) * rows + inner
    return (source[:, None] == jnp.arange(width, dtype=jnp.int32)[None, :]).astype(bf16)


def add_up(blocks):
    total = blocks[0].astype(f32)
    for block in blocks[1:]:
        total = total + block.astype(f32)
    return total


def core_stage(keep, send):
    n_core = lax.axis_size(AXES[1])
    step = keep.shape[0]
    parts = [keep]
    for d in range(1, n_core):
        pairs = [(c, (c + d) % n_core) for c in range(n_core)]
        parts.append(lax.ppermute(send[(d - 1) * step : d * step], AXES[1], pairs))
    return add_up(parts).astype(bf16)


def send_blocks(rows, axes):
    count = lax.axis_size(axes)
    step = rows.shape[0] // count
    sizes = [lax.axis_size(a) for a in axes]
    parts = [rows[:step]]
    for d in range(1, count):
        pairs = []
        for c in range(count):
            there, stride, rest_c, rest_d = 0, 1, c, d
            for n in reversed(sizes):
                there += (rest_c + rest_d) % n * stride
                stride, rest_c, rest_d = stride * n, rest_c // n, rest_d // n
            pairs.append((c, there))
        parts.append(lax.ppermute(rows[d * step : (d + 1) * step], axes, pairs))
    return parts


def local(histories, weight_in, weight_out, candidates, cotangent, owner_ids, hist_slot, lengths):
    devices = lax.axis_size(AXES)
    imp_rows, width = candidates.shape
    capacity = max(2, 2 * imp_rows // devices)
    slots = devices * capacity
    kept = width // lax.axis_size(AXES[1])
    after = lax.optimization_barrier

    def exchange(rows):
        shaped = rows.reshape(devices, capacity, rows.shape[1])
        moved = lax.all_to_all(shaped, AXES, split_axis=0, concat_axis=0, tiled=True)
        return moved.reshape(slots, rows.shape[1])

    send, pick = route(owner_ids, hist_slot, lengths, candidates, cotangent, devices, capacity)
    recv = exchange(send)
    perm = owner_order(width)
    enc, slope, slope_t, v, q, k, q_t, attn_t, grad, normed, nu, gi, xt, mt = layer_forward(
        histories, weight_in, weight_out, perm
    )
    state = (normed, nu, gi, v, k, q_t, attn_t, grad, slope, slope_t)
    d_query, d_enc, dpre, dk, keep, send = owner_backward(recv, enc, weight_out, state, mt, xt, kept)
    returned = exchange(d_query)
    rows = core_stage(keep, send)
    d_enc, rows = after((d_enc, rows))
    d_inputs = input_backward(d_enc, weight_in, dpre, dk)
    parts = send_blocks(rows, (AXES[0], AXES[3]))
    parts, d_inputs, returned = after((parts, d_inputs, returned))
    parts = send_blocks(add_up(parts).astype(bf16), (AXES[2],))
    candidate_grad = lax.dot_general(
        pick, returned, (((0,), (0,)), ((), ())), preferred_element_type=f32
    ).astype(bf16)
    w_in_grad = add_up([p[:, width:] for p in parts])
    w_out_grad = add_up([p[:, :width] for p in parts])
    return d_inputs, candidate_grad, w_in_grad, w_out_grad


def solution(mesh):
    n_hash, n_dp = mesh.devices.shape
    fine = jax.sharding.Mesh(mesh.devices.reshape(n_hash // 2, 2, n_dp // 2, 2), AXES)
    return jax.shard_map(
        local,
        mesh=fine,
        in_specs=(
            P(AXES, None, None),
            P(),
            P(),
            P(AXES, None),
            P(AXES, None),
            P(AXES, None),
            P(AXES),
            P(AXES),
        ),
        out_specs=(
            P(AXES, None, None),
            P(AXES, None),
            P(AXES, None),
            P(AXES, None),
        ),
        check_vma=False,
    )
```

```python
import functools
import math

import jax
import jax.numpy as jnp
from jax import lax
from jax.experimental import pallas as pl
from jax.experimental.pallas import tpu as pltpu
from jax.sharding import PartitionSpec as P

HEADS = 8
TILE = 128
META = 128
AXES = ("hash_hi", "core", "dp_hi", "dp_lo")
norm_eps = 1e-05
f32 = jnp.float32
bf16 = jnp.bfloat16
MIB = 1024 * 1024


def dot_nn(a, b):
    return lax.dot_general(a, b, (((1,), (0,)), ((), ())), preferred_element_type=f32)


def dot_nt(a, b):
    return lax.dot_general(a, b, (((1,), (1,)), ((), ())), preferred_element_type=f32)


def dot_tn(a, b):
    return lax.dot_general(a, b, (((0,), (0,)), ((), ())), preferred_element_type=f32)


def iota(shape, axis):
    return lax.broadcasted_iota(jnp.int32, shape, axis)


def silu_pair(half):
    t = jnp.tanh(half)
    u = 1.0 + t
    act = half * u
    return act, u + act * (1.0 - t)


def lane_masks(width, part):
    lane = iota((1, width), 1)
    return [((lane >= j * part) & (lane < (j + 1) * part)).astype(bf16) for j in range(width // part)]


def both_heads(pair, masks):
    return jnp.concatenate([pair * m for m in masks], axis=0)


def pick_lanes(stacked, head):
    rows = stacked.shape[0] // 2
    lane = iota((1, 2 * head), 1)
    return jnp.where(lane < head, stacked[:rows], stacked[rows:])


def params(mib):
    return pltpu.CompilerParams(dimension_semantics=("arbitrary",), vmem_limit_bytes=mib * MIB)


def whole(shape):
    return pl.BlockSpec(shape, lambda i: (0,) * len(shape))


def cost(flops, nbytes, trans=0):
    return pl.CostEstimate(flops=int(flops), bytes_accessed=int(nbytes), transcendentals=int(trans))


def route_kernel(sizes, capacity, me_ref, own_ref, slot_ref, len_ref, cand_ref, cot_ref, send_ref, pick_ref):
    n_y, n_core, n_z, n_x = sizes
    devices = n_y * n_core * n_z * n_x
    rows, width = cand_ref.shape
    slots = devices * capacity
    own = own_ref[...]
    hot = (own == iota((devices, rows), 0)).astype(f32)
    before = (iota((rows, rows), 0) < iota((rows, rows), 1)).astype(f32).astype(bf16)
    earlier = dot_nn(hot.astype(bf16), before)
    position = jnp.sum(earlier * hot, axis=0, keepdims=True).astype(jnp.int32)
    target = own * capacity + position
    pick = (target == iota((slots, rows), 0)).astype(f32).astype(bf16)
    x, z = own % n_x, own // n_x % n_z
    core, y = own // (n_x * n_z) % n_core, own // (n_x * n_z * n_core)
    y, core, z, x = (
        (me_ref[i] - at + n) % n for i, (at, n) in enumerate(zip((y, core, z, x), sizes))
    )
    back = (((y * n_x + x) * n_z + z) * n_core + core) * capacity + position
    pick_ref[...] = (back == iota((slots, rows), 0)).astype(f32).astype(bf16)
    send_ref[:, :width] = dot_nn(pick, cand_ref[...]).astype(bf16)
    send_ref[:, width : 2 * width] = dot_nn(pick, cot_ref[...]).astype(bf16)
    line = iota((META, rows), 0)
    meta = jnp.where(line == 0, slot_ref[...], jnp.where(line == 1, len_ref[...], 0))
    send_ref[:, 2 * width :] = dot_nt(pick, meta.astype(f32).astype(bf16)).astype(bf16)


def route(me, own, slot, length, cand, cot, sizes, capacity):
    rows, width = cand.shape
    slots = math.prod(sizes) * capacity
    line = whole((1, rows))
    return pl.pallas_call(
        functools.partial(route_kernel, sizes, capacity),
        grid=(1,),
        in_specs=[
            pl.BlockSpec(memory_space=pltpu.SMEM), line, line, line, whole(cand.shape), whole(cot.shape),
        ],
        out_specs=[whole((slots, 2 * width + META)), whole((slots, rows))],
        out_shape=(
            jax.ShapeDtypeStruct((slots, 2 * width + META), bf16),
            jax.ShapeDtypeStruct((slots, rows), bf16),
        ),
        compiler_params=params(60),
        cost_estimate=cost(2e9, 4 * rows * width * 4),
        name="route",
    )(me, own.reshape(1, rows), slot.reshape(1, rows), length.reshape(1, rows), cand, cot)


def forward_kernel(
    x_ref, win_ref, wout_ref, perm_ref,
    enc_ref, slope_ref, slope_t_ref, v_ref, q_ref, k_ref, q_t_ref, attn_t_ref, grad_ref,
    normed_ref, nu_ref, gi_ref, xt_ref, mt_ref,
    gate_ref, mixed_ref, slope_u_ref,
):
    seq, width = x_ref.shape[1:]
    head = width // HEADS
    half_seq = seq // 2
    x = x_ref[0]
    for branch in range(4):
        cols = slice(branch * width, (branch + 1) * width)
        act, slope = silu_pair(0.5 * dot_nn(x, win_ref[:, cols]))
        if branch == 3:
            slope_t_ref[0] = jnp.transpose(0.5 * slope).astype(bf16)
        elif branch > 0:
            slope_ref[0, :, (branch - 1) * width : branch * width] = (0.5 * slope).astype(bf16)
        if branch == 0:
            gate_ref[...] = act
            slope_u_ref[...] = 0.5 * slope
        else:
            (v_ref, q_ref, k_ref)[branch - 1][0] = act.astype(bf16)
        if branch == 2:
            q_t_ref[0] = jnp.transpose(act).astype(bf16)
    masks = lane_masks(2 * head, head)
    scale = 0.5 * head**-0.5
    tri = iota((half_seq, half_seq), 0) >= iota((half_seq, half_seq), 1)
    zero = jnp.zeros((half_seq, half_seq), f32)
    for pair in range(HEADS // 2):
        cols = slice(pair * 2 * head, (pair + 1) * 2 * head)
        q_p = q_ref[0, :, cols] * jnp.asarray(scale, bf16)
        half = dot_nt(both_heads(q_p, masks), k_ref[0, :, cols])
        stack = []
        for j in range(2):
            h = 2 * pair + j
            top = silu_pair(half[j * seq : j * seq + half_seq, :half_seq])
            bot = silu_pair(half[j * seq + half_seq : (j + 1) * seq])
            full = []
            for a, b in zip(top, bot):
                a = jnp.concatenate([jnp.where(tri, a, 0.0), zero], axis=1)
                b = jnp.concatenate([b[:, :half_seq], jnp.where(tri, b[:, half_seq:], 0.0)], axis=1)
                full.append(jnp.concatenate([a, b], axis=0))
            stack.append(full[0].astype(bf16))
            attn_t_ref[0, h] = jnp.transpose(full[0]).astype(bf16)
            grad_ref[0, h] = full[1].astype(bf16)
        mixed = dot_nn(jnp.concatenate(stack, axis=0), v_ref[0, :, cols])
        mixed_ref[:, cols] = pick_lanes(mixed, head) * (1.0 / seq)
    mixed = mixed_ref[...]
    centred = mixed - jnp.mean(mixed, axis=1, keepdims=True)
    inv_std = lax.rsqrt(jnp.mean(centred * centred, axis=1, keepdims=True) + norm_eps)
    normed = centred * inv_std
    gate = gate_ref[...]
    merged = (normed * gate).astype(bf16)
    normed_ref[0] = normed.astype(bf16)
    nu_ref[0] = (normed * slope_u_ref[...]).astype(bf16)
    gi_ref[0] = (gate * inv_std).astype(bf16)
    enc_ref[0] = (x.astype(f32) + dot_nn(merged, wout_ref[...])).astype(bf16)
    perm = perm_ref[...]
    xt_ref[...] = dot_nt(perm, x).astype(bf16)
    mt_ref[...] = dot_nt(perm, merged).astype(bf16)


def layer_forward(x, w_in, w_out, perm):
    hist, seq, width = x.shape
    row = pl.BlockSpec((1, seq, width), lambda i: (i, 0, 0))
    wide = pl.BlockSpec((1, seq, 2 * width), lambda i: (i, 0, 0))
    column = pl.BlockSpec((1, width, seq), lambda i: (i, 0, 0))
    square = pl.BlockSpec((1, HEADS, seq, seq), lambda i: (i, 0, 0, 0))
    turned = pl.BlockSpec((width, seq), lambda i: (0, i))
    row_s = jax.ShapeDtypeStruct((hist, seq, width), bf16)
    column_s = jax.ShapeDtypeStruct((hist, width, seq), bf16)
    square_s = jax.ShapeDtypeStruct((hist, HEADS, seq, seq), bf16)
    turned_s = jax.ShapeDtypeStruct((width, hist * seq), bf16)
    return pl.pallas_call(
        forward_kernel,
        grid=(hist,),
        in_specs=[row, whole(w_in.shape), whole(w_out.shape), whole(perm.shape)],
        out_specs=[
            row, wide, column, row, row, row, column, square, square, row, row, row, turned, turned,
        ],
        out_shape=[
            row_s, jax.ShapeDtypeStruct((hist, seq, 2 * width), bf16), column_s, row_s, row_s, row_s,
            column_s, square_s, square_s, row_s, row_s, row_s, turned_s, turned_s,
        ],
        scratch_shapes=[pltpu.VMEM((seq, width), f32)] * 3,
        compiler_params=params(60),
        cost_estimate=cost(18e9, 24e6),
        name="forward",
    )(x, w_in, w_out, perm)


def group_slots(recv_ref, hist):
    slots, width = recv_ref.shape
    meta = recv_ref[:, width - META :].astype(f32)
    slot_h = meta[:, 0:1]
    valid = meta[:, 1:2] > 0.0
    lane = iota((slots, META), 1).astype(f32)
    hot = jnp.where(valid & (slot_h == lane), 1.0, 0.0)
    lower = (iota((slots, slots), 0) > iota((slots, slots), 1)).astype(f32).astype(bf16)
    rank = jnp.sum(dot_nn(lower, hot.astype(bf16)) * hot, axis=1, keepdims=True)
    starts, start = [], jnp.int32(0)
    begin = jnp.zeros((slots, 1), f32)
    for h in range(hist):
        starts.append(start)
        begin = jnp.where(slot_h == float(h), (start * TILE).astype(f32), begin)
        count = jnp.sum(hot[:, h : h + 1]).astype(jnp.int32)
        start = start + (count + (TILE - 1)) // TILE
    dest = jnp.where(valid, begin + rank, -1.0)
    eye = iota((slots, slots), 0) == iota((slots, slots), 1)
    dest_row = jnp.sum(jnp.where(eye, dest, 0.0), axis=0, keepdims=True).astype(jnp.int32)
    return dest_row, starts, start


def target_tile(tile, starts, dest_row, recv_ref, enc_ref, grouped_ref, turned_ref):
    seq, width = enc_ref.shape[1:]
    head = width // HEADS
    masks = lane_masks(2 * head, head)
    scale = 0.5 * head**-0.5
    base = pl.multiple_of(tile * TILE, TILE)
    hist = jnp.int32(0)
    for start in starts[1:]:
        hist = hist + (tile >= start).astype(jnp.int32)
    choose = (iota((TILE, dest_row.shape[1]), 0) + base == dest_row).astype(f32).astype(bf16)
    rows = dot_nn(choose, recv_ref[...])
    q_all = rows[:, :width] * scale
    g_all = rows[:, width : 2 * width]
    q_all = q_all.astype(bf16)
    g_all = g_all.astype(bf16)
    q_t = jnp.transpose(q_all)
    g_t = jnp.transpose(g_all)
    length = rows[:, 2 * width + 1 : 2 * width + 2]
    positions = iota((TILE, seq), 1).astype(f32)
    weight = jnp.where(positions < length, 1.0 / jnp.maximum(length, 1.0), 0.0)
    for pair in range(HEADS // 2):
        cols = slice(pair * 2 * head, (pair + 1) * 2 * head)
        k_p = enc_ref[hist, :, cols]
        both = dot_nt(
            jnp.concatenate(
                [both_heads(q_all[:, cols], masks), both_heads(g_all[:, cols], masks)], axis=0
            ),
            k_p,
        )
        slopes = []
        for j in range(2):
            h = 2 * pair + j
            mine = slice(h * head, (h + 1) * head)
            act, slope = silu_pair(both[j * TILE : (j + 1) * TILE])
            d_attn = both[(2 + j) * TILE : (3 + j) * TILE]
            attn = (act * weight).astype(bf16)
            d_s = (d_attn * weight * slope).astype(bf16)
            turned_ref[hist, mine, :] += dot_nn(
                jnp.concatenate([g_t[mine], q_t[mine]], axis=1),
                jnp.concatenate([attn, d_s], axis=0),
            )
            slopes.append(d_s)
        d_q = pick_lanes(dot_nn(jnp.concatenate(slopes, axis=0), k_p), head)
        grouped_ref[pl.ds(base, TILE), cols] = (d_q * scale).astype(bf16)


def norm_backward(denc_ref, wout_ref, normed_ref, nu_ref, gi_ref, dmix_ref, dpre_ref):
    hist, seq, width = denc_ref.shape
    for at in range(hist):
        here = slice(at * seq, (at + 1) * seq)
        d_merged = dot_nt(denc_ref[at], wout_ref[...])
        dpre_ref[here, :width] = (d_merged * nu_ref[at].astype(f32)).astype(bf16)
        normed = normed_ref[at].astype(f32)
        d_norm = d_merged * gi_ref[at].astype(f32)
        d_mix = (
            d_norm
            - jnp.mean(d_norm, axis=1, keepdims=True)
            - normed * jnp.mean(d_norm * normed, axis=1, keepdims=True)
        )
        dmix_ref[at] = d_mix.astype(bf16)


def attention_backward(
    at, dmix_ref, v_ref, k_ref, q_t_ref, attn_t_ref, grad_ref, slope_ref, slope_t_ref, dpre_ref, dk_ref
):
    seq, width = dmix_ref.shape[1:]
    head = width // HEADS
    here = slice(at * seq, (at + 1) * seq)
    masks = lane_masks(2 * head, head)
    scale = 0.5 * head**-0.5 / seq
    for pair in range(HEADS // 2):
        cols = slice(pair * 2 * head, (pair + 1) * 2 * head)
        d_p = dmix_ref[at, :, cols]
        d_attn = dot_nt(both_heads(d_p, masks), v_ref[at, :, cols])
        d_s = [
            (d_attn[j * seq : (j + 1) * seq] * grad_ref[at, 2 * pair + j].astype(f32)).astype(bf16)
            for j in range(2)
        ]
        attn_t = jnp.concatenate([attn_t_ref[at, 2 * pair], attn_t_ref[at, 2 * pair + 1]], axis=0)
        d_v = pick_lanes(dot_nn(attn_t, d_p), head) * (1.0 / seq)
        d_q = pick_lanes(dot_nn(jnp.concatenate(d_s, axis=0), k_ref[at, :, cols]), head) * scale
        for branch, grad in ((0, d_v), (1, d_q)):
            old = slice(branch * width + pair * 2 * head, branch * width + (pair + 1) * 2 * head)
            new = slice(old.start + width, old.stop + width)
            dpre_ref[here, new] = (grad * slope_ref[at, :, old].astype(f32)).astype(bf16)
        for j in range(2):
            mine = slice((2 * pair + j) * head, (2 * pair + j + 1) * head)
            d_k = dot_nn(q_t_ref[at, mine], d_s[j]) * scale
            dk_ref[mine, here] = (d_k * slope_t_ref[at, mine].astype(f32)).astype(bf16)


def return_order(sizes, capacity, me_ref, dest_row):
    n_y, n_core, n_z, n_x = sizes
    slots = dest_row.shape[1]
    place = iota((slots, 1), 0)
    inner, block = place % capacity, place // capacity
    x, y = block % n_x, block // n_x % n_y
    z, core = block // (n_x * n_y) % n_z, block // (n_x * n_y * n_z)
    y, core, z, x = ((me_ref[i] + at) % n for i, (at, n) in enumerate(zip((y, core, z, x), sizes)))
    source = (((y * n_core + core) * n_z + z) * n_x + x) * capacity + inner
    hit = source == iota((slots, slots), 1)
    return jnp.sum(jnp.where(hit, dest_row.astype(f32), 0.0), axis=1, keepdims=True).astype(jnp.int32)


def owner_kernel(sizes, capacity, me_ref, *refs):
    n_in, n_out = 15, 6
    sources, outs, refs = refs[:n_in], refs[n_in : n_in + n_out], refs[n_in + n_out :]
    held, refs = refs[:n_in], refs[n_in:]
    (
        recv_ref, enc_ref, wout_ref, normed_ref, nu_ref, gi_ref, v_ref, k_ref, q_t_ref,
        attn_t_ref, grad_ref, slope_ref, slope_t_ref, mt_ref, xt_ref,
    ) = held
    grouped_ref, turned_ref, dmix_ref, dq_ref, denc_ref, dpre_ref, dk_ref, keep_ref, send_ref, sem_in, sem_out = refs
    dq_hbm, denc_hbm, dpre_hbm, dk_hbm, keep_hbm, send_hbm = outs
    hist, seq, width = enc_ref.shape
    slots, padded = recv_ref.shape[0], grouped_ref.shape[0]
    kept = keep_ref.shape[0]

    def load(i, n, at=None):
        source, dest = (sources[i], held[i]) if at is None else (sources[i].at[at], held[i].at[at])
        return pltpu.make_async_copy(source, dest, sem_in.at[n])

    first = [load(i, i) for i in range(6)]
    by_history = [[load(i, i + 7 * at, at) for i in range(6, 13)] for at in range(hist)]
    last = [load(i, 7 * hist + i - 7) for i in (13, 14)]
    for copy in first[:2]:
        copy.start()
    grouped_ref[...] = jnp.zeros_like(grouped_ref)
    turned_ref[...] = jnp.zeros_like(turned_ref)
    first[0].wait()
    first[1].wait()
    for copy in first[2:] + sum(by_history, []) + last:
        copy.start()
    dest_row, starts, tiles = group_slots(recv_ref, hist)

    def one_tile(tile, carry):
        target_tile(tile, starts, dest_row, recv_ref, enc_ref, grouped_ref, turned_ref)
        return carry

    lax.fori_loop(0, tiles, one_tile, 0)
    unit = (iota((seq, seq), 0) == iota((seq, seq), 1)).astype(f32).astype(bf16)
    for h in range(hist):
        denc_ref[h] = dot_nt(unit, turned_ref[h].astype(bf16)).astype(bf16)
    dest = return_order(sizes, capacity, me_ref, dest_row)
    back = (dest == iota((slots, padded), 1)).astype(f32).astype(bf16)
    dq_ref[...] = dot_nn(back, grouped_ref[...]).astype(bf16)
    stores = []

    def store(source, dest):
        copy = pltpu.make_async_copy(source, dest, sem_out.at[len(stores)])
        copy.start()
        stores.append(copy)

    store(denc_ref, denc_hbm)
    store(dq_ref, dq_hbm)
    for copy in first[2:]:
        copy.wait()
    norm_backward(denc_ref, wout_ref, normed_ref, nu_ref, gi_ref, dmix_ref, dpre_ref)
    for at in range(hist):
        for copy in by_history[at]:
            copy.wait()
        attention_backward(
            at, dmix_ref, v_ref, k_ref, q_t_ref, attn_t_ref, grad_ref, slope_ref, slope_t_ref,
            dpre_ref, dk_ref,
        )
        here = pl.ds(at * seq, seq)
        store(dpre_ref.at[here, :], dpre_hbm.at[here, :])
        store(dk_ref.at[:, here], dk_hbm.at[:, here])
    for copy in last:
        copy.wait()
    for block in range(5):
        cols = slice(block * width, (block + 1) * width)
        if block == 0:
            part = dot_nn(mt_ref[...], denc_ref[...].reshape(hist * seq, width))
        elif block == 4:
            part = dot_nt(xt_ref[...], dk_ref[...])
        else:
            part = dot_nn(xt_ref[...], dpre_ref[:, (block - 1) * width : block * width])
        keep_ref[:, cols] = part[:kept].astype(bf16)
        send_ref[:, cols] = part[kept:].astype(bf16)
        store(keep_ref.at[:, cols], keep_hbm.at[:, cols])
        store(send_ref.at[:, cols], send_hbm.at[:, cols])
    for copy in stores:
        copy.wait()


def owner_backward(me, sizes, recv, enc, w_out, state, mt, xt, kept):
    hist, seq, width = enc.shape
    slots = recv.shape[0]
    rows = hist * seq
    padded = ((slots - hist) // TILE + hist) * TILE
    operands = (recv, enc, w_out) + state + (mt, xt)
    raw = pl.BlockSpec(memory_space=pl.ANY)
    outs = [
        jax.ShapeDtypeStruct((slots, width), bf16),
        jax.ShapeDtypeStruct(enc.shape, bf16),
        jax.ShapeDtypeStruct((rows, 3 * width), bf16),
        jax.ShapeDtypeStruct((width, rows), bf16),
        jax.ShapeDtypeStruct((kept, 5 * width), bf16),
        jax.ShapeDtypeStruct((width - kept, 5 * width), bf16),
    ]
    return pl.pallas_call(
        functools.partial(owner_kernel, sizes, slots // math.prod(sizes)),
        grid=(1,),
        in_specs=[pl.BlockSpec(memory_space=pltpu.SMEM)] + [raw] * len(operands),
        out_specs=[raw] * len(outs),
        out_shape=outs,
        scratch_shapes=[pltpu.VMEM(a.shape, a.dtype) for a in operands]
        + [
            pltpu.VMEM((padded, width), bf16),
            pltpu.VMEM((hist, width, seq), f32),
            pltpu.VMEM((hist, seq, width), bf16),
        ]
        + [pltpu.VMEM(a.shape, a.dtype) for a in outs]
        + [
            pltpu.SemaphoreType.DMA((7 * hist + 8,)),
            pltpu.SemaphoreType.DMA((2 * hist + 12,)),
        ],
        compiler_params=params(60),
        cost_estimate=cost(30e9, 30e6),
        name="owner_backward",
    )(me, *operands)


def input_kernel(denc_ref, win_ref, dpre_ref, dk_ref, out_ref):
    width = denc_ref.shape[2]
    total = denc_ref[0].astype(f32) + dot_nt(dpre_ref[...], win_ref[:, : 3 * width])
    total = total + dot_nt(jnp.transpose(dk_ref[...]), win_ref[:, 3 * width :])
    out_ref[0] = total.astype(bf16)


def input_backward(denc, w_in, dpre, dk):
    hist, seq, width = denc.shape
    block = lambda a: pl.BlockSpec((1,) + a.shape[1:], lambda i: (i, 0, 0))
    return pl.pallas_call(
        input_kernel,
        grid=(hist,),
        in_specs=[
            block(denc),
            whole(w_in.shape),
            pl.BlockSpec((seq, 3 * width), lambda i: (i, 0)),
            pl.BlockSpec((width, seq), lambda i: (0, i)),
        ],
        out_specs=block(denc),
        out_shape=jax.ShapeDtypeStruct(denc.shape, bf16),
        compiler_params=params(60),
        cost_estimate=cost(6e9, 8e6),
        name="input_backward",
    )(denc, w_in, dpre, dk)


def owner_order(width):
    n_y, n_core, n_z, n_x = (lax.axis_size(a) for a in AXES)
    rows = width // (n_y * n_core * n_z * n_x)
    place = jnp.arange(width, dtype=jnp.int32)
    inner = place % rows
    place = place // rows
    z, place = place % n_z, place // n_z
    x, place = place % n_x, place // n_x
    y, d_core = place % n_y, place // n_y
    core = (lax.axis_index(AXES[1]) + d_core) % n_core
    y, x = (lax.axis_index(AXES[0]) + y) % n_y, (lax.axis_index(AXES[3]) + x) % n_x
    z = (lax.axis_index(AXES[2]) + z) % n_z
    source = (((y * n_core + core) * n_z + z) * n_x + x) * rows + inner
    return (source[:, None] == jnp.arange(width, dtype=jnp.int32)[None, :]).astype(bf16)


def add_up(blocks):
    total = blocks[0].astype(f32)
    for block in blocks[1:]:
        total = total + block.astype(f32)
    return total


def core_stage(keep, send):
    return add_up(send_blocks([keep] + cut_rows(send, lax.axis_size(AXES[1]) - 1), AXES[1:2])).astype(bf16)


def send_blocks(blocks, axes):
    count = len(blocks)
    sizes = [lax.axis_size(a) for a in axes]
    parts = [blocks[0]]
    for d in range(1, count):
        pairs = []
        for c in range(count):
            there, stride, rest_c, rest_d = 0, 1, c, d
            for n in reversed(sizes):
                there += (rest_c + rest_d) % n * stride
                stride, rest_c, rest_d = stride * n, rest_c // n, rest_d // n
            pairs.append((c, there))
        parts.append(lax.ppermute(blocks[d], axes, pairs))
    return parts


def cut_rows(rows, count):
    step = rows.shape[0] // count
    return [rows[i * step : (i + 1) * step] for i in range(count)]


def local(histories, weight_in, weight_out, candidates, cotangent, owner_ids, hist_slot, lengths):
    devices = lax.axis_size(AXES)
    imp_rows, width = candidates.shape
    capacity = max(2, 2 * imp_rows // devices)
    slots = devices * capacity
    kept = width // lax.axis_size(AXES[1])
    after = lax.optimization_barrier

    sizes = n_y, n_core, n_z, n_x = tuple(lax.axis_size(a) for a in AXES)
    me = jnp.stack([lax.axis_index(a) for a in AXES]).astype(jnp.int32)
    core, line, plane = AXES[1:2], AXES[2:3], (AXES[0], AXES[3])
    send, pick = route(me, owner_ids, hist_slot, lengths, candidates, cotangent, sizes, capacity)
    shaped = send.reshape(devices, capacity, send.shape[1])
    recv = lax.all_to_all(shaped, AXES, split_axis=0, concat_axis=0, tiled=True)
    recv = recv.reshape(slots, send.shape[1])
    perm = owner_order(width)
    enc, slope, slope_t, v, q, k, q_t, attn_t, grad, normed, nu, gi, xt, mt = layer_forward(
        histories, weight_in, weight_out, perm
    )
    state = (normed, nu, gi, v, k, q_t, attn_t, grad, slope, slope_t)
    d_query, d_enc, dpre, dk, keep, send = owner_backward(
        me, sizes, recv, enc, weight_out, state, mt, xt, kept
    )
    rows = core_stage(keep, send)
    back = [cut_rows(b, n_z) for b in send_blocks(cut_rows(d_query, n_core), core)]
    d_enc, rows, back = after((d_enc, rows, back))
    back = [jnp.concatenate([b[d] for b in back], axis=0) for d in range(n_z)]
    d_inputs = input_backward(d_enc, weight_in, dpre, dk)
    parts = send_blocks(cut_rows(rows, n_y * n_x), plane)
    back = send_blocks(back, line)
    parts, back, d_inputs = after((parts, back, d_inputs))
    parts = send_blocks(cut_rows(add_up(parts).astype(bf16), n_z), line)
    back = [b.reshape(n_core, n_y * n_x, capacity, width) for b in back]
    back = [
        jnp.concatenate([b[:, i].reshape(n_core * capacity, width) for b in back], axis=0)
        for i in range(n_y * n_x)
    ]
    returned = jnp.concatenate(send_blocks(back, plane), axis=0)
    candidate_grad = lax.dot_general(
        pick, returned, (((0,), (0,)), ((), ())), preferred_element_type=f32
    ).astype(bf16)
    w_in_grad = add_up([p[:, width:] for p in parts])
    w_out_grad = add_up([p[:, :width] for p in parts])
    return d_inputs, candidate_grad, w_in_grad, w_out_grad


def solution(mesh):
    n_hash, n_dp = mesh.devices.shape
    fine = jax.sharding.Mesh(mesh.devices.reshape(n_hash // 2, 2, n_dp // 2, 2), AXES)
    return jax.shard_map(
        local,
        mesh=fine,
        in_specs=(
            P(AXES, None, None),
            P(),
            P(),
            P(AXES, None),
            P(AXES, None),
            P(AXES, None),
            P(AXES),
            P(AXES),
        ),
        out_specs=(
            P(AXES, None, None),
            P(AXES, None),
            P(AXES, None),
            P(AXES, None),
        ),
        check_vma=False,
    )
```

```python
import functools
import math

import jax
import jax.numpy as jnp
from jax import lax
from jax.experimental import pallas as pl
from jax.experimental.pallas import tpu as pltpu
from jax.sharding import PartitionSpec as P

HEADS = 8
TILE = 128
META = 128
AXES = ("hash_hi", "core", "dp_hi", "dp_lo")
norm_eps = 1e-05
f32 = jnp.float32
bf16 = jnp.bfloat16
MIB = 1024 * 1024


def dot_nn(a, b):
    return lax.dot_general(a, b, (((1,), (0,)), ((), ())), preferred_element_type=f32)


def dot_nt(a, b):
    return lax.dot_general(a, b, (((1,), (1,)), ((), ())), preferred_element_type=f32)


def dot_tn(a, b):
    return lax.dot_general(a, b, (((0,), (0,)), ((), ())), preferred_element_type=f32)


def iota(shape, axis):
    return lax.broadcasted_iota(jnp.int32, shape, axis)


def silu_pair(half):
    t = jnp.tanh(half)
    u = 1.0 + t
    act = half * u
    return act, u + act * (1.0 - t)


def lane_masks(width, part):
    lane = iota((1, width), 1)
    return [((lane >= j * part) & (lane < (j + 1) * part)).astype(bf16) for j in range(width // part)]


def both_heads(pair, masks):
    return jnp.concatenate([pair * m for m in masks], axis=0)


def pick_lanes(stacked, head):
    rows = stacked.shape[0] // 2
    lane = iota((1, 2 * head), 1)
    return jnp.where(lane < head, stacked[:rows], stacked[rows:])


def params(mib):
    return pltpu.CompilerParams(dimension_semantics=("arbitrary",), vmem_limit_bytes=mib * MIB)


def whole(shape):
    return pl.BlockSpec(shape, lambda i: (0,) * len(shape))


def cost(flops, nbytes, trans=0):
    return pl.CostEstimate(flops=int(flops), bytes_accessed=int(nbytes), transcendentals=int(trans))


def route_kernel(sizes, capacity, me_ref, own_ref, slot_ref, len_ref, cand_ref, cot_ref, send_ref, pick_ref):
    n_y, n_core, n_z, n_x = sizes
    devices = n_y * n_core * n_z * n_x
    rows, width = cand_ref.shape
    slots = devices * capacity
    own = own_ref[...]
    hot = (own == iota((devices, rows), 0)).astype(f32)
    before = (iota((rows, rows), 0) < iota((rows, rows), 1)).astype(f32).astype(bf16)
    earlier = dot_nn(hot.astype(bf16), before)
    position = jnp.sum(earlier * hot, axis=0, keepdims=True).astype(jnp.int32)
    target = own * capacity + position
    pick = (target == iota((slots, rows), 0)).astype(f32).astype(bf16)
    x, z = own % n_x, own // n_x % n_z
    core, y = own // (n_x * n_z) % n_core, own // (n_x * n_z * n_core)
    y, core, z, x = (
        (me_ref[i] - at + n) % n for i, (at, n) in enumerate(zip((y, core, z, x), sizes))
    )
    back = (((y * n_x + x) * n_z + z) * n_core + core) * capacity + position
    pick_ref[...] = (back == iota((slots, rows), 0)).astype(f32).astype(bf16)
    send_ref[:, :width] = dot_nn(pick, cand_ref[...]).astype(bf16)
    send_ref[:, width : 2 * width] = dot_nn(pick, cot_ref[...]).astype(bf16)
    line = iota((META, rows), 0)
    meta = jnp.where(line == 0, slot_ref[...], jnp.where(line == 1, len_ref[...], 0))
    send_ref[:, 2 * width :] = dot_nt(pick, meta.astype(f32).astype(bf16)).astype(bf16)


def route(me, own, slot, length, cand, cot, sizes, capacity):
    rows, width = cand.shape
    slots = math.prod(sizes) * capacity
    line = whole((1, rows))
    return pl.pallas_call(
        functools.partial(route_kernel, sizes, capacity),
        grid=(1,),
        in_specs=[
            pl.BlockSpec(memory_space=pltpu.SMEM), line, line, line, whole(cand.shape), whole(cot.shape),
        ],
        out_specs=[whole((slots, 2 * width + META)), whole((slots, rows))],
        out_shape=(
            jax.ShapeDtypeStruct((slots, 2 * width + META), bf16),
            jax.ShapeDtypeStruct((slots, rows), bf16),
        ),
        compiler_params=params(60),
        cost_estimate=cost(2e9, 4 * rows * width * 4),
        name="route",
    )(me, own.reshape(1, rows), slot.reshape(1, rows), length.reshape(1, rows), cand, cot)


def forward_kernel(
    x_ref, win_ref, wout_ref, perm_ref,
    enc_ref, slope_ref, slope_t_ref, v_ref, q_ref, k_ref, q_t_ref, attn_t_ref, grad_ref,
    normed_ref, nu_ref, gi_ref, xt_ref, mt_ref,
    gate_ref, mixed_ref, slope_u_ref,
):
    seq, width = x_ref.shape[1:]
    head = width // HEADS
    half_seq = seq // 2
    x = x_ref[0]
    for branch in range(4):
        cols = slice(branch * width, (branch + 1) * width)
        act, slope = silu_pair(0.5 * dot_nn(x, win_ref[:, cols]))
        if branch == 3:
            slope_t_ref[0] = jnp.transpose(0.5 * slope).astype(bf16)
        elif branch > 0:
            slope_ref[0, :, (branch - 1) * width : branch * width] = (0.5 * slope).astype(bf16)
        if branch == 0:
            gate_ref[...] = act
            slope_u_ref[...] = 0.5 * slope
        else:
            (v_ref, q_ref, k_ref)[branch - 1][0] = act.astype(bf16)
        if branch == 2:
            q_t_ref[0] = jnp.transpose(act).astype(bf16)
    masks = lane_masks(2 * head, head)
    scale = 0.5 * head**-0.5
    tri = iota((half_seq, half_seq), 0) >= iota((half_seq, half_seq), 1)
    zero = jnp.zeros((half_seq, half_seq), f32)
    for pair in range(HEADS // 2):
        cols = slice(pair * 2 * head, (pair + 1) * 2 * head)
        q_p = q_ref[0, :, cols] * jnp.asarray(scale, bf16)
        half = dot_nt(both_heads(q_p, masks), k_ref[0, :, cols])
        stack = []
        for j in range(2):
            h = 2 * pair + j
            top = silu_pair(half[j * seq : j * seq + half_seq, :half_seq])
            bot = silu_pair(half[j * seq + half_seq : (j + 1) * seq])
            full = []
            for a, b in zip(top, bot):
                a = jnp.concatenate([jnp.where(tri, a, 0.0), zero], axis=1)
                b = jnp.concatenate([b[:, :half_seq], jnp.where(tri, b[:, half_seq:], 0.0)], axis=1)
                full.append(jnp.concatenate([a, b], axis=0))
            stack.append(full[0].astype(bf16))
            attn_t_ref[0, h] = jnp.transpose(full[0]).astype(bf16)
            grad_ref[0, h] = full[1].astype(bf16)
        mixed = dot_nn(jnp.concatenate(stack, axis=0), v_ref[0, :, cols])
        mixed_ref[:, cols] = pick_lanes(mixed, head) * (1.0 / seq)
    mixed = mixed_ref[...]
    centred = mixed - jnp.mean(mixed, axis=1, keepdims=True)
    inv_std = lax.rsqrt(jnp.mean(centred * centred, axis=1, keepdims=True) + norm_eps)
    normed = centred * inv_std
    gate = gate_ref[...]
    merged = (normed * gate).astype(bf16)
    normed_ref[0] = normed.astype(bf16)
    nu_ref[0] = (normed * slope_u_ref[...]).astype(bf16)
    gi_ref[0] = (gate * inv_std).astype(bf16)
    enc_ref[0] = (x.astype(f32) + dot_nn(merged, wout_ref[...])).astype(bf16)
    perm = perm_ref[...]
    xt_ref[...] = dot_nt(perm, x).astype(bf16)
    mt_ref[...] = dot_nt(perm, merged).astype(bf16)


def layer_forward(x, w_in, w_out, perm):
    hist, seq, width = x.shape
    row = pl.BlockSpec((1, seq, width), lambda i: (i, 0, 0))
    wide = pl.BlockSpec((1, seq, 2 * width), lambda i: (i, 0, 0))
    column = pl.BlockSpec((1, width, seq), lambda i: (i, 0, 0))
    square = pl.BlockSpec((1, HEADS, seq, seq), lambda i: (i, 0, 0, 0))
    turned = pl.BlockSpec((width, seq), lambda i: (0, i))
    row_s = jax.ShapeDtypeStruct((hist, seq, width), bf16)
    column_s = jax.ShapeDtypeStruct((hist, width, seq), bf16)
    square_s = jax.ShapeDtypeStruct((hist, HEADS, seq, seq), bf16)
    turned_s = jax.ShapeDtypeStruct((width, hist * seq), bf16)
    return pl.pallas_call(
        forward_kernel,
        grid=(hist,),
        in_specs=[row, whole(w_in.shape), whole(w_out.shape), whole(perm.shape)],
        out_specs=[
            row, wide, column, row, row, row, column, square, square, row, row, row, turned, turned,
        ],
        out_shape=[
            row_s, jax.ShapeDtypeStruct((hist, seq, 2 * width), bf16), column_s, row_s, row_s, row_s,
            column_s, square_s, square_s, row_s, row_s, row_s, turned_s, turned_s,
        ],
        scratch_shapes=[pltpu.VMEM((seq, width), f32)] * 3,
        compiler_params=params(60),
        cost_estimate=cost(18e9, 24e6),
        name="forward",
    )(x, w_in, w_out, perm)


def group_slots(recv_ref, hist):
    slots, width = recv_ref.shape
    meta = recv_ref[:, width - META :].astype(f32)
    slot_h = meta[:, 0:1]
    valid = meta[:, 1:2] > 0.0
    lane = iota((slots, META), 1).astype(f32)
    hot = jnp.where(valid & (slot_h == lane), 1.0, 0.0)
    lower = (iota((slots, slots), 0) > iota((slots, slots), 1)).astype(f32).astype(bf16)
    rank = jnp.sum(dot_nn(lower, hot.astype(bf16)) * hot, axis=1, keepdims=True)
    starts, start = [], jnp.int32(0)
    begin = jnp.zeros((slots, 1), f32)
    for h in range(hist):
        starts.append(start)
        begin = jnp.where(slot_h == float(h), (start * TILE).astype(f32), begin)
        count = jnp.sum(hot[:, h : h + 1]).astype(jnp.int32)
        start = start + (count + (TILE - 1)) // TILE
    dest = jnp.where(valid, begin + rank, -1.0)
    eye = iota((slots, slots), 0) == iota((slots, slots), 1)
    dest_row = jnp.sum(jnp.where(eye, dest, 0.0), axis=0, keepdims=True).astype(jnp.int32)
    return dest_row, starts, start


def target_tile(tile, starts, dest_row, recv_ref, enc_ref, grouped_ref, turned_ref):
    seq, width = enc_ref.shape[1:]
    head = width // HEADS
    masks = lane_masks(2 * head, head)
    scale = 0.5 * head**-0.5
    base = pl.multiple_of(tile * TILE, TILE)
    hist = jnp.int32(0)
    for start in starts[1:]:
        hist = hist + (tile >= start).astype(jnp.int32)
    choose = (iota((TILE, dest_row.shape[1]), 0) + base == dest_row).astype(f32).astype(bf16)
    rows = dot_nn(choose, recv_ref[...])
    q_all = rows[:, :width] * scale
    g_all = rows[:, width : 2 * width]
    q_all = q_all.astype(bf16)
    g_all = g_all.astype(bf16)
    q_t = jnp.transpose(q_all)
    g_t = jnp.transpose(g_all)
    length = rows[:, 2 * width + 1 : 2 * width + 2]
    positions = iota((TILE, seq), 1).astype(f32)
    weight = jnp.where(positions < length, 1.0 / jnp.maximum(length, 1.0), 0.0)
    for pair in range(HEADS // 2):
        cols = slice(pair * 2 * head, (pair + 1) * 2 * head)
        k_p = enc_ref[hist, :, cols]
        both = dot_nt(
            jnp.concatenate(
                [both_heads(q_all[:, cols], masks), both_heads(g_all[:, cols], masks)], axis=0
            ),
            k_p,
        )
        slopes = []
        for j in range(2):
            h = 2 * pair + j
            mine = slice(h * head, (h + 1) * head)
            act, slope = silu_pair(both[j * TILE : (j + 1) * TILE])
            d_attn = both[(2 + j) * TILE : (3 + j) * TILE]
            attn = (act * weight).astype(bf16)
            d_s = (d_attn * weight * slope).astype(bf16)
            turned_ref[hist, mine, :] += dot_nn(
                jnp.concatenate([g_t[mine], q_t[mine]], axis=1),
                jnp.concatenate([attn, d_s], axis=0),
            )
            slopes.append(d_s)
        d_q = pick_lanes(dot_nn(jnp.concatenate(slopes, axis=0), k_p), head)
        grouped_ref[pl.ds(base, TILE), cols] = (d_q * scale).astype(bf16)


def norm_backward(denc_ref, wout_ref, normed_ref, nu_ref, gi_ref, dmix_ref, dpre_ref):
    hist, seq, width = denc_ref.shape
    for at in range(hist):
        here = slice(at * seq, (at + 1) * seq)
        d_merged = dot_nt(denc_ref[at], wout_ref[...])
        dpre_ref[here, :width] = (d_merged * nu_ref[at].astype(f32)).astype(bf16)
        normed = normed_ref[at].astype(f32)
        d_norm = d_merged * gi_ref[at].astype(f32)
        d_mix = (
            d_norm
            - jnp.mean(d_norm, axis=1, keepdims=True)
            - normed * jnp.mean(d_norm * normed, axis=1, keepdims=True)
        )
        dmix_ref[at] = d_mix.astype(bf16)


def attention_backward(
    at, dmix_ref, v_ref, k_ref, q_t_ref, attn_t_ref, grad_ref, slope_ref, slope_t_ref, dpre_ref, dk_ref
):
    seq, width = dmix_ref.shape[1:]
    head = width // HEADS
    here = slice(at * seq, (at + 1) * seq)
    masks = lane_masks(2 * head, head)
    scale = 0.5 * head**-0.5 / seq
    for pair in range(HEADS // 2):
        cols = slice(pair * 2 * head, (pair + 1) * 2 * head)
        d_p = dmix_ref[at, :, cols]
        d_attn = dot_nt(both_heads(d_p, masks), v_ref[at, :, cols])
        d_s = [
            (d_attn[j * seq : (j + 1) * seq] * grad_ref[at, 2 * pair + j].astype(f32)).astype(bf16)
            for j in range(2)
        ]
        attn_t = jnp.concatenate([attn_t_ref[at, 2 * pair], attn_t_ref[at, 2 * pair + 1]], axis=0)
        d_v = pick_lanes(dot_nn(attn_t, d_p), head) * (1.0 / seq)
        d_q = pick_lanes(dot_nn(jnp.concatenate(d_s, axis=0), k_ref[at, :, cols]), head) * scale
        for branch, grad in ((0, d_v), (1, d_q)):
            old = slice(branch * width + pair * 2 * head, branch * width + (pair + 1) * 2 * head)
            new = slice(old.start + width, old.stop + width)
            dpre_ref[here, new] = (grad * slope_ref[at, :, old].astype(f32)).astype(bf16)
        for j in range(2):
            mine = slice((2 * pair + j) * head, (2 * pair + j + 1) * head)
            d_k = dot_nn(q_t_ref[at, mine], d_s[j]) * scale
            dk_ref[mine, here] = (d_k * slope_t_ref[at, mine].astype(f32)).astype(bf16)


def return_order(sizes, capacity, me_ref, dest_row):
    n_y, n_core, n_z, n_x = sizes
    slots = dest_row.shape[1]
    place = iota((slots, 1), 0)
    inner, block = place % capacity, place // capacity
    x, y = block % n_x, block // n_x % n_y
    z, core = block // (n_x * n_y) % n_z, block // (n_x * n_y * n_z)
    y, core, z, x = ((me_ref[i] + at) % n for i, (at, n) in enumerate(zip((y, core, z, x), sizes)))
    source = (((y * n_core + core) * n_z + z) * n_x + x) * capacity + inner
    hit = source == iota((slots, slots), 1)
    return jnp.sum(jnp.where(hit, dest_row.astype(f32), 0.0), axis=1, keepdims=True).astype(jnp.int32)


def owner_kernel(sizes, capacity, me_ref, recv_ref, *refs):
    n_in, n_out = 14, 7
    sources, outs, refs = refs[:n_in], refs[n_in : n_in + n_out], refs[n_in + n_out :]
    held, refs = refs[:n_in], refs[n_in:]
    (
        enc_ref, wout_ref, normed_ref, nu_ref, gi_ref, v_ref, k_ref, q_t_ref,
        attn_t_ref, grad_ref, slope_ref, slope_t_ref, mt_ref, xt_ref,
    ) = held
    grouped_ref, turned_ref, dmix_ref, dq_ref, dq_far_ref, denc_ref, dpre_ref, dk_ref, keep_ref, send_ref, sem_in, sem_out = refs
    dq_hbm, dq_far_hbm, denc_hbm, dpre_hbm, dk_hbm, keep_hbm, send_hbm = outs
    hist, seq, width = enc_ref.shape
    slots, padded = recv_ref.shape[0], grouped_ref.shape[0]
    kept = keep_ref.shape[0]

    def load(i, n, at=None):
        source, dest = (sources[i], held[i]) if at is None else (sources[i].at[at], held[i].at[at])
        return pltpu.make_async_copy(source, dest, sem_in.at[n])

    first = [load(i, i) for i in range(5)]
    by_history = [[load(i, i + 7 * at, at) for i in range(5, 12)] for at in range(hist)]
    last = [load(i, 7 * hist + i - 7) for i in (12, 13)]
    for copy in first + sum(by_history, []) + last:
        copy.start()
    grouped_ref[...] = jnp.zeros_like(grouped_ref)
    turned_ref[...] = jnp.zeros_like(turned_ref)
    dest_row, starts, tiles = group_slots(recv_ref, hist)
    first[0].wait()

    def one_tile(tile, carry):
        target_tile(tile, starts, dest_row, recv_ref, enc_ref, grouped_ref, turned_ref)
        return carry

    lax.fori_loop(0, tiles, one_tile, 0)
    unit = (iota((seq, seq), 0) == iota((seq, seq), 1)).astype(f32).astype(bf16)
    for h in range(hist):
        denc_ref[h] = dot_nt(unit, turned_ref[h].astype(bf16)).astype(bf16)
    dest = return_order(sizes, capacity, me_ref, dest_row)
    back = (dest == iota((slots, padded), 1)).astype(f32).astype(bf16)
    near = dq_ref.shape[0]
    dq_ref[...] = dot_nn(back[:near], grouped_ref[...]).astype(bf16)
    dq_far_ref[...] = dot_nn(back[near:], grouped_ref[...]).astype(bf16)
    stores = []

    def store(source, dest):
        copy = pltpu.make_async_copy(source, dest, sem_out.at[len(stores)])
        copy.start()
        stores.append(copy)

    store(denc_ref, denc_hbm)
    store(dq_ref, dq_hbm)
    store(dq_far_ref, dq_far_hbm)
    for copy in first[1:]:
        copy.wait()
    norm_backward(denc_ref, wout_ref, normed_ref, nu_ref, gi_ref, dmix_ref, dpre_ref)
    for at in range(hist):
        for copy in by_history[at]:
            copy.wait()
        attention_backward(
            at, dmix_ref, v_ref, k_ref, q_t_ref, attn_t_ref, grad_ref, slope_ref, slope_t_ref,
            dpre_ref, dk_ref,
        )
        here = pl.ds(at * seq, seq)
        store(dpre_ref.at[here, :], dpre_hbm.at[here, :])
        store(dk_ref.at[:, here], dk_hbm.at[:, here])
    for copy in last:
        copy.wait()
    for block in range(5):
        cols = slice(block * width, (block + 1) * width)
        if block == 0:
            part = dot_nn(mt_ref[...], denc_ref[...].reshape(hist * seq, width))
        elif block == 4:
            part = dot_nt(xt_ref[...], dk_ref[...])
        else:
            part = dot_nn(xt_ref[...], dpre_ref[:, (block - 1) * width : block * width])
        keep_ref[:, cols] = part[:kept].astype(bf16)
        send_ref[:, cols] = part[kept:].astype(bf16)
        store(keep_ref.at[:, cols], keep_hbm.at[:, cols])
        store(send_ref.at[:, cols], send_hbm.at[:, cols])
    for copy in stores:
        copy.wait()


def owner_backward(me, sizes, recv, enc, w_out, state, mt, xt, kept):
    hist, seq, width = enc.shape
    slots = recv.shape[0]
    rows = hist * seq
    padded = ((slots - hist) // TILE + hist) * TILE
    operands = (enc, w_out) + state + (mt, xt)
    raw = pl.BlockSpec(memory_space=pl.ANY)
    outs = [
        jax.ShapeDtypeStruct((slots // sizes[1], width), bf16),
        jax.ShapeDtypeStruct((slots - slots // sizes[1], width), bf16),
        jax.ShapeDtypeStruct(enc.shape, bf16),
        jax.ShapeDtypeStruct((rows, 3 * width), bf16),
        jax.ShapeDtypeStruct((width, rows), bf16),
        jax.ShapeDtypeStruct((kept, 5 * width), bf16),
        jax.ShapeDtypeStruct((width - kept, 5 * width), bf16),
    ]
    return pl.pallas_call(
        functools.partial(owner_kernel, sizes, slots // math.prod(sizes)),
        grid=(1,),
        in_specs=[
            pl.BlockSpec(memory_space=pltpu.SMEM), pl.BlockSpec(memory_space=pltpu.VMEM),
        ] + [raw] * len(operands),
        out_specs=[raw] * len(outs),
        out_shape=outs,
        scratch_shapes=[pltpu.VMEM(a.shape, a.dtype) for a in operands]
        + [
            pltpu.VMEM((padded, width), bf16),
            pltpu.VMEM((hist, width, seq), f32),
            pltpu.VMEM((hist, seq, width), bf16),
        ]
        + [pltpu.VMEM(a.shape, a.dtype) for a in outs]
        + [
            pltpu.SemaphoreType.DMA((7 * hist + 8,)),
            pltpu.SemaphoreType.DMA((2 * hist + 13,)),
        ],
        compiler_params=params(56),
        cost_estimate=cost(30e9, 30e6),
        name="owner_backward",
    )(me, recv, *operands)


def input_kernel(denc_ref, win_ref, dpre_ref, dk_ref, out_ref):
    width = denc_ref.shape[2]
    total = denc_ref[0].astype(f32) + dot_nt(dpre_ref[...], win_ref[:, : 3 * width])
    total = total + dot_nt(jnp.transpose(dk_ref[...]), win_ref[:, 3 * width :])
    out_ref[0] = total.astype(bf16)


def input_backward(denc, w_in, dpre, dk):
    hist, seq, width = denc.shape
    block = lambda a: pl.BlockSpec((1,) + a.shape[1:], lambda i: (i, 0, 0))
    return pl.pallas_call(
        input_kernel,
        grid=(hist,),
        in_specs=[
            block(denc),
            whole(w_in.shape),
            pl.BlockSpec((seq, 3 * width), lambda i: (i, 0)),
            pl.BlockSpec((width, seq), lambda i: (0, i)),
        ],
        out_specs=block(denc),
        out_shape=jax.ShapeDtypeStruct(denc.shape, bf16),
        compiler_params=params(60),
        cost_estimate=cost(6e9, 8e6),
        name="input_backward",
    )(denc, w_in, dpre, dk)


def owner_order(width):
    n_y, n_core, n_z, n_x = (lax.axis_size(a) for a in AXES)
    rows = width // (n_y * n_core * n_z * n_x)
    place = jnp.arange(width, dtype=jnp.int32)
    inner = place % rows
    place = place // rows
    z, place = place % n_z, place // n_z
    x, place = place % n_x, place // n_x
    y, d_core = place % n_y, place // n_y
    core = (lax.axis_index(AXES[1]) + d_core) % n_core
    y, x = (lax.axis_index(AXES[0]) + y) % n_y, (lax.axis_index(AXES[3]) + x) % n_x
    z = (lax.axis_index(AXES[2]) + z) % n_z
    source = (((y * n_core + core) * n_z + z) * n_x + x) * rows + inner
    return (source[:, None] == jnp.arange(width, dtype=jnp.int32)[None, :]).astype(bf16)


def add_up(blocks):
    total = blocks[0].astype(f32)
    for block in blocks[1:]:
        total = total + block.astype(f32)
    return total


def core_stage(keep, send):
    return add_up(send_blocks([keep] + cut_rows(send, lax.axis_size(AXES[1]) - 1), AXES[1:2])).astype(bf16)


def send_blocks(blocks, axes):
    count = len(blocks)
    sizes = [lax.axis_size(a) for a in axes]
    parts = [blocks[0]]
    for d in range(1, count):
        pairs = []
        for c in range(count):
            there, stride, rest_c, rest_d = 0, 1, c, d
            for n in reversed(sizes):
                there += (rest_c + rest_d) % n * stride
                stride, rest_c, rest_d = stride * n, rest_c // n, rest_d // n
            pairs.append((c, there))
        parts.append(lax.ppermute(blocks[d], axes, pairs))
    return parts


def cut_rows(rows, count):
    step = rows.shape[0] // count
    return [rows[i * step : (i + 1) * step] for i in range(count)]


def local(histories, weight_in, weight_out, candidates, cotangent, owner_ids, hist_slot, lengths):
    devices = lax.axis_size(AXES)
    imp_rows, width = candidates.shape
    capacity = max(2, 2 * imp_rows // devices)
    slots = devices * capacity
    kept = width // lax.axis_size(AXES[1])
    after = lax.optimization_barrier

    sizes = n_y, n_core, n_z, n_x = tuple(lax.axis_size(a) for a in AXES)
    me = jnp.stack([lax.axis_index(a) for a in AXES]).astype(jnp.int32)
    core, line, plane = AXES[1:2], AXES[2:3], (AXES[0], AXES[3])
    send, pick = route(me, owner_ids, hist_slot, lengths, candidates, cotangent, sizes, capacity)
    shaped = send.reshape(devices, capacity, send.shape[1])
    recv = lax.all_to_all(shaped, AXES, split_axis=0, concat_axis=0, tiled=True)
    recv = recv.reshape(slots, send.shape[1])
    perm = owner_order(width)
    enc, slope, slope_t, v, q, k, q_t, attn_t, grad, normed, nu, gi, xt, mt = layer_forward(
        histories, weight_in, weight_out, perm
    )
    state = (normed, nu, gi, v, k, q_t, attn_t, grad, slope, slope_t)
    near, far, d_enc, dpre, dk, keep, send = owner_backward(
        me, sizes, recv, enc, weight_out, state, mt, xt, kept
    )
    rows = core_stage(keep, send)
    d_enc, rows, near, far = after((d_enc, rows, near, far))
    back = [cut_rows(b, n_z) for b in send_blocks([near] + cut_rows(far, n_core - 1), core)]
    back = [jnp.concatenate([b[d] for b in back], axis=0) for d in range(n_z)]
    d_inputs = input_backward(d_enc, weight_in, dpre, dk)
    back = send_blocks(back, line)
    parts = send_blocks(cut_rows(rows, n_y * n_x), plane)
    back, parts, d_inputs = after((back, parts, d_inputs))
    parts = send_blocks(cut_rows(add_up(parts).astype(bf16), n_z), line)
    back = [b.reshape(n_core, n_y * n_x, capacity, width) for b in back]
    back = [
        jnp.concatenate([b[:, i].reshape(n_core * capacity, width) for b in back], axis=0)
        for i in range(n_y * n_x)
    ]
    returned = jnp.concatenate(send_blocks(back, plane), axis=0)
    candidate_grad = lax.dot_general(
        pick, returned, (((0,), (0,)), ((), ())), preferred_element_type=f32
    ).astype(bf16)
    w_in_grad = add_up([p[:, width:] for p in parts])
    w_out_grad = add_up([p[:, :width] for p in parts])
    return d_inputs, candidate_grad, w_in_grad, w_out_grad


def solution(mesh):
    n_hash, n_dp = mesh.devices.shape
    fine = jax.sharding.Mesh(mesh.devices.reshape(n_hash // 2, 2, n_dp // 2, 2), AXES)
    return jax.shard_map(
        local,
        mesh=fine,
        in_specs=(
            P(AXES, None, None),
            P(),
            P(),
            P(AXES, None),
            P(AXES, None),
            P(AXES, None),
            P(AXES),
            P(AXES),
        ),
        out_specs=(
            P(AXES, None, None),
            P(AXES, None),
            P(AXES, None),
            P(AXES, None),
        ),
        check_vma=False,
    )
```

```python
import functools

import jax
import jax.numpy as jnp
from jax import lax
from jax.experimental import pallas as pl
from jax.experimental.pallas import tpu as pltpu
from jax.sharding import PartitionSpec as P

HEADS = 8
TILE = 128
META = 128
AXES = ("hash_hi", "core", "dp_hi", "dp_lo")
norm_eps = 1e-05
f32 = jnp.float32
bf16 = jnp.bfloat16
MIB = 1024 * 1024


def dot_nn(a, b):
    return lax.dot_general(a, b, (((1,), (0,)), ((), ())), preferred_element_type=f32)


def dot_nt(a, b):
    return lax.dot_general(a, b, (((1,), (1,)), ((), ())), preferred_element_type=f32)


def dot_tn(a, b):
    return lax.dot_general(a, b, (((0,), (0,)), ((), ())), preferred_element_type=f32)


def iota(shape, axis):
    return lax.broadcasted_iota(jnp.int32, shape, axis)


def silu_pair(half):
    t = jnp.tanh(half)
    u = 1.0 + t
    act = half * u
    return act, u + act * (1.0 - t)


def lane_masks(width, part):
    lane = iota((1, width), 1)
    return [((lane >= j * part) & (lane < (j + 1) * part)).astype(bf16) for j in range(width // part)]


def both_heads(pair, masks):
    return jnp.concatenate([pair * m for m in masks], axis=0)


def pick_lanes(stacked, head):
    rows = stacked.shape[0] // 2
    lane = iota((1, 2 * head), 1)
    return jnp.where(lane < head, stacked[:rows], stacked[rows:])


def params(mib):
    return pltpu.CompilerParams(dimension_semantics=("arbitrary",), vmem_limit_bytes=mib * MIB)


def whole(shape):
    return pl.BlockSpec(shape, lambda i: (0,) * len(shape))


def cost(flops, nbytes, trans=0):
    return pl.CostEstimate(flops=int(flops), bytes_accessed=int(nbytes), transcendentals=int(trans))


def route_kernel(devices, capacity, own_ref, slot_ref, len_ref, cand_ref, cot_ref, send_ref, pick_ref):
    rows, width = cand_ref.shape
    slots = devices * capacity
    own = own_ref[...]
    hot = (own == iota((devices, rows), 0)).astype(f32)
    before = (iota((rows, rows), 0) < iota((rows, rows), 1)).astype(f32).astype(bf16)
    earlier = dot_nn(hot.astype(bf16), before)
    position = jnp.sum(earlier * hot, axis=0, keepdims=True).astype(jnp.int32)
    target = own * capacity + position
    pick = (target == iota((slots, rows), 0)).astype(f32).astype(bf16)
    pick_ref[...] = pick
    send_ref[:, :width] = dot_nn(pick, cand_ref[...]).astype(bf16)
    send_ref[:, width : 2 * width] = dot_nn(pick, cot_ref[...]).astype(bf16)
    line = iota((META, rows), 0)
    meta = jnp.where(line == 0, slot_ref[...], jnp.where(line == 1, len_ref[...], 0))
    send_ref[:, 2 * width :] = dot_nt(pick, meta.astype(f32).astype(bf16)).astype(bf16)


def route(own, slot, length, cand, cot, devices, capacity):
    rows, width = cand.shape
    slots = devices * capacity
    line = whole((1, rows))
    return pl.pallas_call(
        functools.partial(route_kernel, devices, capacity),
        grid=(1,),
        in_specs=[line, line, line, whole(cand.shape), whole(cot.shape)],
        out_specs=[whole((slots, 2 * width + META)), whole((slots, rows))],
        out_shape=(
            jax.ShapeDtypeStruct((slots, 2 * width + META), bf16),
            jax.ShapeDtypeStruct((slots, rows), bf16),
        ),
        compiler_params=params(60),
        cost_estimate=cost(2e9, 4 * rows * width * 4),
        name="route",
    )(own.reshape(1, rows), slot.reshape(1, rows), length.reshape(1, rows), cand, cot)


def forward_kernel(
    x_ref, win_ref, wout_ref, perm_ref,
    enc_ref, slope_ref, slope_t_ref, v_ref, q_ref, k_ref, q_t_ref, attn_t_ref, grad_ref,
    normed_ref, nu_ref, gi_ref, xt_ref, mt_ref,
    gate_ref, mixed_ref, slope_u_ref,
):
    seq, width = x_ref.shape[1:]
    head = width // HEADS
    half_seq = seq // 2
    x = x_ref[0]
    for branch in range(4):
        cols = slice(branch * width, (branch + 1) * width)
        act, slope = silu_pair(0.5 * dot_nn(x, win_ref[:, cols]))
        if branch == 3:
            slope_t_ref[0] = jnp.transpose(0.5 * slope).astype(bf16)
        elif branch > 0:
            slope_ref[0, :, (branch - 1) * width : branch * width] = (0.5 * slope).astype(bf16)
        if branch == 0:
            gate_ref[...] = act
            slope_u_ref[...] = 0.5 * slope
        else:
            (v_ref, q_ref, k_ref)[branch - 1][0] = act.astype(bf16)
        if branch == 2:
            q_t_ref[0] = jnp.transpose(act).astype(bf16)
    masks = lane_masks(2 * head, head)
    scale = 0.5 * head**-0.5
    tri = iota((half_seq, half_seq), 0) >= iota((half_seq, half_seq), 1)
    zero = jnp.zeros((half_seq, half_seq), f32)
    for pair in range(HEADS // 2):
        cols = slice(pair * 2 * head, (pair + 1) * 2 * head)
        q_p = q_ref[0, :, cols] * jnp.asarray(scale, bf16)
        half = dot_nt(both_heads(q_p, masks), k_ref[0, :, cols])
        stack = []
        for j in range(2):
            h = 2 * pair + j
            top = silu_pair(half[j * seq : j * seq + half_seq, :half_seq])
            bot = silu_pair(half[j * seq + half_seq : (j + 1) * seq])
            full = []
            for a, b in zip(top, bot):
                a = jnp.concatenate([jnp.where(tri, a, 0.0), zero], axis=1)
                b = jnp.concatenate([b[:, :half_seq], jnp.where(tri, b[:, half_seq:], 0.0)], axis=1)
                full.append(jnp.concatenate([a, b], axis=0))
            stack.append(full[0].astype(bf16))
            attn_t_ref[0, h] = jnp.transpose(full[0]).astype(bf16)
            grad_ref[0, h] = full[1].astype(bf16)
        mixed = dot_nn(jnp.concatenate(stack, axis=0), v_ref[0, :, cols])
        mixed_ref[:, cols] = pick_lanes(mixed, head) * (1.0 / seq)
    mixed = mixed_ref[...]
    centred = mixed - jnp.mean(mixed, axis=1, keepdims=True)
    inv_std = lax.rsqrt(jnp.mean(centred * centred, axis=1, keepdims=True) + norm_eps)
    normed = centred * inv_std
    gate = gate_ref[...]
    merged = (normed * gate).astype(bf16)
    normed_ref[0] = normed.astype(bf16)
    nu_ref[0] = (normed * slope_u_ref[...]).astype(bf16)
    gi_ref[0] = (gate * inv_std).astype(bf16)
    enc_ref[0] = (x.astype(f32) + dot_nn(merged, wout_ref[...])).astype(bf16)
    perm = perm_ref[...]
    xt_ref[...] = dot_nt(perm, x).astype(bf16)
    mt_ref[...] = dot_nt(perm, merged).astype(bf16)


def layer_forward(x, w_in, w_out, perm):
    hist, seq, width = x.shape
    row = pl.BlockSpec((1, seq, width), lambda i: (i, 0, 0))
    wide = pl.BlockSpec((1, seq, 2 * width), lambda i: (i, 0, 0))
    column = pl.BlockSpec((1, width, seq), lambda i: (i, 0, 0))
    square = pl.BlockSpec((1, HEADS, seq, seq), lambda i: (i, 0, 0, 0))
    turned = pl.BlockSpec((width, seq), lambda i: (0, i))
    row_s = jax.ShapeDtypeStruct((hist, seq, width), bf16)
    column_s = jax.ShapeDtypeStruct((hist, width, seq), bf16)
    square_s = jax.ShapeDtypeStruct((hist, HEADS, seq, seq), bf16)
    turned_s = jax.ShapeDtypeStruct((width, hist * seq), bf16)
    return pl.pallas_call(
        forward_kernel,
        grid=(hist,),
        in_specs=[row, whole(w_in.shape), whole(w_out.shape), whole(perm.shape)],
        out_specs=[
            row, wide, column, row, row, row, column, square, square, row, row, row, turned, turned,
        ],
        out_shape=[
            row_s, jax.ShapeDtypeStruct((hist, seq, 2 * width), bf16), column_s, row_s, row_s, row_s,
            column_s, square_s, square_s, row_s, row_s, row_s, turned_s, turned_s,
        ],
        scratch_shapes=[pltpu.VMEM((seq, width), f32)] * 3,
        compiler_params=params(60),
        cost_estimate=cost(18e9, 24e6),
        name="forward",
    )(x, w_in, w_out, perm)


def group_slots(recv_ref, hist):
    slots, width = recv_ref.shape
    meta = recv_ref[:, width - META :].astype(f32)
    slot_h = meta[:, 0:1]
    valid = meta[:, 1:2] > 0.0
    lane = iota((slots, META), 1).astype(f32)
    hot = jnp.where(valid & (slot_h == lane), 1.0, 0.0)
    lower = (iota((slots, slots), 0) > iota((slots, slots), 1)).astype(f32).astype(bf16)
    rank = jnp.sum(dot_nn(lower, hot.astype(bf16)) * hot, axis=1, keepdims=True)
    starts, start = [], jnp.int32(0)
    begin = jnp.zeros((slots, 1), f32)
    for h in range(hist):
        starts.append(start)
        begin = jnp.where(slot_h == float(h), (start * TILE).astype(f32), begin)
        count = jnp.sum(hot[:, h : h + 1]).astype(jnp.int32)
        start = start + (count + (TILE - 1)) // TILE
    dest = jnp.where(valid, begin + rank, -1.0)
    eye = iota((slots, slots), 0) == iota((slots, slots), 1)
    dest_row = jnp.sum(jnp.where(eye, dest, 0.0), axis=0, keepdims=True).astype(jnp.int32)
    return dest.astype(jnp.int32), dest_row, starts, start


def target_tile(tile, starts, dest_row, recv_ref, enc_ref, grouped_ref, turned_ref):
    seq, width = enc_ref.shape[1:]
    head = width // HEADS
    masks = lane_masks(2 * head, head)
    scale = 0.5 * head**-0.5
    base = pl.multiple_of(tile * TILE, TILE)
    hist = jnp.int32(0)
    for start in starts[1:]:
        hist = hist + (tile >= start).astype(jnp.int32)
    choose = (iota((TILE, dest_row.shape[1]), 0) + base == dest_row).astype(f32).astype(bf16)
    rows = dot_nn(choose, recv_ref[...])
    q_all = rows[:, :width] * scale
    g_all = rows[:, width : 2 * width]
    q_t = jnp.transpose(q_all).astype(bf16)
    g_t = jnp.transpose(g_all).astype(bf16)
    q_all = q_all.astype(bf16)
    g_all = g_all.astype(bf16)
    length = rows[:, 2 * width + 1 : 2 * width + 2]
    positions = iota((TILE, seq), 1).astype(f32)
    weight = jnp.where(positions < length, 1.0 / jnp.maximum(length, 1.0), 0.0)
    for pair in range(HEADS // 2):
        cols = slice(pair * 2 * head, (pair + 1) * 2 * head)
        k_p = enc_ref[hist, :, cols]
        both = dot_nt(
            jnp.concatenate(
                [both_heads(q_all[:, cols], masks), both_heads(g_all[:, cols], masks)], axis=0
            ),
            k_p,
        )
        slopes = []
        for j in range(2):
            h = 2 * pair + j
            mine = slice(h * head, (h + 1) * head)
            act, slope = silu_pair(both[j * TILE : (j + 1) * TILE])
            d_attn = both[(2 + j) * TILE : (3 + j) * TILE]
            attn = (act * weight).astype(bf16)
            d_s = (d_attn * weight * slope).astype(bf16)
            turned_ref[hist, mine, :] += dot_nn(
                jnp.concatenate([g_t[mine], q_t[mine]], axis=1),
                jnp.concatenate([attn, d_s], axis=0),
            )
            slopes.append(d_s)
        d_q = pick_lanes(dot_nn(jnp.concatenate(slopes, axis=0), k_p), head)
        grouped_ref[pl.ds(base, TILE), cols] = (d_q * scale).astype(bf16)


def norm_backward(denc_ref, wout_ref, normed_ref, nu_ref, gi_ref, dmix_ref, dpre_ref):
    hist, seq, width = denc_ref.shape
    for at in range(hist):
        here = slice(at * seq, (at + 1) * seq)
        d_merged = dot_nt(denc_ref[at], wout_ref[...])
        dpre_ref[here, :width] = (d_merged * nu_ref[at].astype(f32)).astype(bf16)
        normed = normed_ref[at].astype(f32)
        d_norm = d_merged * gi_ref[at].astype(f32)
        d_mix = (
            d_norm
            - jnp.mean(d_norm, axis=1, keepdims=True)
            - normed * jnp.mean(d_norm * normed, axis=1, keepdims=True)
        )
        dmix_ref[at] = d_mix.astype(bf16)


def attention_backward(
    at, dmix_ref, v_ref, k_ref, q_t_ref, attn_t_ref, grad_ref, slope_ref, slope_t_ref, dpre_ref, dk_ref
):
    seq, width = dmix_ref.shape[1:]
    head = width // HEADS
    here = slice(at * seq, (at + 1) * seq)
    masks = lane_masks(2 * head, head)
    scale = 0.5 * head**-0.5 / seq
    for pair in range(HEADS // 2):
        cols = slice(pair * 2 * head, (pair + 1) * 2 * head)
        d_p = dmix_ref[at, :, cols]
        d_attn = dot_nt(both_heads(d_p, masks), v_ref[at, :, cols])
        d_s = [
            (d_attn[j * seq : (j + 1) * seq] * grad_ref[at, 2 * pair + j].astype(f32)).astype(bf16)
            for j in range(2)
        ]
        attn_t = jnp.concatenate([attn_t_ref[at, 2 * pair], attn_t_ref[at, 2 * pair + 1]], axis=0)
        d_v = pick_lanes(dot_nn(attn_t, d_p), head) * (1.0 / seq)
        d_q = pick_lanes(dot_nn(jnp.concatenate(d_s, axis=0), k_ref[at, :, cols]), head) * scale
        for branch, grad in ((0, d_v), (1, d_q)):
            old = slice(branch * width + pair * 2 * head, branch * width + (pair + 1) * 2 * head)
            new = slice(old.start + width, old.stop + width)
            dpre_ref[here, new] = (grad * slope_ref[at, :, old].astype(f32)).astype(bf16)
        for j in range(2):
            mine = slice((2 * pair + j) * head, (2 * pair + j + 1) * head)
            d_k = dot_nn(q_t_ref[at, mine], d_s[j]) * scale
            dk_ref[mine, here] = (d_k * slope_t_ref[at, mine].astype(f32)).astype(bf16)


def owner_kernel(recv_ref, *refs):
    n_in, n_out = 15, 7
    sources, outs, refs = refs[:n_in], refs[n_in : n_in + n_out], refs[n_in + n_out :]
    held, refs = refs[:n_in], refs[n_in:]
    (
        enc_ref, order_ref, wout_ref, normed_ref, nu_ref, gi_ref, v_ref, k_ref, q_t_ref,
        attn_t_ref, grad_ref, slope_ref, slope_t_ref, mt_ref, xt_ref,
    ) = held
    grouped_ref, turned_ref, dmix_ref, dq_ref, dq_far_ref, denc_ref, dpre_ref, dk_ref, keep_ref, send_ref, sem_in, sem_out = refs
    dq_hbm, dq_far_hbm, denc_hbm, dpre_hbm, dk_hbm, keep_hbm, send_hbm = outs
    hist, seq, width = enc_ref.shape
    slots, padded = recv_ref.shape[0], grouped_ref.shape[0]
    kept = keep_ref.shape[0]

    def load(i, n, at=None):
        source, dest = (sources[i], held[i]) if at is None else (sources[i].at[at], held[i].at[at])
        return pltpu.make_async_copy(source, dest, sem_in.at[n])

    first = [load(i, i) for i in range(6)]
    by_history = [[load(i, i + 7 * at, at) for i in range(6, 13)] for at in range(hist)]
    last = [load(i, 7 * hist + i - 7) for i in (13, 14)]
    for copy in first + sum(by_history, []) + last:
        copy.start()
    grouped_ref[...] = jnp.zeros_like(grouped_ref)
    turned_ref[...] = jnp.zeros_like(turned_ref)
    dest, dest_row, starts, tiles = group_slots(recv_ref, hist)
    first[0].wait()

    def one_tile(tile, carry):
        target_tile(tile, starts, dest_row, recv_ref, enc_ref, grouped_ref, turned_ref)
        return carry

    lax.fori_loop(0, tiles, one_tile, 0)
    for h in range(hist):
        denc_ref[h] = jnp.transpose(turned_ref[h]).astype(bf16)
    back = (dest == iota((slots, padded), 1)).astype(f32).astype(bf16)
    d_query = dot_nn(back, grouped_ref[...]).astype(bf16)
    near = dq_ref.shape[0]
    first[1].wait()
    dq_ref[...] = dot_nn(order_ref[:near], d_query).astype(bf16)
    dq_far_ref[...] = dot_nn(order_ref[near:], d_query).astype(bf16)
    stores = []

    def store(source, dest):
        copy = pltpu.make_async_copy(source, dest, sem_out.at[len(stores)])
        copy.start()
        stores.append(copy)

    store(denc_ref, denc_hbm)
    store(dq_ref, dq_hbm)
    store(dq_far_ref, dq_far_hbm)
    for copy in first[2:]:
        copy.wait()
    norm_backward(denc_ref, wout_ref, normed_ref, nu_ref, gi_ref, dmix_ref, dpre_ref)
    for at in range(hist):
        for copy in by_history[at]:
            copy.wait()
        attention_backward(
            at, dmix_ref, v_ref, k_ref, q_t_ref, attn_t_ref, grad_ref, slope_ref, slope_t_ref,
            dpre_ref, dk_ref,
        )
        here = pl.ds(at * seq, seq)
        store(dpre_ref.at[here, :], dpre_hbm.at[here, :])
        store(dk_ref.at[:, here], dk_hbm.at[:, here])
    for copy in last:
        copy.wait()
    for block in range(5):
        cols = slice(block * width, (block + 1) * width)
        if block == 0:
            part = dot_nn(mt_ref[...], denc_ref[...].reshape(hist * seq, width))
        elif block == 4:
            part = dot_nt(xt_ref[...], dk_ref[...])
        else:
            part = dot_nn(xt_ref[...], dpre_ref[:, (block - 1) * width : block * width])
        keep_ref[:, cols] = part[:kept].astype(bf16)
        send_ref[:, cols] = part[kept:].astype(bf16)
        store(keep_ref.at[:, cols], keep_hbm.at[:, cols])
        store(send_ref.at[:, cols], send_hbm.at[:, cols])
    for copy in stores:
        copy.wait()


def owner_backward(order, recv, enc, w_out, state, mt, xt, kept):
    hist, seq, width = enc.shape
    slots = recv.shape[0]
    rows = hist * seq
    padded = ((slots - hist) // TILE + hist) * TILE
    operands = (enc, order, w_out) + state + (mt, xt)
    raw = pl.BlockSpec(memory_space=pl.ANY)
    outs = [
        jax.ShapeDtypeStruct((slots // 2, width), bf16),
        jax.ShapeDtypeStruct((slots - slots // 2, width), bf16),
        jax.ShapeDtypeStruct(enc.shape, bf16),
        jax.ShapeDtypeStruct((rows, 3 * width), bf16),
        jax.ShapeDtypeStruct((width, rows), bf16),
        jax.ShapeDtypeStruct((kept, 5 * width), bf16),
        jax.ShapeDtypeStruct((width - kept, 5 * width), bf16),
    ]
    return pl.pallas_call(
        owner_kernel,
        grid=(1,),
        in_specs=[pl.BlockSpec(memory_space=pltpu.VMEM)] + [raw] * len(operands),
        out_specs=[raw] * len(outs),
        out_shape=outs,
        scratch_shapes=[pltpu.VMEM(a.shape, a.dtype) for a in operands]
        + [
            pltpu.VMEM((padded, width), bf16),
            pltpu.VMEM((hist, width, seq), f32),
            pltpu.VMEM((hist, seq, width), bf16),
        ]
        + [pltpu.VMEM(a.shape, a.dtype) for a in outs]
        + [
            pltpu.SemaphoreType.DMA((7 * hist + 8,)),
            pltpu.SemaphoreType.DMA((2 * hist + 13,)),
        ],
        compiler_params=params(44),
        cost_estimate=cost(30e9, 30e6),
        name="owner_backward",
    )(recv, *operands)


def input_kernel(denc_ref, win_ref, dpre_ref, dk_ref, out_ref):
    width = denc_ref.shape[2]
    total = denc_ref[0].astype(f32) + dot_nt(dpre_ref[...], win_ref[:, : 3 * width])
    total = total + dot_nt(jnp.transpose(dk_ref[...]), win_ref[:, 3 * width :])
    out_ref[0] = total.astype(bf16)


def input_backward(denc, w_in, dpre, dk):
    hist, seq, width = denc.shape
    block = lambda a: pl.BlockSpec((1,) + a.shape[1:], lambda i: (i, 0, 0))
    return pl.pallas_call(
        input_kernel,
        grid=(hist,),
        in_specs=[
            block(denc),
            whole(w_in.shape),
            pl.BlockSpec((seq, 3 * width), lambda i: (i, 0)),
            pl.BlockSpec((width, seq), lambda i: (0, i)),
        ],
        out_specs=block(denc),
        out_shape=jax.ShapeDtypeStruct(denc.shape, bf16),
        compiler_params=params(60),
        cost_estimate=cost(6e9, 8e6),
        name="input_backward",
    )(denc, w_in, dpre, dk)


def owner_order(width):
    n_y, n_core, n_z, n_x = (lax.axis_size(a) for a in AXES)
    rows = width // (n_y * n_core * n_z * n_x)
    place = jnp.arange(width, dtype=jnp.int32)
    inner = place % rows
    place = place // rows
    z, place = place % n_z, place // n_z
    x, place = place % n_x, place // n_x
    y, d_core = place % n_y, place // n_y
    core = (lax.axis_index(AXES[1]) + d_core) % n_core
    y, x = (lax.axis_index(AXES[0]) + y) % n_y, (lax.axis_index(AXES[3]) + x) % n_x
    z = (lax.axis_index(AXES[2]) + z) % n_z
    source = (((y * n_core + core) * n_z + z) * n_x + x) * rows + inner
    return (source[:, None] == jnp.arange(width, dtype=jnp.int32)[None, :]).astype(bf16)


def return_orders(capacity):
    sizes = n_y, n_core, n_z, n_x = tuple(lax.axis_size(a) for a in AXES)
    slots = n_y * n_core * n_z * n_x * capacity
    place = jnp.arange(slots, dtype=jnp.int32)
    inner, block = place % capacity, place // capacity
    plane = n_y * n_x
    orders = []
    for sign, (d_core, d_z, d_plane) in (
        (1, (block // (plane * n_z), block // plane % n_z, block % plane)),
        (-1, (block % n_core, block // n_core % n_z, block // (n_core * n_z))),
    ):
        y, core, z, x = (
            (lax.axis_index(a) + sign * d + n) % n
            for a, d, n in zip(AXES, (d_plane // n_x, d_core, d_z, d_plane % n_x), sizes)
        )
        source = (((y * n_core + core) * n_z + z) * n_x + x) * capacity + inner
        orders.append((source[:, None] == place[None, :]).astype(bf16))
    return orders


def add_up(blocks):
    total = blocks[0].astype(f32)
    for block in blocks[1:]:
        total = total + block.astype(f32)
    return total


def core_stage(keep, send):
    return add_up(send_blocks([keep] + cut_rows(send, lax.axis_size(AXES[1]) - 1), AXES[1:2])).astype(bf16)


def send_blocks(blocks, axes):
    count = len(blocks)
    sizes = [lax.axis_size(a) for a in axes]
    parts = [blocks[0]]
    for d in range(1, count):
        pairs = []
        for c in range(count):
            there, stride, rest_c, rest_d = 0, 1, c, d
            for n in reversed(sizes):
                there += (rest_c + rest_d) % n * stride
                stride, rest_c, rest_d = stride * n, rest_c // n, rest_d // n
            pairs.append((c, there))
        parts.append(lax.ppermute(blocks[d], axes, pairs))
    return parts


def cut_rows(rows, count):
    step = rows.shape[0] // count
    return [rows[i * step : (i + 1) * step] for i in range(count)]


def local(histories, weight_in, weight_out, candidates, cotangent, owner_ids, hist_slot, lengths):
    devices = lax.axis_size(AXES)
    imp_rows, width = candidates.shape
    capacity = max(2, 2 * imp_rows // devices)
    slots = devices * capacity
    kept = width // lax.axis_size(AXES[1])
    after = lax.optimization_barrier

    sizes = n_y, n_core, n_z, n_x = tuple(lax.axis_size(a) for a in AXES)
    core, line, plane = AXES[1:2], AXES[2:3], (AXES[0], AXES[3])
    send, pick = route(owner_ids, hist_slot, lengths, candidates, cotangent, devices, capacity)
    shaped = send.reshape(devices, capacity, send.shape[1])
    recv = lax.all_to_all(shaped, AXES, split_axis=0, concat_axis=0, tiled=True)
    recv = recv.reshape(slots, send.shape[1])
    perm = owner_order(width)
    leaving, arriving = return_orders(capacity)
    pick = dot_nn(arriving, pick).astype(bf16)
    enc, slope, slope_t, v, q, k, q_t, attn_t, grad, normed, nu, gi, xt, mt = layer_forward(
        histories, weight_in, weight_out, perm
    )
    state = (normed, nu, gi, v, k, q_t, attn_t, grad, slope, slope_t)
    near, far, d_enc, dpre, dk, keep, send = owner_backward(
        leaving, recv, enc, weight_out, state, mt, xt, kept
    )
    rows = core_stage(keep, send)
    d_enc, rows, near, far = after((d_enc, rows, near, far))
    back = [cut_rows(b, n_z) for b in send_blocks([near] + cut_rows(far, n_core - 1), core)]
    back = [jnp.concatenate([b[d] for b in back], axis=0) for d in range(n_z)]
    d_inputs = input_backward(d_enc, weight_in, dpre, dk)
    back = send_blocks(back, line)
    parts = send_blocks(cut_rows(rows, n_y * n_x), plane)
    back, parts, d_inputs = after((back, parts, d_inputs))
    parts = send_blocks(cut_rows(add_up(parts).astype(bf16), n_z), line)
    back = [b.reshape(n_core, n_y * n_x, capacity, width) for b in back]
    back = [
        jnp.concatenate([b[:, i].reshape(n_core * capacity, width) for b in back], axis=0)
        for i in range(n_y * n_x)
    ]
    returned = jnp.concatenate(send_blocks(back, plane), axis=0)
    candidate_grad = lax.dot_general(
        pick, returned, (((0,), (0,)), ((), ())), preferred_element_type=f32
    ).astype(bf16)
    w_in_grad = add_up([p[:, width:] for p in parts])
    w_out_grad = add_up([p[:, :width] for p in parts])
    return d_inputs, candidate_grad, w_in_grad, w_out_grad


def solution(mesh):
    n_hash, n_dp = mesh.devices.shape
    fine = jax.sharding.Mesh(mesh.devices.reshape(n_hash // 2, 2, n_dp // 2, 2), AXES)
    return jax.shard_map(
        local,
        mesh=fine,
        in_specs=(
            P(AXES, None, None),
            P(),
            P(),
            P(AXES, None),
            P(AXES, None),
            P(AXES, None),
            P(AXES),
            P(AXES),
        ),
        out_specs=(
            P(AXES, None, None),
            P(AXES, None),
            P(AXES, None),
            P(AXES, None),
        ),
        check_vma=False,
    )
```

```python
import functools

import jax
import jax.numpy as jnp
from jax import lax
from jax.experimental import pallas as pl
from jax.experimental.pallas import tpu as pltpu
from jax.sharding import PartitionSpec as P

HEADS = 8
TILE = 128
META = 128
AXES = ("hash_hi", "core", "dp_hi", "dp_lo")
norm_eps = 1e-05
f32 = jnp.float32
bf16 = jnp.bfloat16
MIB = 1024 * 1024


def dot_nn(a, b):
    return lax.dot_general(a, b, (((1,), (0,)), ((), ())), preferred_element_type=f32)


def dot_nt(a, b):
    return lax.dot_general(a, b, (((1,), (1,)), ((), ())), preferred_element_type=f32)


def dot_tn(a, b):
    return lax.dot_general(a, b, (((0,), (0,)), ((), ())), preferred_element_type=f32)


def iota(shape, axis):
    return lax.broadcasted_iota(jnp.int32, shape, axis)


def silu_pair(half):
    t = jnp.tanh(half)
    u = 1.0 + t
    act = half * u
    return act, u + act * (1.0 - t)


def lane_masks(width, part):
    lane = iota((1, width), 1)
    return [((lane >= j * part) & (lane < (j + 1) * part)).astype(bf16) for j in range(width // part)]


def both_heads(pair, masks):
    return jnp.concatenate([pair * m for m in masks], axis=0)


def pick_lanes(stacked, head):
    rows = stacked.shape[0] // 2
    lane = iota((1, 2 * head), 1)
    return jnp.where(lane < head, stacked[:rows], stacked[rows:])


def params(mib):
    return pltpu.CompilerParams(dimension_semantics=("arbitrary",), vmem_limit_bytes=mib * MIB)


def whole(shape):
    return pl.BlockSpec(shape, lambda i: (0,) * len(shape))


def cost(flops, nbytes, trans=0):
    return pl.CostEstimate(flops=int(flops), bytes_accessed=int(nbytes), transcendentals=int(trans))


def route_kernel(devices, capacity, own_ref, slot_ref, len_ref, cand_ref, cot_ref, send_ref, pick_ref):
    rows, width = cand_ref.shape
    slots = devices * capacity
    own = own_ref[...]
    hot = (own == iota((devices, rows), 0)).astype(f32)
    before = (iota((rows, rows), 0) < iota((rows, rows), 1)).astype(f32).astype(bf16)
    earlier = dot_nn(hot.astype(bf16), before)
    position = jnp.sum(earlier * hot, axis=0, keepdims=True).astype(jnp.int32)
    target = own * capacity + position
    pick = (target == iota((slots, rows), 0)).astype(f32).astype(bf16)
    pick_ref[...] = pick
    send_ref[:, :width] = dot_nn(pick, cand_ref[...]).astype(bf16)
    send_ref[:, width : 2 * width] = dot_nn(pick, cot_ref[...]).astype(bf16)
    line = iota((META, rows), 0)
    meta = jnp.where(line == 0, slot_ref[...], jnp.where(line == 1, len_ref[...], 0))
    send_ref[:, 2 * width :] = dot_nt(pick, meta.astype(f32).astype(bf16)).astype(bf16)


def route(own, slot, length, cand, cot, devices, capacity):
    rows, width = cand.shape
    slots = devices * capacity
    line = whole((1, rows))
    return pl.pallas_call(
        functools.partial(route_kernel, devices, capacity),
        grid=(1,),
        in_specs=[line, line, line, whole(cand.shape), whole(cot.shape)],
        out_specs=[whole((slots, 2 * width + META)), whole((slots, rows))],
        out_shape=(
            jax.ShapeDtypeStruct((slots, 2 * width + META), bf16),
            jax.ShapeDtypeStruct((slots, rows), bf16),
        ),
        compiler_params=params(60),
        cost_estimate=cost(2e9, 4 * rows * width * 4),
        name="route",
    )(own.reshape(1, rows), slot.reshape(1, rows), length.reshape(1, rows), cand, cot)


def forward_kernel(
    x_ref, win_ref, wout_ref, perm_ref,
    enc_ref, slope_ref, slope_t_ref, v_ref, q_ref, k_ref, q_t_ref, attn_t_ref, grad_ref,
    normed_ref, nu_ref, gi_ref, xt_ref, mt_ref,
    gate_ref, mixed_ref, slope_u_ref,
):
    seq, width = x_ref.shape[1:]
    head = width // HEADS
    half_seq = seq // 2
    x = x_ref[0]
    for branch in range(4):
        cols = slice(branch * width, (branch + 1) * width)
        act, slope = silu_pair(0.5 * dot_nn(x, win_ref[:, cols]))
        if branch == 3:
            slope_t_ref[0] = jnp.transpose(0.5 * slope).astype(bf16)
        elif branch > 0:
            slope_ref[0, :, (branch - 1) * width : branch * width] = (0.5 * slope).astype(bf16)
        if branch == 0:
            gate_ref[...] = act
            slope_u_ref[...] = 0.5 * slope
        else:
            (v_ref, q_ref, k_ref)[branch - 1][0] = act.astype(bf16)
        if branch == 2:
            q_t_ref[0] = jnp.transpose(act).astype(bf16)
    masks = lane_masks(2 * head, head)
    scale = 0.5 * head**-0.5
    tri = iota((half_seq, half_seq), 0) >= iota((half_seq, half_seq), 1)
    zero = jnp.zeros((half_seq, half_seq), f32)
    for pair in range(HEADS // 2):
        cols = slice(pair * 2 * head, (pair + 1) * 2 * head)
        q_p = q_ref[0, :, cols] * jnp.asarray(scale, bf16)
        half = dot_nt(both_heads(q_p, masks), k_ref[0, :, cols])
        stack = []
        for j in range(2):
            h = 2 * pair + j
            top = silu_pair(half[j * seq : j * seq + half_seq, :half_seq])
            bot = silu_pair(half[j * seq + half_seq : (j + 1) * seq])
            full = []
            for a, b in zip(top, bot):
                a = jnp.concatenate([jnp.where(tri, a, 0.0), zero], axis=1)
                b = jnp.concatenate([b[:, :half_seq], jnp.where(tri, b[:, half_seq:], 0.0)], axis=1)
                full.append(jnp.concatenate([a, b], axis=0))
            stack.append(full[0].astype(bf16))
            attn_t_ref[0, h] = jnp.transpose(full[0]).astype(bf16)
            grad_ref[0, h] = full[1].astype(bf16)
        mixed = dot_nn(jnp.concatenate(stack, axis=0), v_ref[0, :, cols])
        mixed_ref[:, cols] = pick_lanes(mixed, head) * (1.0 / seq)
    mixed = mixed_ref[...]
    centred = mixed - jnp.mean(mixed, axis=1, keepdims=True)
    inv_std = lax.rsqrt(jnp.mean(centred * centred, axis=1, keepdims=True) + norm_eps)
    normed = centred * inv_std
    gate = gate_ref[...]
    merged = (normed * gate).astype(bf16)
    normed_ref[0] = normed.astype(bf16)
    nu_ref[0] = (normed * slope_u_ref[...]).astype(bf16)
    gi_ref[0] = (gate * inv_std).astype(bf16)
    enc_ref[0] = (x.astype(f32) + dot_nn(merged, wout_ref[...])).astype(bf16)
    perm = perm_ref[...]
    xt_ref[...] = dot_nt(perm, x).astype(bf16)
    mt_ref[...] = dot_nt(perm, merged).astype(bf16)


def layer_forward(x, w_in, w_out, perm):
    hist, seq, width = x.shape
    row = pl.BlockSpec((1, seq, width), lambda i: (i, 0, 0))
    wide = pl.BlockSpec((1, seq, 2 * width), lambda i: (i, 0, 0))
    column = pl.BlockSpec((1, width, seq), lambda i: (i, 0, 0))
    square = pl.BlockSpec((1, HEADS, seq, seq), lambda i: (i, 0, 0, 0))
    turned = pl.BlockSpec((width, seq), lambda i: (0, i))
    row_s = jax.ShapeDtypeStruct((hist, seq, width), bf16)
    column_s = jax.ShapeDtypeStruct((hist, width, seq), bf16)
    square_s = jax.ShapeDtypeStruct((hist, HEADS, seq, seq), bf16)
    turned_s = jax.ShapeDtypeStruct((width, hist * seq), bf16)
    return pl.pallas_call(
        forward_kernel,
        grid=(hist,),
        in_specs=[row, whole(w_in.shape), whole(w_out.shape), whole(perm.shape)],
        out_specs=[
            row, wide, column, row, row, row, column, square, square, row, row, row, turned, turned,
        ],
        out_shape=[
            row_s, jax.ShapeDtypeStruct((hist, seq, 2 * width), bf16), column_s, row_s, row_s, row_s,
            column_s, square_s, square_s, row_s, row_s, row_s, turned_s, turned_s,
        ],
        scratch_shapes=[pltpu.VMEM((seq, width), f32)] * 3,
        compiler_params=params(60),
        cost_estimate=cost(18e9, 24e6),
        name="forward",
    )(x, w_in, w_out, perm)


def group_slots(recv_ref, hist):
    slots, width = recv_ref.shape
    meta = recv_ref[:, width - META :].astype(f32)
    slot_h = meta[:, 0:1]
    valid = meta[:, 1:2] > 0.0
    lane = iota((slots, META), 1).astype(f32)
    hot = jnp.where(valid & (slot_h == lane), 1.0, 0.0)
    lower = (iota((slots, slots), 0) > iota((slots, slots), 1)).astype(f32).astype(bf16)
    rank = jnp.sum(dot_nn(lower, hot.astype(bf16)) * hot, axis=1, keepdims=True)
    starts, start = [], jnp.int32(0)
    begin = jnp.zeros((slots, 1), f32)
    for h in range(hist):
        starts.append(start)
        begin = jnp.where(slot_h == float(h), (start * TILE).astype(f32), begin)
        count = jnp.sum(hot[:, h : h + 1]).astype(jnp.int32)
        start = start + (count + (TILE - 1)) // TILE
    dest = jnp.where(valid, begin + rank, -1.0)
    eye = iota((slots, slots), 0) == iota((slots, slots), 1)
    dest_row = jnp.sum(jnp.where(eye, dest, 0.0), axis=0, keepdims=True).astype(jnp.int32)
    return dest.astype(jnp.int32), dest_row, starts, start


def target_tile(tile, starts, dest_row, recv_ref, enc_ref, grouped_ref, turned_ref):
    seq, width = enc_ref.shape[1:]
    head = width // HEADS
    masks = lane_masks(2 * head, head)
    scale = 0.5 * head**-0.5
    base = pl.multiple_of(tile * TILE, TILE)
    hist = jnp.int32(0)
    for start in starts[1:]:
        hist = hist + (tile >= start).astype(jnp.int32)
    choose = (iota((TILE, dest_row.shape[1]), 0) + base == dest_row).astype(f32).astype(bf16)
    rows = dot_nn(choose, recv_ref[...])
    q_all = rows[:, :width] * scale
    g_all = rows[:, width : 2 * width]
    q_t = jnp.transpose(q_all).astype(bf16)
    g_t = jnp.transpose(g_all).astype(bf16)
    q_all = q_all.astype(bf16)
    g_all = g_all.astype(bf16)
    length = rows[:, 2 * width + 1 : 2 * width + 2]
    positions = iota((TILE, seq), 1).astype(f32)
    weight = jnp.where(positions < length, 1.0 / jnp.maximum(length, 1.0), 0.0)
    for pair in range(HEADS // 2):
        cols = slice(pair * 2 * head, (pair + 1) * 2 * head)
        k_p = enc_ref[hist, :, cols]
        both = dot_nt(
            jnp.concatenate(
                [both_heads(q_all[:, cols], masks), both_heads(g_all[:, cols], masks)], axis=0
            ),
            k_p,
        )
        slopes = []
        for j in range(2):
            h = 2 * pair + j
            mine = slice(h * head, (h + 1) * head)
            act, slope = silu_pair(both[j * TILE : (j + 1) * TILE])
            d_attn = both[(2 + j) * TILE : (3 + j) * TILE]
            attn = (act * weight).astype(bf16)
            d_s = (d_attn * weight * slope).astype(bf16)
            turned_ref[hist, mine, :] += dot_nn(
                jnp.concatenate([g_t[mine], q_t[mine]], axis=1),
                jnp.concatenate([attn, d_s], axis=0),
            )
            slopes.append(d_s)
        d_q = pick_lanes(dot_nn(jnp.concatenate(slopes, axis=0), k_p), head)
        grouped_ref[pl.ds(base, TILE), cols] = (d_q * scale).astype(bf16)


def norm_backward(denc_ref, wout_ref, normed_ref, nu_ref, gi_ref, dmix_ref, dpre_ref):
    hist, seq, width = denc_ref.shape
    for at in range(hist):
        here = slice(at * seq, (at + 1) * seq)
        d_merged = dot_nt(denc_ref[at], wout_ref[...])
        dpre_ref[here, :width] = (d_merged * nu_ref[at].astype(f32)).astype(bf16)
        normed = normed_ref[at].astype(f32)
        d_norm = d_merged * gi_ref[at].astype(f32)
        d_mix = (
            d_norm
            - jnp.mean(d_norm, axis=1, keepdims=True)
            - normed * jnp.mean(d_norm * normed, axis=1, keepdims=True)
        )
        dmix_ref[at] = d_mix.astype(bf16)


def attention_backward(
    at, dmix_ref, v_ref, k_ref, q_t_ref, attn_t_ref, grad_ref, slope_ref, slope_t_ref, dpre_ref, dk_ref
):
    seq, width = dmix_ref.shape[1:]
    head = width // HEADS
    here = slice(at * seq, (at + 1) * seq)
    masks = lane_masks(2 * head, head)
    scale = 0.5 * head**-0.5 / seq
    for pair in range(HEADS // 2):
        cols = slice(pair * 2 * head, (pair + 1) * 2 * head)
        d_p = dmix_ref[at, :, cols]
        d_attn = dot_nt(both_heads(d_p, masks), v_ref[at, :, cols])
        d_s = [
            (d_attn[j * seq : (j + 1) * seq] * grad_ref[at, 2 * pair + j].astype(f32)).astype(bf16)
            for j in range(2)
        ]
        attn_t = jnp.concatenate([attn_t_ref[at, 2 * pair], attn_t_ref[at, 2 * pair + 1]], axis=0)
        d_v = pick_lanes(dot_nn(attn_t, d_p), head) * (1.0 / seq)
        d_q = pick_lanes(dot_nn(jnp.concatenate(d_s, axis=0), k_ref[at, :, cols]), head) * scale
        for branch, grad in ((0, d_v), (1, d_q)):
            old = slice(branch * width + pair * 2 * head, branch * width + (pair + 1) * 2 * head)
            new = slice(old.start + width, old.stop + width)
            dpre_ref[here, new] = (grad * slope_ref[at, :, old].astype(f32)).astype(bf16)
        for j in range(2):
            mine = slice((2 * pair + j) * head, (2 * pair + j + 1) * head)
            d_k = dot_nn(q_t_ref[at, mine], d_s[j]) * scale
            dk_ref[mine, here] = (d_k * slope_t_ref[at, mine].astype(f32)).astype(bf16)


def owner_kernel(*refs):
    n_in, n_out = 15, 6
    sources, outs, refs = refs[:n_in], refs[n_in : n_in + n_out], refs[n_in + n_out :]
    held, refs = refs[:n_in], refs[n_in:]
    (
        recv_ref, enc_ref, wout_ref, normed_ref, nu_ref, gi_ref, v_ref, k_ref, q_t_ref,
        attn_t_ref, grad_ref, slope_ref, slope_t_ref, mt_ref, xt_ref,
    ) = held
    grouped_ref, turned_ref, dmix_ref, dq_ref, denc_ref, dpre_ref, dk_ref, keep_ref, send_ref, sem_in, sem_out = refs
    dq_hbm, denc_hbm, dpre_hbm, dk_hbm, keep_hbm, send_hbm = outs
    hist, seq, width = enc_ref.shape
    slots, padded = recv_ref.shape[0], grouped_ref.shape[0]
    kept = keep_ref.shape[0]

    def load(i, n, at=None):
        source, dest = (sources[i], held[i]) if at is None else (sources[i].at[at], held[i].at[at])
        return pltpu.make_async_copy(source, dest, sem_in.at[n])

    first = [load(i, i) for i in range(6)]
    by_history = [[load(i, i + 7 * at, at) for i in range(6, 13)] for at in range(hist)]
    last = [load(i, 7 * hist + i - 7) for i in (13, 14)]
    for copy in first + sum(by_history, []) + last:
        copy.start()
    grouped_ref[...] = jnp.zeros_like(grouped_ref)
    turned_ref[...] = jnp.zeros_like(turned_ref)
    first[0].wait()
    dest, dest_row, starts, tiles = group_slots(recv_ref, hist)
    first[1].wait()

    def one_tile(tile, carry):
        target_tile(tile, starts, dest_row, recv_ref, enc_ref, grouped_ref, turned_ref)
        return carry

    lax.fori_loop(0, tiles, one_tile, 0)
    for h in range(hist):
        denc_ref[h] = jnp.transpose(turned_ref[h]).astype(bf16)
    back = (dest == iota((slots, padded), 1)).astype(f32).astype(bf16)
    dq_ref[...] = dot_nn(back, grouped_ref[...]).astype(bf16)
    stores = []

    def store(source, dest):
        copy = pltpu.make_async_copy(source, dest, sem_out.at[len(stores)])
        copy.start()
        stores.append(copy)

    store(denc_ref, denc_hbm)
    store(dq_ref, dq_hbm)
    for copy in first[2:]:
        copy.wait()
    norm_backward(denc_ref, wout_ref, normed_ref, nu_ref, gi_ref, dmix_ref, dpre_ref)
    for at in range(hist):
        for copy in by_history[at]:
            copy.wait()
        attention_backward(
            at, dmix_ref, v_ref, k_ref, q_t_ref, attn_t_ref, grad_ref, slope_ref, slope_t_ref,
            dpre_ref, dk_ref,
        )
        here = pl.ds(at * seq, seq)
        store(dpre_ref.at[here, :], dpre_hbm.at[here, :])
        store(dk_ref.at[:, here], dk_hbm.at[:, here])
    for copy in last:
        copy.wait()
    for block in range(5):
        cols = slice(block * width, (block + 1) * width)
        if block == 0:
            part = dot_nn(mt_ref[...], denc_ref[...].reshape(hist * seq, width))
        elif block == 4:
            part = dot_nt(xt_ref[...], dk_ref[...])
        else:
            part = dot_nn(xt_ref[...], dpre_ref[:, (block - 1) * width : block * width])
        keep_ref[:, cols] = part[:kept].astype(bf16)
        send_ref[:, cols] = part[kept:].astype(bf16)
        store(keep_ref.at[:, cols], keep_hbm.at[:, cols])
        store(send_ref.at[:, cols], send_hbm.at[:, cols])
    for copy in stores:
        copy.wait()


def owner_backward(recv, enc, w_out, state, mt, xt, kept):
    hist, seq, width = enc.shape
    slots = recv.shape[0]
    rows = hist * seq
    padded = ((slots - hist) // TILE + hist) * TILE
    operands = (recv, enc, w_out) + state + (mt, xt)
    raw = pl.BlockSpec(memory_space=pl.ANY)
    outs = [
        jax.ShapeDtypeStruct((slots, width), bf16),
        jax.ShapeDtypeStruct(enc.shape, bf16),
        jax.ShapeDtypeStruct((rows, 3 * width), bf16),
        jax.ShapeDtypeStruct((width, rows), bf16),
        jax.ShapeDtypeStruct((kept, 5 * width), bf16),
        jax.ShapeDtypeStruct((width - kept, 5 * width), bf16),
    ]
    return pl.pallas_call(
        owner_kernel,
        grid=(1,),
        in_specs=[raw] * len(operands),
        out_specs=[raw] * len(outs),
        out_shape=outs,
        scratch_shapes=[pltpu.VMEM(a.shape, a.dtype) for a in operands]
        + [
            pltpu.VMEM((padded, width), bf16),
            pltpu.VMEM((hist, width, seq), f32),
            pltpu.VMEM((hist, seq, width), bf16),
        ]
        + [pltpu.VMEM(a.shape, a.dtype) for a in outs]
        + [
            pltpu.SemaphoreType.DMA((7 * hist + 8,)),
            pltpu.SemaphoreType.DMA((2 * hist + 12,)),
        ],
        compiler_params=params(60),
        cost_estimate=cost(30e9, 30e6),
        name="owner_backward",
    )(*operands)


def input_kernel(denc_ref, win_ref, dpre_ref, dk_ref, out_ref):
    width = denc_ref.shape[2]
    total = denc_ref[0].astype(f32) + dot_nt(dpre_ref[...], win_ref[:, : 3 * width])
    total = total + dot_nt(jnp.transpose(dk_ref[...]), win_ref[:, 3 * width :])
    out_ref[0] = total.astype(bf16)


def input_backward(denc, w_in, dpre, dk):
    hist, seq, width = denc.shape
    block = lambda a: pl.BlockSpec((1,) + a.shape[1:], lambda i: (i, 0, 0))
    return pl.pallas_call(
        input_kernel,
        grid=(hist,),
        in_specs=[
            block(denc),
            whole(w_in.shape),
            pl.BlockSpec((seq, 3 * width), lambda i: (i, 0)),
            pl.BlockSpec((width, seq), lambda i: (0, i)),
        ],
        out_specs=block(denc),
        out_shape=jax.ShapeDtypeStruct(denc.shape, bf16),
        compiler_params=params(60),
        cost_estimate=cost(6e9, 8e6),
        name="input_backward",
    )(denc, w_in, dpre, dk)


def owner_order(width):
    n_y, n_core, n_z, n_x = (lax.axis_size(a) for a in AXES)
    rows = width // (n_y * n_core * n_z * n_x)
    place = jnp.arange(width, dtype=jnp.int32)
    inner = place % rows
    place = place // rows
    z, place = place % n_z, place // n_z
    x, place = place % n_x, place // n_x
    y, d_core = place % n_y, place // n_y
    core = (lax.axis_index(AXES[1]) + d_core) % n_core
    y, x = (lax.axis_index(AXES[0]) + y) % n_y, (lax.axis_index(AXES[3]) + x) % n_x
    z = (lax.axis_index(AXES[2]) + z) % n_z
    source = (((y * n_core + core) * n_z + z) * n_x + x) * rows + inner
    return (source[:, None] == jnp.arange(width, dtype=jnp.int32)[None, :]).astype(bf16)


def return_orders(capacity):
    sizes = n_y, n_core, n_z, n_x = tuple(lax.axis_size(a) for a in AXES)
    slots = n_y * n_core * n_z * n_x * capacity
    place = jnp.arange(slots, dtype=jnp.int32)
    inner, block = place % capacity, place // capacity
    plane = n_y * n_x
    orders = []
    for sign, (d_core, d_z, d_plane) in (
        (1, (block // (plane * n_z), block // plane % n_z, block % plane)),
        (-1, (block % n_core, block // n_core % n_z, block // (n_core * n_z))),
    ):
        y, core, z, x = (
            (lax.axis_index(a) + sign * d + n) % n
            for a, d, n in zip(AXES, (d_plane // n_x, d_core, d_z, d_plane % n_x), sizes)
        )
        source = (((y * n_core + core) * n_z + z) * n_x + x) * capacity + inner
        orders.append((source[:, None] == place[None, :]).astype(bf16))
    return orders


def add_up(blocks):
    total = blocks[0].astype(f32)
    for block in blocks[1:]:
        total = total + block.astype(f32)
    return total


def core_stage(keep, send):
    return add_up(send_blocks([keep] + cut_rows(send, lax.axis_size(AXES[1]) - 1), AXES[1:2])).astype(bf16)


def send_blocks(blocks, axes):
    count = len(blocks)
    sizes = [lax.axis_size(a) for a in axes]
    parts = [blocks[0]]
    for d in range(1, count):
        pairs = []
        for c in range(count):
            there, stride, rest_c, rest_d = 0, 1, c, d
            for n in reversed(sizes):
                there += (rest_c + rest_d) % n * stride
                stride, rest_c, rest_d = stride * n, rest_c // n, rest_d // n
            pairs.append((c, there))
        parts.append(lax.ppermute(blocks[d], axes, pairs))
    return parts


def cut_rows(rows, count):
    step = rows.shape[0] // count
    return [rows[i * step : (i + 1) * step] for i in range(count)]


def local(histories, weight_in, weight_out, candidates, cotangent, owner_ids, hist_slot, lengths):
    devices = lax.axis_size(AXES)
    imp_rows, width = candidates.shape
    capacity = max(2, 2 * imp_rows // devices)
    slots = devices * capacity
    kept = width // lax.axis_size(AXES[1])
    after = lax.optimization_barrier

    n_y, n_core, n_z, n_x = (lax.axis_size(a) for a in AXES)
    core, line, plane = AXES[1:2], AXES[2:3], (AXES[0], AXES[3])
    send, pick = route(owner_ids, hist_slot, lengths, candidates, cotangent, devices, capacity)
    shaped = send.reshape(devices, capacity, send.shape[1])
    recv = lax.all_to_all(shaped, AXES, split_axis=0, concat_axis=0, tiled=True)
    recv = recv.reshape(slots, send.shape[1])
    perm = owner_order(width)
    leaving, arriving = return_orders(capacity)
    pick = dot_nn(arriving, pick).astype(bf16)
    enc, slope, slope_t, v, q, k, q_t, attn_t, grad, normed, nu, gi, xt, mt = layer_forward(
        histories, weight_in, weight_out, perm
    )
    state = (normed, nu, gi, v, k, q_t, attn_t, grad, slope, slope_t)
    d_query, d_enc, dpre, dk, keep, send = owner_backward(recv, enc, weight_out, state, mt, xt, kept)
    d_query = dot_nn(leaving, d_query).astype(bf16)
    rows = core_stage(keep, send)
    d_enc, rows, d_query = after((d_enc, rows, d_query))
    back = [cut_rows(b, n_z) for b in send_blocks(cut_rows(d_query, n_core), core)]
    back = [jnp.concatenate([b[d] for b in back], axis=0) for d in range(n_z)]
    d_inputs = input_backward(d_enc, weight_in, dpre, dk)
    back = send_blocks(back, line)
    parts = send_blocks(cut_rows(rows, n_y * n_x), plane)
    back, parts, d_inputs = after((back, parts, d_inputs))
    parts = send_blocks(cut_rows(add_up(parts).astype(bf16), n_z), line)
    back = [b.reshape(n_core, n_y * n_x, capacity, width) for b in back]
    back = [
        jnp.concatenate([b[:, i].reshape(n_core * capacity, width) for b in back], axis=0)
        for i in range(n_y * n_x)
    ]
    returned = jnp.concatenate(send_blocks(back, plane), axis=0)
    candidate_grad = lax.dot_general(
        pick, returned, (((0,), (0,)), ((), ())), preferred_element_type=f32
    ).astype(bf16)
    w_in_grad = add_up([p[:, width:] for p in parts])
    w_out_grad = add_up([p[:, :width] for p in parts])
    return d_inputs, candidate_grad, w_in_grad, w_out_grad


def solution(mesh):
    n_hash, n_dp = mesh.devices.shape
    fine = jax.sharding.Mesh(mesh.devices.reshape(n_hash // 2, 2, n_dp // 2, 2), AXES)
    return jax.shard_map(
        local,
        mesh=fine,
        in_specs=(
            P(AXES, None, None),
            P(),
            P(),
            P(AXES, None),
            P(AXES, None),
            P(AXES, None),
            P(AXES),
            P(AXES),
        ),
        out_specs=(
            P(AXES, None, None),
            P(AXES, None),
            P(AXES, None),
            P(AXES, None),
        ),
        check_vma=False,
    )
```

```python
import functools

import jax
import jax.numpy as jnp
from jax import lax
from jax.experimental import pallas as pl
from jax.experimental.pallas import tpu as pltpu
from jax.sharding import PartitionSpec as P

HEADS = 8
TILE = 128
META = 128
AXES = ("hash_hi", "core", "dp_hi", "dp_lo")
norm_eps = 1e-05
f32 = jnp.float32
bf16 = jnp.bfloat16
MIB = 1024 * 1024


def dot_nn(a, b):
    return lax.dot_general(a, b, (((1,), (0,)), ((), ())), preferred_element_type=f32)


def dot_nt(a, b):
    return lax.dot_general(a, b, (((1,), (1,)), ((), ())), preferred_element_type=f32)


def dot_tn(a, b):
    return lax.dot_general(a, b, (((0,), (0,)), ((), ())), preferred_element_type=f32)


def iota(shape, axis):
    return lax.broadcasted_iota(jnp.int32, shape, axis)


def silu_pair(half):
    t = jnp.tanh(half)
    u = 1.0 + t
    act = half * u
    return act, u + act * (1.0 - t)


def lane_masks(width, part):
    lane = iota((1, width), 1)
    return [((lane >= j * part) & (lane < (j + 1) * part)).astype(bf16) for j in range(width // part)]


def both_heads(pair, masks):
    return jnp.concatenate([pair * m for m in masks], axis=0)


def pick_lanes(stacked, head):
    rows = stacked.shape[0] // 2
    lane = iota((1, 2 * head), 1)
    return jnp.where(lane < head, stacked[:rows], stacked[rows:])


def params(mib):
    return pltpu.CompilerParams(dimension_semantics=("arbitrary",), vmem_limit_bytes=mib * MIB)


def whole(shape):
    return pl.BlockSpec(shape, lambda i: (0,) * len(shape))


def cost(flops, nbytes, trans=0):
    return pl.CostEstimate(flops=int(flops), bytes_accessed=int(nbytes), transcendentals=int(trans))


def route_kernel(devices, capacity, own_ref, slot_ref, len_ref, cand_ref, cot_ref, send_ref, pick_ref):
    rows, width = cand_ref.shape
    slots = devices * capacity
    own = own_ref[...]
    hot = (own == iota((devices, rows), 0)).astype(f32)
    before = (iota((rows, rows), 0) < iota((rows, rows), 1)).astype(f32).astype(bf16)
    earlier = dot_nn(hot.astype(bf16), before)
    position = jnp.sum(earlier * hot, axis=0, keepdims=True).astype(jnp.int32)
    target = own * capacity + position
    pick = (target == iota((slots, rows), 0)).astype(f32).astype(bf16)
    pick_ref[...] = pick
    send_ref[:, :width] = dot_nn(pick, cand_ref[...]).astype(bf16)
    send_ref[:, width : 2 * width] = dot_nn(pick, cot_ref[...]).astype(bf16)
    line = iota((META, rows), 0)
    meta = jnp.where(line == 0, slot_ref[...], jnp.where(line == 1, len_ref[...], 0))
    send_ref[:, 2 * width :] = dot_nt(pick, meta.astype(f32).astype(bf16)).astype(bf16)


def route(own, slot, length, cand, cot, devices, capacity):
    rows, width = cand.shape
    slots = devices * capacity
    line = whole((1, rows))
    return pl.pallas_call(
        functools.partial(route_kernel, devices, capacity),
        grid=(1,),
        in_specs=[line, line, line, whole(cand.shape), whole(cot.shape)],
        out_specs=[whole((slots, 2 * width + META)), whole((slots, rows))],
        out_shape=(
            jax.ShapeDtypeStruct((slots, 2 * width + META), bf16),
            jax.ShapeDtypeStruct((slots, rows), bf16),
        ),
        compiler_params=params(60),
        cost_estimate=cost(2e9, 4 * rows * width * 4),
        name="route",
    )(own.reshape(1, rows), slot.reshape(1, rows), length.reshape(1, rows), cand, cot)


def forward_kernel(
    x_ref, win_ref, wout_ref, perm_ref,
    enc_ref, slope_ref, slope_t_ref, v_ref, q_ref, k_ref, q_t_ref, attn_t_ref, grad_ref,
    normed_ref, nu_ref, gi_ref, xt_ref, mt_ref,
    gate_ref, mixed_ref, slope_u_ref,
):
    seq, width = x_ref.shape[1:]
    head = width // HEADS
    half_seq = seq // 2
    x = x_ref[0]
    for branch in range(4):
        cols = slice(branch * width, (branch + 1) * width)
        act, slope = silu_pair(0.5 * dot_nn(x, win_ref[:, cols]))
        if branch == 3:
            slope_t_ref[0] = jnp.transpose(0.5 * slope).astype(bf16)
        elif branch > 0:
            slope_ref[0, :, (branch - 1) * width : branch * width] = (0.5 * slope).astype(bf16)
        if branch == 0:
            gate_ref[...] = act
            slope_u_ref[...] = 0.5 * slope
        else:
            (v_ref, q_ref, k_ref)[branch - 1][0] = act.astype(bf16)
        if branch == 2:
            q_t_ref[0] = jnp.transpose(act).astype(bf16)
    masks = lane_masks(2 * head, head)
    scale = 0.5 * head**-0.5
    tri = iota((half_seq, half_seq), 0) >= iota((half_seq, half_seq), 1)
    zero = jnp.zeros((half_seq, half_seq), f32)
    for pair in range(HEADS // 2):
        cols = slice(pair * 2 * head, (pair + 1) * 2 * head)
        q_p = q_ref[0, :, cols] * jnp.asarray(scale, bf16)
        half = dot_nt(both_heads(q_p, masks), k_ref[0, :, cols])
        stack = []
        for j in range(2):
            h = 2 * pair + j
            top = silu_pair(half[j * seq : j * seq + half_seq, :half_seq])
            bot = silu_pair(half[j * seq + half_seq : (j + 1) * seq])
            full = []
            for a, b in zip(top, bot):
                a = jnp.concatenate([jnp.where(tri, a, 0.0), zero], axis=1)
                b = jnp.concatenate([b[:, :half_seq], jnp.where(tri, b[:, half_seq:], 0.0)], axis=1)
                full.append(jnp.concatenate([a, b], axis=0))
            stack.append(full[0].astype(bf16))
            attn_t_ref[0, h] = jnp.transpose(full[0]).astype(bf16)
            grad_ref[0, h] = full[1].astype(bf16)
        mixed = dot_nn(jnp.concatenate(stack, axis=0), v_ref[0, :, cols])
        mixed_ref[:, cols] = pick_lanes(mixed, head) * (1.0 / seq)
    mixed = mixed_ref[...]
    centred = mixed - jnp.mean(mixed, axis=1, keepdims=True)
    inv_std = lax.rsqrt(jnp.mean(centred * centred, axis=1, keepdims=True) + norm_eps)
    normed = centred * inv_std
    gate = gate_ref[...]
    merged = (normed * gate).astype(bf16)
    normed_ref[0] = normed.astype(bf16)
    nu_ref[0] = (normed * slope_u_ref[...]).astype(bf16)
    gi_ref[0] = (gate * inv_std).astype(bf16)
    enc_ref[0] = (x.astype(f32) + dot_nn(merged, wout_ref[...])).astype(bf16)
    perm = perm_ref[...]
    xt_ref[...] = dot_nt(perm, x).astype(bf16)
    mt_ref[...] = dot_nt(perm, merged).astype(bf16)


def layer_forward(x, w_in, w_out, perm):
    hist, seq, width = x.shape
    row = pl.BlockSpec((1, seq, width), lambda i: (i, 0, 0))
    wide = pl.BlockSpec((1, seq, 2 * width), lambda i: (i, 0, 0))
    column = pl.BlockSpec((1, width, seq), lambda i: (i, 0, 0))
    square = pl.BlockSpec((1, HEADS, seq, seq), lambda i: (i, 0, 0, 0))
    turned = pl.BlockSpec((width, seq), lambda i: (0, i))
    row_s = jax.ShapeDtypeStruct((hist, seq, width), bf16)
    column_s = jax.ShapeDtypeStruct((hist, width, seq), bf16)
    square_s = jax.ShapeDtypeStruct((hist, HEADS, seq, seq), bf16)
    turned_s = jax.ShapeDtypeStruct((width, hist * seq), bf16)
    return pl.pallas_call(
        forward_kernel,
        grid=(hist,),
        in_specs=[row, whole(w_in.shape), whole(w_out.shape), whole(perm.shape)],
        out_specs=[
            row, wide, column, row, row, row, column, square, square, row, row, row, turned, turned,
        ],
        out_shape=[
            row_s, jax.ShapeDtypeStruct((hist, seq, 2 * width), bf16), column_s, row_s, row_s, row_s,
            column_s, square_s, square_s, row_s, row_s, row_s, turned_s, turned_s,
        ],
        scratch_shapes=[pltpu.VMEM((seq, width), f32)] * 3,
        compiler_params=params(60),
        cost_estimate=cost(18e9, 24e6),
        name="forward",
    )(x, w_in, w_out, perm)


def group_slots(recv_ref, hist):
    slots, width = recv_ref.shape
    meta = recv_ref[:, width - META :].astype(f32)
    slot_h = meta[:, 0:1]
    valid = meta[:, 1:2] > 0.0
    lane = iota((slots, META), 1).astype(f32)
    hot = jnp.where(valid & (slot_h == lane), 1.0, 0.0)
    lower = (iota((slots, slots), 0) > iota((slots, slots), 1)).astype(f32).astype(bf16)
    rank = jnp.sum(dot_nn(lower, hot.astype(bf16)) * hot, axis=1, keepdims=True)
    starts, start = [], jnp.int32(0)
    begin = jnp.zeros((slots, 1), f32)
    for h in range(hist):
        starts.append(start)
        begin = jnp.where(slot_h == float(h), (start * TILE).astype(f32), begin)
        count = jnp.sum(hot[:, h : h + 1]).astype(jnp.int32)
        start = start + (count + (TILE - 1)) // TILE
    dest = jnp.where(valid, begin + rank, -1.0)
    eye = iota((slots, slots), 0) == iota((slots, slots), 1)
    dest_row = jnp.sum(jnp.where(eye, dest, 0.0), axis=0, keepdims=True).astype(jnp.int32)
    return dest.astype(jnp.int32), dest_row, starts, start


def target_tile(tile, starts, dest_row, recv_ref, enc_ref, grouped_ref, turned_ref):
    seq, width = enc_ref.shape[1:]
    head = width // HEADS
    masks = lane_masks(2 * head, head)
    scale = 0.5 * head**-0.5
    base = pl.multiple_of(tile * TILE, TILE)
    hist = jnp.int32(0)
    for start in starts[1:]:
        hist = hist + (tile >= start).astype(jnp.int32)
    choose = (iota((TILE, dest_row.shape[1]), 0) + base == dest_row).astype(f32).astype(bf16)
    rows = dot_nn(choose, recv_ref[...])
    q_all = rows[:, :width] * scale
    g_all = rows[:, width : 2 * width]
    q_t = jnp.transpose(q_all).astype(bf16)
    g_t = jnp.transpose(g_all).astype(bf16)
    q_all = q_all.astype(bf16)
    g_all = g_all.astype(bf16)
    length = rows[:, 2 * width + 1 : 2 * width + 2]
    positions = iota((TILE, seq), 1).astype(f32)
    weight = jnp.where(positions < length, 1.0 / jnp.maximum(length, 1.0), 0.0)
    for pair in range(HEADS // 2):
        cols = slice(pair * 2 * head, (pair + 1) * 2 * head)
        k_p = enc_ref[hist, :, cols]
        both = dot_nt(
            jnp.concatenate(
                [both_heads(q_all[:, cols], masks), both_heads(g_all[:, cols], masks)], axis=0
            ),
            k_p,
        )
        slopes = []
        for j in range(2):
            h = 2 * pair + j
            mine = slice(h * head, (h + 1) * head)
            act, slope = silu_pair(both[j * TILE : (j + 1) * TILE])
            d_attn = both[(2 + j) * TILE : (3 + j) * TILE]
            attn = (act * weight).astype(bf16)
            d_s = (d_attn * weight * slope).astype(bf16)
            turned_ref[hist, mine, :] += dot_nn(
                jnp.concatenate([g_t[mine], q_t[mine]], axis=1),
                jnp.concatenate([attn, d_s], axis=0),
            )
            slopes.append(d_s)
        d_q = pick_lanes(dot_nn(jnp.concatenate(slopes, axis=0), k_p), head)
        grouped_ref[pl.ds(base, TILE), cols] = (d_q * scale).astype(bf16)


def norm_backward(denc_ref, wout_ref, normed_ref, nu_ref, gi_ref, dmix_ref, dpre_ref):
    hist, seq, width = denc_ref.shape
    for at in range(hist):
        here = slice(at * seq, (at + 1) * seq)
        d_merged = dot_nt(denc_ref[at], wout_ref[...])
        dpre_ref[here, :width] = (d_merged * nu_ref[at].astype(f32)).astype(bf16)
        normed = normed_ref[at].astype(f32)
        d_norm = d_merged * gi_ref[at].astype(f32)
        d_mix = (
            d_norm
            - jnp.mean(d_norm, axis=1, keepdims=True)
            - normed * jnp.mean(d_norm * normed, axis=1, keepdims=True)
        )
        dmix_ref[at] = d_mix.astype(bf16)


def attention_backward(
    at, dmix_ref, v_ref, k_ref, q_t_ref, attn_t_ref, grad_ref, slope_ref, slope_t_ref, dpre_ref, dk_ref
):
    seq, width = dmix_ref.shape[1:]
    head = width // HEADS
    here = slice(at * seq, (at + 1) * seq)
    masks = lane_masks(2 * head, head)
    scale = 0.5 * head**-0.5 / seq
    for pair in range(HEADS // 2):
        cols = slice(pair * 2 * head, (pair + 1) * 2 * head)
        d_p = dmix_ref[at, :, cols]
        d_attn = dot_nt(both_heads(d_p, masks), v_ref[at, :, cols])
        d_s = [
            (d_attn[j * seq : (j + 1) * seq] * grad_ref[at, 2 * pair + j].astype(f32)).astype(bf16)
            for j in range(2)
        ]
        attn_t = jnp.concatenate([attn_t_ref[at, 2 * pair], attn_t_ref[at, 2 * pair + 1]], axis=0)
        d_v = pick_lanes(dot_nn(attn_t, d_p), head) * (1.0 / seq)
        d_q = pick_lanes(dot_nn(jnp.concatenate(d_s, axis=0), k_ref[at, :, cols]), head) * scale
        for branch, grad in ((0, d_v), (1, d_q)):
            old = slice(branch * width + pair * 2 * head, branch * width + (pair + 1) * 2 * head)
            new = slice(old.start + width, old.stop + width)
            dpre_ref[here, new] = (grad * slope_ref[at, :, old].astype(f32)).astype(bf16)
        for j in range(2):
            mine = slice((2 * pair + j) * head, (2 * pair + j + 1) * head)
            d_k = dot_nn(q_t_ref[at, mine], d_s[j]) * scale
            dk_ref[mine, here] = (d_k * slope_t_ref[at, mine].astype(f32)).astype(bf16)


def owner_kernel(*refs):
    n_in, n_out = 15, 6
    sources, outs, refs = refs[:n_in], refs[n_in : n_in + n_out], refs[n_in + n_out :]
    held, refs = refs[:n_in], refs[n_in:]
    (
        recv_ref, enc_ref, wout_ref, normed_ref, nu_ref, gi_ref, v_ref, k_ref, q_t_ref,
        attn_t_ref, grad_ref, slope_ref, slope_t_ref, mt_ref, xt_ref,
    ) = held
    grouped_ref, turned_ref, dmix_ref, dq_ref, denc_ref, dpre_ref, dk_ref, keep_ref, send_ref, sem_in, sem_out = refs
    dq_hbm, denc_hbm, dpre_hbm, dk_hbm, keep_hbm, send_hbm = outs
    hist, seq, width = enc_ref.shape
    slots, padded = recv_ref.shape[0], grouped_ref.shape[0]
    kept = keep_ref.shape[0]

    def load(i, n, at=None):
        source, dest = (sources[i], held[i]) if at is None else (sources[i].at[at], held[i].at[at])
        return pltpu.make_async_copy(source, dest, sem_in.at[n])

    first = [load(i, i) for i in range(6)]
    by_history = [[load(i, i + 7 * at, at) for i in range(6, 13)] for at in range(hist)]
    last = [load(i, 7 * hist + i - 7) for i in (13, 14)]
    for copy in first + sum(by_history, []) + last:
        copy.start()
    grouped_ref[...] = jnp.zeros_like(grouped_ref)
    turned_ref[...] = jnp.zeros_like(turned_ref)
    first[0].wait()
    dest, dest_row, starts, tiles = group_slots(recv_ref, hist)
    first[1].wait()

    def one_tile(tile, carry):
        target_tile(tile, starts, dest_row, recv_ref, enc_ref, grouped_ref, turned_ref)
        return carry

    lax.fori_loop(0, tiles, one_tile, 0)
    for h in range(hist):
        denc_ref[h] = jnp.transpose(turned_ref[h]).astype(bf16)
    back = (dest == iota((slots, padded), 1)).astype(f32).astype(bf16)
    dq_ref[...] = dot_nn(back, grouped_ref[...]).astype(bf16)
    stores = []

    def store(source, dest):
        copy = pltpu.make_async_copy(source, dest, sem_out.at[len(stores)])
        copy.start()
        stores.append(copy)

    store(denc_ref, denc_hbm)
    store(dq_ref, dq_hbm)
    for copy in first[2:]:
        copy.wait()
    norm_backward(denc_ref, wout_ref, normed_ref, nu_ref, gi_ref, dmix_ref, dpre_ref)
    for at in range(hist):
        for copy in by_history[at]:
            copy.wait()
        attention_backward(
            at, dmix_ref, v_ref, k_ref, q_t_ref, attn_t_ref, grad_ref, slope_ref, slope_t_ref,
            dpre_ref, dk_ref,
        )
        here = pl.ds(at * seq, seq)
        store(dpre_ref.at[here, :], dpre_hbm.at[here, :])
        store(dk_ref.at[:, here], dk_hbm.at[:, here])
    for copy in last:
        copy.wait()
    for block in range(5):
        cols = slice(block * width, (block + 1) * width)
        if block == 0:
            part = dot_nn(mt_ref[...], denc_ref[...].reshape(hist * seq, width))
        elif block == 4:
            part = dot_nt(xt_ref[...], dk_ref[...])
        else:
            part = dot_nn(xt_ref[...], dpre_ref[:, (block - 1) * width : block * width])
        keep_ref[:, cols] = part[:kept].astype(bf16)
        send_ref[:, cols] = part[kept:].astype(bf16)
        store(keep_ref.at[:, cols], keep_hbm.at[:, cols])
        store(send_ref.at[:, cols], send_hbm.at[:, cols])
    for copy in stores:
        copy.wait()


def owner_backward(recv, enc, w_out, state, mt, xt, kept):
    hist, seq, width = enc.shape
    slots = recv.shape[0]
    rows = hist * seq
    padded = ((slots - hist) // TILE + hist) * TILE
    operands = (recv, enc, w_out) + state + (mt, xt)
    raw = pl.BlockSpec(memory_space=pl.ANY)
    outs = [
        jax.ShapeDtypeStruct((slots, width), bf16),
        jax.ShapeDtypeStruct(enc.shape, bf16),
        jax.ShapeDtypeStruct((rows, 3 * width), bf16),
        jax.ShapeDtypeStruct((width, rows), bf16),
        jax.ShapeDtypeStruct((kept, 5 * width), bf16),
        jax.ShapeDtypeStruct((width - kept, 5 * width), bf16),
    ]
    return pl.pallas_call(
        owner_kernel,
        grid=(1,),
        in_specs=[raw] * len(operands),
        out_specs=[raw] * len(outs),
        out_shape=outs,
        scratch_shapes=[pltpu.VMEM(a.shape, a.dtype) for a in operands]
        + [
            pltpu.VMEM((padded, width), bf16),
            pltpu.VMEM((hist, width, seq), f32),
            pltpu.VMEM((hist, seq, width), bf16),
        ]
        + [pltpu.VMEM(a.shape, a.dtype) for a in outs]
        + [
            pltpu.SemaphoreType.DMA((7 * hist + 8,)),
            pltpu.SemaphoreType.DMA((2 * hist + 12,)),
        ],
        compiler_params=params(60),
        cost_estimate=cost(30e9, 30e6),
        name="owner_backward",
    )(*operands)


def input_kernel(denc_ref, win_ref, dpre_ref, dk_ref, *refs):
    out_ref = refs[-1]
    width = denc_ref.shape[2]
    total = denc_ref[0].astype(f32) + dot_nt(dpre_ref[...], win_ref[:, : 3 * width])
    total = total + dot_nt(jnp.transpose(dk_ref[...]), win_ref[:, 3 * width :])
    out_ref[0] = total.astype(bf16)


def input_backward(denc, w_in, dpre, dk, part, parts, earlier=None):
    hist, seq, width = denc.shape
    count = hist // parts
    begin = part * count
    block = pl.BlockSpec((1, seq, width), lambda i: (i + begin, 0, 0))
    held = [] if earlier is None else [earlier]
    return pl.pallas_call(
        input_kernel,
        grid=(count,),
        in_specs=[
            block,
            whole(w_in.shape),
            pl.BlockSpec((seq, 3 * width), lambda i: (i + begin, 0)),
            pl.BlockSpec((width, seq), lambda i: (0, i + begin)),
        ]
        + [pl.BlockSpec(memory_space=pl.ANY)] * len(held),
        out_specs=block,
        out_shape=jax.ShapeDtypeStruct(denc.shape, bf16),
        input_output_aliases={4: 0} if held else {},
        compiler_params=params(60),
        cost_estimate=cost(6e9 / parts, 8e6 / parts),
        name="input_backward",
    )(denc, w_in, dpre, dk, *held)


def owner_order(width):
    n_y, n_core, n_z, n_x = (lax.axis_size(a) for a in AXES)
    rows = width // (n_y * n_core * n_z * n_x)
    place = jnp.arange(width, dtype=jnp.int32)
    inner = place % rows
    place = place // rows
    z, place = place % n_z, place // n_z
    x, place = place % n_x, place // n_x
    y, d_core = place % n_y, place // n_y
    core = (lax.axis_index(AXES[1]) + d_core) % n_core
    y, x = (lax.axis_index(AXES[0]) + y) % n_y, (lax.axis_index(AXES[3]) + x) % n_x
    z = (lax.axis_index(AXES[2]) + z) % n_z
    source = (((y * n_core + core) * n_z + z) * n_x + x) * rows + inner
    return (source[:, None] == jnp.arange(width, dtype=jnp.int32)[None, :]).astype(bf16)


def return_orders(capacity):
    sizes = n_y, n_core, n_z, n_x = tuple(lax.axis_size(a) for a in AXES)
    slots = n_y * n_core * n_z * n_x * capacity
    place = jnp.arange(slots, dtype=jnp.int32)
    inner, block = place % capacity, place // capacity
    plane = n_y * n_x
    orders = []
    for sign, (d_core, d_z, d_plane) in (
        (1, (block // (plane * n_z), block // plane % n_z, block % plane)),
        (-1, (block % n_core, block // n_core % n_z, block // (n_core * n_z))),
    ):
        y, core, z, x = (
            (lax.axis_index(a) + sign * d + n) % n
            for a, d, n in zip(AXES, (d_plane // n_x, d_core, d_z, d_plane % n_x), sizes)
        )
        source = (((y * n_core + core) * n_z + z) * n_x + x) * capacity + inner
        orders.append((source[:, None] == place[None, :]).astype(bf16))
    return orders


def add_up(blocks):
    total = blocks[0].astype(f32)
    for block in blocks[1:]:
        total = total + block.astype(f32)
    return total


def core_stage(keep, send):
    return add_up(send_blocks([keep] + cut_rows(send, lax.axis_size(AXES[1]) - 1), AXES[1:2])).astype(bf16)


def send_blocks(blocks, axes):
    count = len(blocks)
    sizes = [lax.axis_size(a) for a in axes]
    parts = [blocks[0]]
    for d in range(1, count):
        pairs = []
        for c in range(count):
            there, stride, rest_c, rest_d = 0, 1, c, d
            for n in reversed(sizes):
                there += (rest_c + rest_d) % n * stride
                stride, rest_c, rest_d = stride * n, rest_c // n, rest_d // n
            pairs.append((c, there))
        parts.append(lax.ppermute(blocks[d], axes, pairs))
    return parts


def cut_rows(rows, count):
    step = rows.shape[0] // count
    return [rows[i * step : (i + 1) * step] for i in range(count)]


def local(histories, weight_in, weight_out, candidates, cotangent, owner_ids, hist_slot, lengths):
    devices = lax.axis_size(AXES)
    imp_rows, width = candidates.shape
    capacity = max(2, 2 * imp_rows // devices)
    slots = devices * capacity
    kept = width // lax.axis_size(AXES[1])
    after = lax.optimization_barrier

    n_y, n_core, n_z, n_x = (lax.axis_size(a) for a in AXES)
    core, line, plane = AXES[1:2], AXES[2:3], (AXES[0], AXES[3])
    send, pick = route(owner_ids, hist_slot, lengths, candidates, cotangent, devices, capacity)
    shaped = send.reshape(devices, capacity, send.shape[1])
    recv = lax.all_to_all(shaped, AXES, split_axis=0, concat_axis=0, tiled=True)
    recv = recv.reshape(slots, send.shape[1])
    perm = owner_order(width)
    leaving, arriving = return_orders(capacity)
    pick = dot_nn(arriving, pick).astype(bf16)
    enc, slope, slope_t, v, q, k, q_t, attn_t, grad, normed, nu, gi, xt, mt = layer_forward(
        histories, weight_in, weight_out, perm
    )
    state = (normed, nu, gi, v, k, q_t, attn_t, grad, slope, slope_t)
    d_query, d_enc, dpre, dk, keep, send = owner_backward(recv, enc, weight_out, state, mt, xt, kept)
    d_query = dot_nn(leaving, d_query).astype(bf16)
    rows = core_stage(keep, send)
    d_enc, rows, d_query = after((d_enc, rows, d_query))
    back = [cut_rows(b, n_z) for b in send_blocks(cut_rows(d_query, n_core), core)]
    back = [jnp.concatenate([b[d] for b in back], axis=0) for d in range(n_z)]
    d_inputs = input_backward(d_enc, weight_in, dpre, dk, 0, 2)
    back = send_blocks(back, line)
    parts = send_blocks(cut_rows(rows, n_y * n_x), plane)
    back, parts, d_inputs = after((back, parts, d_inputs))
    parts = send_blocks(cut_rows(add_up(parts).astype(bf16), n_z), line)
    parts, d_inputs = after((parts, d_inputs))
    d_inputs = input_backward(d_enc, weight_in, dpre, dk, 1, 2, d_inputs)
    back = [b.reshape(n_core, n_y * n_x, capacity, width) for b in back]
    back = [
        jnp.concatenate([b[:, i].reshape(n_core * capacity, width) for b in back], axis=0)
        for i in range(n_y * n_x)
    ]
    returned = jnp.concatenate(send_blocks(back, plane), axis=0)
    candidate_grad = lax.dot_general(
        pick, returned, (((0,), (0,)), ((), ())), preferred_element_type=f32
    ).astype(bf16)
    w_in_grad = add_up([p[:, width:] for p in parts])
    w_out_grad = add_up([p[:, :width] for p in parts])
    return d_inputs, candidate_grad, w_in_grad, w_out_grad


def solution(mesh):
    n_hash, n_dp = mesh.devices.shape
    fine = jax.sharding.Mesh(mesh.devices.reshape(n_hash // 2, 2, n_dp // 2, 2), AXES)
    return jax.shard_map(
        local,
        mesh=fine,
        in_specs=(
            P(AXES, None, None),
            P(),
            P(),
            P(AXES, None),
            P(AXES, None),
            P(AXES, None),
            P(AXES),
            P(AXES),
        ),
        out_specs=(
            P(AXES, None, None),
            P(AXES, None),
            P(AXES, None),
            P(AXES, None),
        ),
        check_vma=False,
    )
```

```python
import functools

import jax
import jax.numpy as jnp
from jax import lax
from jax.experimental import pallas as pl
from jax.experimental.pallas import tpu as pltpu
from jax.sharding import PartitionSpec as P

HEADS = 8
TILE = 128
META = 128
AXES = ("hash_hi", "core", "dp_hi", "dp_lo")
norm_eps = 1e-05
f32 = jnp.float32
bf16 = jnp.bfloat16
MIB = 1024 * 1024


def dot_nn(a, b):
    return lax.dot_general(a, b, (((1,), (0,)), ((), ())), preferred_element_type=f32)


def dot_nt(a, b):
    return lax.dot_general(a, b, (((1,), (1,)), ((), ())), preferred_element_type=f32)


def dot_tn(a, b):
    return lax.dot_general(a, b, (((0,), (0,)), ((), ())), preferred_element_type=f32)


def iota(shape, axis):
    return lax.broadcasted_iota(jnp.int32, shape, axis)


def silu_pair(half):
    t = jnp.tanh(half)
    u = 1.0 + t
    act = half * u
    return act, u + act * (1.0 - t)


def lane_masks(width, part):
    lane = iota((1, width), 1)
    return [((lane >= j * part) & (lane < (j + 1) * part)).astype(bf16) for j in range(width // part)]


def both_heads(pair, masks):
    return jnp.concatenate([pair * m for m in masks], axis=0)


def pick_lanes(stacked, head):
    rows = stacked.shape[0] // 2
    lane = iota((1, 2 * head), 1)
    return jnp.where(lane < head, stacked[:rows], stacked[rows:])


def params(mib):
    return pltpu.CompilerParams(dimension_semantics=("arbitrary",), vmem_limit_bytes=mib * MIB)


def whole(shape):
    return pl.BlockSpec(shape, lambda i: (0,) * len(shape))


def cost(flops, nbytes, trans=0):
    return pl.CostEstimate(flops=int(flops), bytes_accessed=int(nbytes), transcendentals=int(trans))


def route_kernel(devices, capacity, own_ref, slot_ref, len_ref, cand_ref, cot_ref, send_ref, pick_ref):
    rows, width = cand_ref.shape
    slots = devices * capacity
    own = own_ref[...]
    hot = (own == iota((devices, rows), 0)).astype(f32)
    before = (iota((rows, rows), 0) < iota((rows, rows), 1)).astype(f32).astype(bf16)
    earlier = dot_nn(hot.astype(bf16), before)
    position = jnp.sum(earlier * hot, axis=0, keepdims=True).astype(jnp.int32)
    target = own * capacity + position
    pick = (target == iota((slots, rows), 0)).astype(f32).astype(bf16)
    pick_ref[...] = pick
    send_ref[:, :width] = dot_nn(pick, cand_ref[...]).astype(bf16)
    send_ref[:, width : 2 * width] = dot_nn(pick, cot_ref[...]).astype(bf16)
    line = iota((META, rows), 0)
    meta = jnp.where(line == 0, slot_ref[...], jnp.where(line == 1, len_ref[...], 0))
    send_ref[:, 2 * width :] = dot_nt(pick, meta.astype(f32).astype(bf16)).astype(bf16)


def route(own, slot, length, cand, cot, devices, capacity):
    rows, width = cand.shape
    slots = devices * capacity
    line = whole((1, rows))
    return pl.pallas_call(
        functools.partial(route_kernel, devices, capacity),
        grid=(1,),
        in_specs=[line, line, line, whole(cand.shape), whole(cot.shape)],
        out_specs=[whole((slots, 2 * width + META)), whole((slots, rows))],
        out_shape=(
            jax.ShapeDtypeStruct((slots, 2 * width + META), bf16),
            jax.ShapeDtypeStruct((slots, rows), bf16),
        ),
        compiler_params=params(60),
        cost_estimate=cost(2e9, 4 * rows * width * 4),
        name="route",
    )(own.reshape(1, rows), slot.reshape(1, rows), length.reshape(1, rows), cand, cot)


def forward_kernel(
    x_ref, win_ref, wout_ref, perm_ref,
    enc_ref, slope_ref, slope_t_ref, v_ref, q_ref, k_ref, q_t_ref, attn_t_ref, grad_ref,
    normed_ref, nu_ref, gi_ref, xt_ref, mt_ref,
    gate_ref, mixed_ref, slope_u_ref,
):
    seq, width = x_ref.shape[1:]
    head = width // HEADS
    half_seq = seq // 2
    x = x_ref[0]
    for branch in range(4):
        cols = slice(branch * width, (branch + 1) * width)
        act, slope = silu_pair(0.5 * dot_nn(x, win_ref[:, cols]))
        if branch == 3:
            slope_t_ref[0] = jnp.transpose(0.5 * slope).astype(bf16)
        elif branch > 0:
            slope_ref[0, :, (branch - 1) * width : branch * width] = (0.5 * slope).astype(bf16)
        if branch == 0:
            gate_ref[...] = act
            slope_u_ref[...] = 0.5 * slope
        else:
            (v_ref, q_ref, k_ref)[branch - 1][0] = act.astype(bf16)
        if branch == 2:
            q_t_ref[0] = jnp.transpose(act).astype(bf16)
    masks = lane_masks(2 * head, head)
    scale = 0.5 * head**-0.5
    tri = iota((half_seq, half_seq), 0) >= iota((half_seq, half_seq), 1)
    zero = jnp.zeros((half_seq, half_seq), f32)
    for pair in range(HEADS // 2):
        cols = slice(pair * 2 * head, (pair + 1) * 2 * head)
        q_p = q_ref[0, :, cols] * jnp.asarray(scale, bf16)
        half = dot_nt(both_heads(q_p, masks), k_ref[0, :, cols])
        stack = []
        for j in range(2):
            h = 2 * pair + j
            top = silu_pair(half[j * seq : j * seq + half_seq, :half_seq])
            bot = silu_pair(half[j * seq + half_seq : (j + 1) * seq])
            full = []
            for a, b in zip(top, bot):
                a = jnp.concatenate([jnp.where(tri, a, 0.0), zero], axis=1)
                b = jnp.concatenate([b[:, :half_seq], jnp.where(tri, b[:, half_seq:], 0.0)], axis=1)
                full.append(jnp.concatenate([a, b], axis=0))
            stack.append(full[0].astype(bf16))
            attn_t_ref[0, h] = jnp.transpose(full[0]).astype(bf16)
            grad_ref[0, h] = full[1].astype(bf16)
        mixed = dot_nn(jnp.concatenate(stack, axis=0), v_ref[0, :, cols])
        mixed_ref[:, cols] = pick_lanes(mixed, head) * (1.0 / seq)
    mixed = mixed_ref[...]
    centred = mixed - jnp.mean(mixed, axis=1, keepdims=True)
    inv_std = lax.rsqrt(jnp.mean(centred * centred, axis=1, keepdims=True) + norm_eps)
    normed = centred * inv_std
    gate = gate_ref[...]
    merged = (normed * gate).astype(bf16)
    normed_ref[0] = normed.astype(bf16)
    nu_ref[0] = (normed * slope_u_ref[...]).astype(bf16)
    gi_ref[0] = (gate * inv_std).astype(bf16)
    enc_ref[0] = (x.astype(f32) + dot_nn(merged, wout_ref[...])).astype(bf16)
    perm = perm_ref[...]
    xt_ref[...] = dot_nt(perm, x).astype(bf16)
    mt_ref[...] = dot_nt(perm, merged).astype(bf16)


def layer_forward(x, w_in, w_out, perm):
    hist, seq, width = x.shape
    row = pl.BlockSpec((1, seq, width), lambda i: (i, 0, 0))
    wide = pl.BlockSpec((1, seq, 2 * width), lambda i: (i, 0, 0))
    column = pl.BlockSpec((1, width, seq), lambda i: (i, 0, 0))
    square = pl.BlockSpec((1, HEADS, seq, seq), lambda i: (i, 0, 0, 0))
    turned = pl.BlockSpec((width, seq), lambda i: (0, i))
    row_s = jax.ShapeDtypeStruct((hist, seq, width), bf16)
    column_s = jax.ShapeDtypeStruct((hist, width, seq), bf16)
    square_s = jax.ShapeDtypeStruct((hist, HEADS, seq, seq), bf16)
    turned_s = jax.ShapeDtypeStruct((width, hist * seq), bf16)
    return pl.pallas_call(
        forward_kernel,
        grid=(hist,),
        in_specs=[row, whole(w_in.shape), whole(w_out.shape), whole(perm.shape)],
        out_specs=[
            row, wide, column, row, row, row, column, square, square, row, row, row, turned, turned,
        ],
        out_shape=[
            row_s, jax.ShapeDtypeStruct((hist, seq, 2 * width), bf16), column_s, row_s, row_s, row_s,
            column_s, square_s, square_s, row_s, row_s, row_s, turned_s, turned_s,
        ],
        scratch_shapes=[pltpu.VMEM((seq, width), f32)] * 3,
        compiler_params=params(60),
        cost_estimate=cost(18e9, 24e6),
        name="forward",
    )(x, w_in, w_out, perm)


def group_slots(recv_ref, hist):
    slots, width = recv_ref.shape
    meta = recv_ref[:, width - META :].astype(f32)
    slot_h = meta[:, 0:1]
    valid = meta[:, 1:2] > 0.0
    lane = iota((slots, META), 1).astype(f32)
    hot = jnp.where(valid & (slot_h == lane), 1.0, 0.0)
    lower = (iota((slots, slots), 0) > iota((slots, slots), 1)).astype(f32).astype(bf16)
    rank = jnp.sum(dot_nn(lower, hot.astype(bf16)) * hot, axis=1, keepdims=True)
    starts, start = [], jnp.int32(0)
    begin = jnp.zeros((slots, 1), f32)
    for h in range(hist):
        starts.append(start)
        begin = jnp.where(slot_h == float(h), (start * TILE).astype(f32), begin)
        count = jnp.sum(hot[:, h : h + 1]).astype(jnp.int32)
        start = start + (count + (TILE - 1)) // TILE
    dest = jnp.where(valid, begin + rank, -1.0)
    eye = iota((slots, slots), 0) == iota((slots, slots), 1)
    dest_row = jnp.sum(jnp.where(eye, dest, 0.0), axis=0, keepdims=True).astype(jnp.int32)
    return dest.astype(jnp.int32), dest_row, starts, start


def target_tile(tile, starts, dest_row, recv_ref, enc_ref, grouped_ref, turned_ref):
    seq, width = enc_ref.shape[1:]
    head = width // HEADS
    masks = lane_masks(2 * head, head)
    scale = 0.5 * head**-0.5
    base = pl.multiple_of(tile * TILE, TILE)
    hist = jnp.int32(0)
    for start in starts[1:]:
        hist = hist + (tile >= start).astype(jnp.int32)
    choose = (iota((TILE, dest_row.shape[1]), 0) + base == dest_row).astype(f32).astype(bf16)
    rows = dot_nn(choose, recv_ref[...])
    q_all = rows[:, :width] * scale
    g_all = rows[:, width : 2 * width]
    q_t = jnp.transpose(q_all).astype(bf16)
    g_t = jnp.transpose(g_all).astype(bf16)
    q_all = q_all.astype(bf16)
    g_all = g_all.astype(bf16)
    length = rows[:, 2 * width + 1 : 2 * width + 2]
    positions = iota((TILE, seq), 1).astype(f32)
    weight = jnp.where(positions < length, 1.0 / jnp.maximum(length, 1.0), 0.0)
    for pair in range(HEADS // 2):
        cols = slice(pair * 2 * head, (pair + 1) * 2 * head)
        k_p = enc_ref[hist, :, cols]
        both = dot_nt(
            jnp.concatenate(
                [both_heads(q_all[:, cols], masks), both_heads(g_all[:, cols], masks)], axis=0
            ),
            k_p,
        )
        slopes = []
        for j in range(2):
            h = 2 * pair + j
            mine = slice(h * head, (h + 1) * head)
            act, slope = silu_pair(both[j * TILE : (j + 1) * TILE])
            d_attn = both[(2 + j) * TILE : (3 + j) * TILE]
            attn = (act * weight).astype(bf16)
            d_s = (d_attn * weight * slope).astype(bf16)
            turned_ref[hist, mine, :] += dot_nn(
                jnp.concatenate([g_t[mine], q_t[mine]], axis=1),
                jnp.concatenate([attn, d_s], axis=0),
            )
            slopes.append(d_s)
        d_q = pick_lanes(dot_nn(jnp.concatenate(slopes, axis=0), k_p), head)
        grouped_ref[pl.ds(base, TILE), cols] = (d_q * scale).astype(bf16)


def norm_backward(denc_ref, wout_ref, normed_ref, nu_ref, gi_ref, dmix_ref, dpre_ref):
    hist, seq, width = denc_ref.shape
    for at in range(hist):
        here = slice(at * seq, (at + 1) * seq)
        d_merged = dot_nt(denc_ref[at], wout_ref[...])
        dpre_ref[here, :width] = (d_merged * nu_ref[at].astype(f32)).astype(bf16)
        normed = normed_ref[at].astype(f32)
        d_norm = d_merged * gi_ref[at].astype(f32)
        d_mix = (
            d_norm
            - jnp.mean(d_norm, axis=1, keepdims=True)
            - normed * jnp.mean(d_norm * normed, axis=1, keepdims=True)
        )
        dmix_ref[at] = d_mix.astype(bf16)


def attention_backward(
    at, dmix_ref, v_ref, k_ref, q_t_ref, attn_t_ref, grad_ref, slope_ref, slope_t_ref, dpre_ref, dk_ref
):
    seq, width = dmix_ref.shape[1:]
    head = width // HEADS
    here = slice(at * seq, (at + 1) * seq)
    masks = lane_masks(2 * head, head)
    scale = 0.5 * head**-0.5 / seq
    for pair in range(HEADS // 2):
        cols = slice(pair * 2 * head, (pair + 1) * 2 * head)
        d_p = dmix_ref[at, :, cols]
        d_attn = dot_nt(both_heads(d_p, masks), v_ref[at, :, cols])
        d_s = [
            (d_attn[j * seq : (j + 1) * seq] * grad_ref[at, 2 * pair + j].astype(f32)).astype(bf16)
            for j in range(2)
        ]
        attn_t = jnp.concatenate([attn_t_ref[at, 2 * pair], attn_t_ref[at, 2 * pair + 1]], axis=0)
        d_v = pick_lanes(dot_nn(attn_t, d_p), head) * (1.0 / seq)
        d_q = pick_lanes(dot_nn(jnp.concatenate(d_s, axis=0), k_ref[at, :, cols]), head) * scale
        for branch, grad in ((0, d_v), (1, d_q)):
            old = slice(branch * width + pair * 2 * head, branch * width + (pair + 1) * 2 * head)
            new = slice(old.start + width, old.stop + width)
            dpre_ref[here, new] = (grad * slope_ref[at, :, old].astype(f32)).astype(bf16)
        for j in range(2):
            mine = slice((2 * pair + j) * head, (2 * pair + j + 1) * head)
            d_k = dot_nn(q_t_ref[at, mine], d_s[j]) * scale
            dk_ref[mine, here] = (d_k * slope_t_ref[at, mine].astype(f32)).astype(bf16)


def owner_kernel(*refs):
    n_in, n_out = 15, 6
    sources, outs, refs = refs[:n_in], refs[n_in : n_in + n_out], refs[n_in + n_out :]
    held, refs = refs[:n_in], refs[n_in:]
    (
        recv_ref, enc_ref, wout_ref, normed_ref, nu_ref, gi_ref, v_ref, k_ref, q_t_ref,
        attn_t_ref, grad_ref, slope_ref, slope_t_ref, mt_ref, xt_ref,
    ) = held
    grouped_ref, turned_ref, dmix_ref, dq_ref, denc_ref, dpre_ref, dk_ref, keep_ref, send_ref, sem_in, sem_out = refs
    dq_hbm, denc_hbm, dpre_hbm, dk_hbm, keep_hbm, send_hbm = outs
    hist, seq, width = enc_ref.shape
    slots, padded = recv_ref.shape[0], grouped_ref.shape[0]
    kept = keep_ref.shape[0]

    def load(i, n, at=None):
        source, dest = (sources[i], held[i]) if at is None else (sources[i].at[at], held[i].at[at])
        return pltpu.make_async_copy(source, dest, sem_in.at[n])

    first = [load(i, i) for i in range(6)]
    by_history = [[load(i, i + 7 * at, at) for i in range(6, 13)] for at in range(hist)]
    last = [load(i, 7 * hist + i - 7) for i in (13, 14)]
    for copy in first + sum(by_history, []) + last:
        copy.start()
    grouped_ref[...] = jnp.zeros_like(grouped_ref)
    turned_ref[...] = jnp.zeros_like(turned_ref)
    first[0].wait()
    dest, dest_row, starts, tiles = group_slots(recv_ref, hist)
    first[1].wait()

    def one_tile(tile, carry):
        target_tile(tile, starts, dest_row, recv_ref, enc_ref, grouped_ref, turned_ref)
        return carry

    lax.fori_loop(0, tiles, one_tile, 0)
    for h in range(hist):
        denc_ref[h] = jnp.transpose(turned_ref[h]).astype(bf16)
    back = (dest == iota((slots, padded), 1)).astype(f32).astype(bf16)
    dq_ref[...] = dot_nn(back, grouped_ref[...]).astype(bf16)
    stores = []

    def store(source, dest):
        copy = pltpu.make_async_copy(source, dest, sem_out.at[len(stores)])
        copy.start()
        stores.append(copy)

    store(denc_ref, denc_hbm)
    store(dq_ref, dq_hbm)
    for copy in first[2:]:
        copy.wait()
    norm_backward(denc_ref, wout_ref, normed_ref, nu_ref, gi_ref, dmix_ref, dpre_ref)
    for at in range(hist):
        for copy in by_history[at]:
            copy.wait()
        attention_backward(
            at, dmix_ref, v_ref, k_ref, q_t_ref, attn_t_ref, grad_ref, slope_ref, slope_t_ref,
            dpre_ref, dk_ref,
        )
        here = pl.ds(at * seq, seq)
        store(dpre_ref.at[here, :], dpre_hbm.at[here, :])
        store(dk_ref.at[:, here], dk_hbm.at[:, here])
    for copy in last:
        copy.wait()
    for block in range(5):
        cols = slice(block * width, (block + 1) * width)
        if block == 0:
            part = dot_nn(mt_ref[...], denc_ref[...].reshape(hist * seq, width))
        elif block == 4:
            part = dot_nt(xt_ref[...], dk_ref[...])
        else:
            part = dot_nn(xt_ref[...], dpre_ref[:, (block - 1) * width : block * width])
        keep_ref[:, cols] = part[:kept].astype(bf16)
        send_ref[:, cols] = part[kept:].astype(bf16)
        store(keep_ref.at[:, cols], keep_hbm.at[:, cols])
        store(send_ref.at[:, cols], send_hbm.at[:, cols])
    for copy in stores:
        copy.wait()


def owner_backward(recv, enc, w_out, state, mt, xt, kept):
    hist, seq, width = enc.shape
    slots = recv.shape[0]
    rows = hist * seq
    padded = ((slots - hist) // TILE + hist) * TILE
    operands = (recv, enc, w_out) + state + (mt, xt)
    raw = pl.BlockSpec(memory_space=pl.ANY)
    outs = [
        jax.ShapeDtypeStruct((slots, width), bf16),
        jax.ShapeDtypeStruct(enc.shape, bf16),
        jax.ShapeDtypeStruct((rows, 3 * width), bf16),
        jax.ShapeDtypeStruct((width, rows), bf16),
        jax.ShapeDtypeStruct((kept, 5 * width), bf16),
        jax.ShapeDtypeStruct((width - kept, 5 * width), bf16),
    ]
    return pl.pallas_call(
        owner_kernel,
        grid=(1,),
        in_specs=[pl.BlockSpec(memory_space=pltpu.HBM)] + [raw] * (len(operands) - 1),
        out_specs=[raw] * len(outs),
        out_shape=outs,
        scratch_shapes=[pltpu.VMEM(a.shape, a.dtype) for a in operands]
        + [
            pltpu.VMEM((padded, width), bf16),
            pltpu.VMEM((hist, width, seq), f32),
            pltpu.VMEM((hist, seq, width), bf16),
        ]
        + [pltpu.VMEM(a.shape, a.dtype) for a in outs]
        + [
            pltpu.SemaphoreType.DMA((7 * hist + 8,)),
            pltpu.SemaphoreType.DMA((2 * hist + 12,)),
        ],
        compiler_params=params(60),
        cost_estimate=cost(30e9, 30e6),
        name="owner_backward",
    )(*operands)


def input_kernel(denc_ref, win_ref, dpre_ref, dk_ref, out_ref):
    width = denc_ref.shape[2]
    total = denc_ref[0].astype(f32) + dot_nt(dpre_ref[...], win_ref[:, : 3 * width])
    total = total + dot_nt(jnp.transpose(dk_ref[...]), win_ref[:, 3 * width :])
    out_ref[0] = total.astype(bf16)


def input_backward(denc, w_in, dpre, dk):
    hist, seq, width = denc.shape
    block = lambda a: pl.BlockSpec((1,) + a.shape[1:], lambda i: (i, 0, 0))
    return pl.pallas_call(
        input_kernel,
        grid=(hist,),
        in_specs=[
            block(denc),
            whole(w_in.shape),
            pl.BlockSpec((seq, 3 * width), lambda i: (i, 0)),
            pl.BlockSpec((width, seq), lambda i: (0, i)),
        ],
        out_specs=block(denc),
        out_shape=jax.ShapeDtypeStruct(denc.shape, bf16),
        compiler_params=params(60),
        cost_estimate=cost(6e9, 8e6),
        name="input_backward",
    )(denc, w_in, dpre, dk)


def owner_order(width):
    n_y, n_core, n_z, n_x = (lax.axis_size(a) for a in AXES)
    rows = width // (n_y * n_core * n_z * n_x)
    place = jnp.arange(width, dtype=jnp.int32)
    inner = place % rows
    place = place // rows
    z, place = place % n_z, place // n_z
    x, place = place % n_x, place // n_x
    y, d_core = place % n_y, place // n_y
    core = (lax.axis_index(AXES[1]) + d_core) % n_core
    y, x = (lax.axis_index(AXES[0]) + y) % n_y, (lax.axis_index(AXES[3]) + x) % n_x
    z = (lax.axis_index(AXES[2]) + z) % n_z
    source = (((y * n_core + core) * n_z + z) * n_x + x) * rows + inner
    return (source[:, None] == jnp.arange(width, dtype=jnp.int32)[None, :]).astype(bf16)


def return_orders(capacity):
    sizes = n_y, n_core, n_z, n_x = tuple(lax.axis_size(a) for a in AXES)
    slots = n_y * n_core * n_z * n_x * capacity
    place = jnp.arange(slots, dtype=jnp.int32)
    inner, block = place % capacity, place // capacity
    plane = n_y * n_x
    orders = []
    for sign, (d_core, d_z, d_plane) in (
        (1, (block // (plane * n_z), block // plane % n_z, block % plane)),
        (-1, (block % n_core, block // n_core % n_z, block // (n_core * n_z))),
    ):
        y, core, z, x = (
            (lax.axis_index(a) + sign * d + n) % n
            for a, d, n in zip(AXES, (d_plane // n_x, d_core, d_z, d_plane % n_x), sizes)
        )
        source = (((y * n_core + core) * n_z + z) * n_x + x) * capacity + inner
        orders.append((source[:, None] == place[None, :]).astype(bf16))
    return orders


def add_up(blocks):
    total = blocks[0].astype(f32)
    for block in blocks[1:]:
        total = total + block.astype(f32)
    return total


def core_stage(keep, send):
    return add_up(send_blocks([keep] + cut_rows(send, lax.axis_size(AXES[1]) - 1), AXES[1:2])).astype(bf16)


def send_blocks(blocks, axes):
    count = len(blocks)
    sizes = [lax.axis_size(a) for a in axes]
    parts = [blocks[0]]
    for d in range(1, count):
        pairs = []
        for c in range(count):
            there, stride, rest_c, rest_d = 0, 1, c, d
            for n in reversed(sizes):
                there += (rest_c + rest_d) % n * stride
                stride, rest_c, rest_d = stride * n, rest_c // n, rest_d // n
            pairs.append((c, there))
        parts.append(lax.ppermute(blocks[d], axes, pairs))
    return parts


def cut_rows(rows, count):
    step = rows.shape[0] // count
    return [rows[i * step : (i + 1) * step] for i in range(count)]


def local(histories, weight_in, weight_out, candidates, cotangent, owner_ids, hist_slot, lengths):
    devices = lax.axis_size(AXES)
    imp_rows, width = candidates.shape
    capacity = max(2, 2 * imp_rows // devices)
    slots = devices * capacity
    kept = width // lax.axis_size(AXES[1])
    after = lax.optimization_barrier

    n_y, n_core, n_z, n_x = (lax.axis_size(a) for a in AXES)
    core, line, plane = AXES[1:2], AXES[2:3], (AXES[0], AXES[3])
    send, pick = route(owner_ids, hist_slot, lengths, candidates, cotangent, devices, capacity)
    shaped = send.reshape(devices, capacity, send.shape[1])
    recv = lax.all_to_all(shaped, AXES, split_axis=0, concat_axis=0, tiled=True)
    recv = recv.reshape(slots, send.shape[1])
    perm = owner_order(width)
    leaving, arriving = return_orders(capacity)
    pick = dot_nn(arriving, pick).astype(bf16)
    enc, slope, slope_t, v, q, k, q_t, attn_t, grad, normed, nu, gi, xt, mt = layer_forward(
        histories, weight_in, weight_out, perm
    )
    state = (normed, nu, gi, v, k, q_t, attn_t, grad, slope, slope_t)
    d_query, d_enc, dpre, dk, keep, send = owner_backward(recv, enc, weight_out, state, mt, xt, kept)
    d_query = dot_nn(leaving, d_query).astype(bf16)
    rows = core_stage(keep, send)
    d_enc, rows, d_query = after((d_enc, rows, d_query))
    back = [cut_rows(b, n_z) for b in send_blocks(cut_rows(d_query, n_core), core)]
    back = [jnp.concatenate([b[d] for b in back], axis=0) for d in range(n_z)]
    d_inputs = input_backward(d_enc, weight_in, dpre, dk)
    back = send_blocks(back, line)
    parts = send_blocks(cut_rows(rows, n_y * n_x), plane)
    back, parts, d_inputs = after((back, parts, d_inputs))
    parts = send_blocks(cut_rows(add_up(parts).astype(bf16), n_z), line)
    back = [b.reshape(n_core, n_y * n_x, capacity, width) for b in back]
    back = [
        jnp.concatenate([b[:, i].reshape(n_core * capacity, width) for b in back], axis=0)
        for i in range(n_y * n_x)
    ]
    picks = cut_rows(pick, n_y * n_x)
    candidate_grad = sum(dot_tn(p, b) for p, b in zip(picks, send_blocks(back, plane))).astype(bf16)
    w_in_grad = add_up([p[:, width:] for p in parts])
    w_out_grad = add_up([p[:, :width] for p in parts])
    return d_inputs, candidate_grad, w_in_grad, w_out_grad


def solution(mesh):
    n_hash, n_dp = mesh.devices.shape
    fine = jax.sharding.Mesh(mesh.devices.reshape(n_hash // 2, 2, n_dp // 2, 2), AXES)
    return jax.shard_map(
        local,
        mesh=fine,
        in_specs=(
            P(AXES, None, None),
            P(),
            P(),
            P(AXES, None),
            P(AXES, None),
            P(AXES, None),
            P(AXES),
            P(AXES),
        ),
        out_specs=(
            P(AXES, None, None),
            P(AXES, None),
            P(AXES, None),
            P(AXES, None),
        ),
        check_vma=False,
    )
```

```python
import functools

import jax
import jax.numpy as jnp
from jax import lax
from jax.experimental import pallas as pl
from jax.experimental.pallas import tpu as pltpu
from jax.sharding import PartitionSpec as P

HEADS = 8
TILE = 128
META = 128
AXES = ("hash_hi", "core", "dp_hi", "dp_lo")
norm_eps = 1e-05
f32 = jnp.float32
bf16 = jnp.bfloat16
MIB = 1024 * 1024


def dot_nn(a, b):
    return lax.dot_general(a, b, (((1,), (0,)), ((), ())), preferred_element_type=f32)


def dot_nt(a, b):
    return lax.dot_general(a, b, (((1,), (1,)), ((), ())), preferred_element_type=f32)


def dot_tn(a, b):
    return lax.dot_general(a, b, (((0,), (0,)), ((), ())), preferred_element_type=f32)


def iota(shape, axis):
    return lax.broadcasted_iota(jnp.int32, shape, axis)


def silu_pair(half):
    t = jnp.tanh(half)
    u = 1.0 + t
    act = half * u
    return act, u + act * (1.0 - t)


def lane_masks(width, part):
    lane = iota((1, width), 1)
    return [((lane >= j * part) & (lane < (j + 1) * part)).astype(bf16) for j in range(width // part)]


def both_heads(pair, masks):
    return jnp.concatenate([pair * m for m in masks], axis=0)


def pick_lanes(stacked, head):
    rows = stacked.shape[0] // 2
    lane = iota((1, 2 * head), 1)
    return jnp.where(lane < head, stacked[:rows], stacked[rows:])


def params(mib):
    return pltpu.CompilerParams(dimension_semantics=("arbitrary",), vmem_limit_bytes=mib * MIB)


def whole(shape):
    return pl.BlockSpec(shape, lambda i: (0,) * len(shape))


def cost(flops, nbytes, trans=0):
    return pl.CostEstimate(flops=int(flops), bytes_accessed=int(nbytes), transcendentals=int(trans))


def route_kernel(devices, capacity, own_ref, slot_ref, len_ref, cand_ref, cot_ref, send_ref, pick_ref):
    rows, width = cand_ref.shape
    slots = devices * capacity
    own = own_ref[...]
    hot = (own == iota((devices, rows), 0)).astype(f32)
    before = (iota((rows, rows), 0) < iota((rows, rows), 1)).astype(f32).astype(bf16)
    earlier = dot_nn(hot.astype(bf16), before)
    position = jnp.sum(earlier * hot, axis=0, keepdims=True).astype(jnp.int32)
    target = own * capacity + position
    pick = (target == iota((slots, rows), 0)).astype(f32).astype(bf16)
    pick_ref[...] = pick
    send_ref[:, :width] = dot_nn(pick, cand_ref[...]).astype(bf16)
    send_ref[:, width : 2 * width] = dot_nn(pick, cot_ref[...]).astype(bf16)
    line = iota((META, rows), 0)
    meta = jnp.where(line == 0, slot_ref[...], jnp.where(line == 1, len_ref[...], 0))
    send_ref[:, 2 * width :] = dot_nt(pick, meta.astype(f32).astype(bf16)).astype(bf16)


def route(own, slot, length, cand, cot, devices, capacity):
    rows, width = cand.shape
    slots = devices * capacity
    line = whole((1, rows))
    return pl.pallas_call(
        functools.partial(route_kernel, devices, capacity),
        grid=(1,),
        in_specs=[line, line, line, whole(cand.shape), whole(cot.shape)],
        out_specs=[whole((slots, 2 * width + META)), whole((slots, rows))],
        out_shape=(
            jax.ShapeDtypeStruct((slots, 2 * width + META), bf16),
            jax.ShapeDtypeStruct((slots, rows), bf16),
        ),
        compiler_params=params(60),
        cost_estimate=cost(2e9, 4 * rows * width * 4),
        name="route",
    )(own.reshape(1, rows), slot.reshape(1, rows), length.reshape(1, rows), cand, cot)


def forward_kernel(
    x_ref, win_ref, wout_ref, perm_ref,
    enc_ref, slope_ref, slope_t_ref, v_ref, q_ref, k_ref, q_t_ref, attn_t_ref, grad_ref,
    normed_ref, nu_ref, gi_ref, xt_ref, mt_ref,
    gate_ref, mixed_ref, slope_u_ref,
):
    seq, width = x_ref.shape[1:]
    head = width // HEADS
    half_seq = seq // 2
    x = x_ref[0]
    for branch in range(4):
        cols = slice(branch * width, (branch + 1) * width)
        act, slope = silu_pair(0.5 * dot_nn(x, win_ref[:, cols]))
        if branch == 3:
            slope_t_ref[0] = jnp.transpose(0.5 * slope).astype(bf16)
        elif branch > 0:
            slope_ref[0, :, (branch - 1) * width : branch * width] = (0.5 * slope).astype(bf16)
        if branch == 0:
            gate_ref[...] = act
            slope_u_ref[...] = 0.5 * slope
        else:
            (v_ref, q_ref, k_ref)[branch - 1][0] = act.astype(bf16)
        if branch == 2:
            q_t_ref[0] = jnp.transpose(act).astype(bf16)
    masks = lane_masks(2 * head, head)
    scale = 0.5 * head**-0.5
    tri = iota((half_seq, half_seq), 0) >= iota((half_seq, half_seq), 1)
    zero = jnp.zeros((half_seq, half_seq), f32)
    for pair in range(HEADS // 2):
        cols = slice(pair * 2 * head, (pair + 1) * 2 * head)
        q_p = q_ref[0, :, cols] * jnp.asarray(scale, bf16)
        half = dot_nt(both_heads(q_p, masks), k_ref[0, :, cols])
        stack = []
        for j in range(2):
            h = 2 * pair + j
            top = silu_pair(half[j * seq : j * seq + half_seq, :half_seq])
            bot = silu_pair(half[j * seq + half_seq : (j + 1) * seq])
            full = []
            for a, b in zip(top, bot):
                a = jnp.concatenate([jnp.where(tri, a, 0.0), zero], axis=1)
                b = jnp.concatenate([b[:, :half_seq], jnp.where(tri, b[:, half_seq:], 0.0)], axis=1)
                full.append(jnp.concatenate([a, b], axis=0))
            stack.append(full[0].astype(bf16))
            attn_t_ref[0, h] = jnp.transpose(full[0]).astype(bf16)
            grad_ref[0, h] = full[1].astype(bf16)
        mixed = dot_nn(jnp.concatenate(stack, axis=0), v_ref[0, :, cols])
        mixed_ref[:, cols] = pick_lanes(mixed, head) * (1.0 / seq)
    mixed = mixed_ref[...]
    centred = mixed - jnp.mean(mixed, axis=1, keepdims=True)
    inv_std = lax.rsqrt(jnp.mean(centred * centred, axis=1, keepdims=True) + norm_eps)
    normed = centred * inv_std
    gate = gate_ref[...]
    merged = (normed * gate).astype(bf16)
    normed_ref[0] = normed.astype(bf16)
    nu_ref[0] = (normed * slope_u_ref[...]).astype(bf16)
    gi_ref[0] = (gate * inv_std).astype(bf16)
    enc_ref[0] = (x.astype(f32) + dot_nn(merged, wout_ref[...])).astype(bf16)
    perm = perm_ref[...]
    xt_ref[...] = dot_nt(perm, x).astype(bf16)
    mt_ref[...] = dot_nt(perm, merged).astype(bf16)


def layer_forward(x, w_in, w_out, perm):
    hist, seq, width = x.shape
    row = pl.BlockSpec((1, seq, width), lambda i: (i, 0, 0))
    wide = pl.BlockSpec((1, seq, 2 * width), lambda i: (i, 0, 0))
    column = pl.BlockSpec((1, width, seq), lambda i: (i, 0, 0))
    square = pl.BlockSpec((1, HEADS, seq, seq), lambda i: (i, 0, 0, 0))
    turned = pl.BlockSpec((width, seq), lambda i: (0, i))
    row_s = jax.ShapeDtypeStruct((hist, seq, width), bf16)
    column_s = jax.ShapeDtypeStruct((hist, width, seq), bf16)
    square_s = jax.ShapeDtypeStruct((hist, HEADS, seq, seq), bf16)
    turned_s = jax.ShapeDtypeStruct((width, hist * seq), bf16)
    return pl.pallas_call(
        forward_kernel,
        grid=(hist,),
        in_specs=[row, whole(w_in.shape), whole(w_out.shape), whole(perm.shape)],
        out_specs=[
            row, wide, column, row, row, row, column, square, square, row, row, row, turned, turned,
        ],
        out_shape=[
            row_s, jax.ShapeDtypeStruct((hist, seq, 2 * width), bf16), column_s, row_s, row_s, row_s,
            column_s, square_s, square_s, row_s, row_s, row_s, turned_s, turned_s,
        ],
        scratch_shapes=[pltpu.VMEM((seq, width), f32)] * 3,
        compiler_params=params(60),
        cost_estimate=cost(18e9, 24e6),
        name="forward",
    )(x, w_in, w_out, perm)


def group_slots(recv_ref, hist):
    slots, width = recv_ref.shape
    meta = recv_ref[:, width - META :].astype(f32)
    slot_h = meta[:, 0:1]
    valid = meta[:, 1:2] > 0.0
    lane = iota((slots, META), 1).astype(f32)
    hot = jnp.where(valid & (slot_h == lane), 1.0, 0.0)
    lower = (iota((slots, slots), 0) > iota((slots, slots), 1)).astype(f32).astype(bf16)
    rank = jnp.sum(dot_nn(lower, hot.astype(bf16)) * hot, axis=1, keepdims=True)
    starts, start = [], jnp.int32(0)
    begin = jnp.zeros((slots, 1), f32)
    for h in range(hist):
        starts.append(start)
        begin = jnp.where(slot_h == float(h), (start * TILE).astype(f32), begin)
        count = jnp.sum(hot[:, h : h + 1]).astype(jnp.int32)
        start = start + (count + (TILE - 1)) // TILE
    dest = jnp.where(valid, begin + rank, -1.0)
    eye = iota((slots, slots), 0) == iota((slots, slots), 1)
    dest_row = jnp.sum(jnp.where(eye, dest, 0.0), axis=0, keepdims=True).astype(jnp.int32)
    return dest.astype(jnp.int32), dest_row, starts, start


def target_tile(tile, starts, dest_row, recv_ref, enc_ref, grouped_ref, turned_ref):
    seq, width = enc_ref.shape[1:]
    head = width // HEADS
    masks = lane_masks(2 * head, head)
    scale = 0.5 * head**-0.5
    base = pl.multiple_of(tile * TILE, TILE)
    hist = jnp.int32(0)
    for start in starts[1:]:
        hist = hist + (tile >= start).astype(jnp.int32)
    choose = (iota((TILE, dest_row.shape[1]), 0) + base == dest_row).astype(f32).astype(bf16)
    rows = dot_nn(choose, recv_ref[...])
    q_all = rows[:, :width] * scale
    g_all = rows[:, width : 2 * width]
    q_t = jnp.transpose(q_all).astype(bf16)
    g_t = jnp.transpose(g_all).astype(bf16)
    q_all = q_all.astype(bf16)
    g_all = g_all.astype(bf16)
    length = rows[:, 2 * width + 1 : 2 * width + 2]
    positions = iota((TILE, seq), 1).astype(f32)
    weight = jnp.where(positions < length, 1.0 / jnp.maximum(length, 1.0), 0.0)
    for pair in range(HEADS // 2):
        cols = slice(pair * 2 * head, (pair + 1) * 2 * head)
        k_p = enc_ref[hist, :, cols]
        both = dot_nt(
            jnp.concatenate(
                [both_heads(q_all[:, cols], masks), both_heads(g_all[:, cols], masks)], axis=0
            ),
            k_p,
        )
        slopes = []
        for j in range(2):
            h = 2 * pair + j
            mine = slice(h * head, (h + 1) * head)
            act, slope = silu_pair(both[j * TILE : (j + 1) * TILE])
            d_attn = both[(2 + j) * TILE : (3 + j) * TILE]
            attn = (act * weight).astype(bf16)
            d_s = (d_attn * weight * slope).astype(bf16)
            turned_ref[hist, mine, :] += dot_nn(
                jnp.concatenate([g_t[mine], q_t[mine]], axis=1),
                jnp.concatenate([attn, d_s], axis=0),
            )
            slopes.append(d_s)
        d_q = pick_lanes(dot_nn(jnp.concatenate(slopes, axis=0), k_p), head)
        grouped_ref[pl.ds(base, TILE), cols] = (d_q * scale).astype(bf16)


def norm_backward(denc_ref, wout_ref, normed_ref, nu_ref, gi_ref, dmix_ref, dpre_ref):
    hist, seq, width = denc_ref.shape
    d_merged_all = dot_nt(denc_ref[...].reshape(hist * seq, width), wout_ref[...])
    for at in range(hist):
        here = slice(at * seq, (at + 1) * seq)
        d_merged = d_merged_all[here]
        dpre_ref[here, :width] = (d_merged * nu_ref[at].astype(f32)).astype(bf16)
        normed = normed_ref[at].astype(f32)
        d_norm = d_merged * gi_ref[at].astype(f32)
        d_mix = (
            d_norm
            - jnp.mean(d_norm, axis=1, keepdims=True)
            - normed * jnp.mean(d_norm * normed, axis=1, keepdims=True)
        )
        dmix_ref[at] = d_mix.astype(bf16)


def attention_backward(
    at, dmix_ref, v_ref, k_ref, q_t_ref, attn_t_ref, grad_ref, slope_ref, slope_t_ref, dpre_ref, dk_ref
):
    seq, width = dmix_ref.shape[1:]
    head = width // HEADS
    half_seq = seq // 2
    zero = jnp.zeros((half_seq, half_seq), bf16)
    here = slice(at * seq, (at + 1) * seq)
    masks = lane_masks(2 * head, head)
    scale = 0.5 * head**-0.5 / seq
    for pair in range(HEADS // 2):
        cols = slice(pair * 2 * head, (pair + 1) * 2 * head)
        d_p = dmix_ref[at, :, cols]
        v_p = v_ref[at, :, cols]
        top = dot_nt(both_heads(d_p[:half_seq], masks), v_p[:half_seq])
        bot = dot_nt(both_heads(d_p[half_seq:], masks), v_p)
        d_s = []
        for j in range(2):
            part = slice(j * half_seq, (j + 1) * half_seq)
            grad = grad_ref[at, 2 * pair + j]
            d_top = (top[part] * grad[:half_seq, :half_seq].astype(f32)).astype(bf16)
            d_bot = (bot[part] * grad[half_seq:].astype(f32)).astype(bf16)
            d_s.append(jnp.concatenate([jnp.concatenate([d_top, zero], axis=1), d_bot], axis=0))
        attn_t = jnp.concatenate([attn_t_ref[at, 2 * pair], attn_t_ref[at, 2 * pair + 1]], axis=0)
        d_v = pick_lanes(dot_nn(attn_t, d_p), head) * (1.0 / seq)
        d_q = pick_lanes(dot_nn(jnp.concatenate(d_s, axis=0), k_ref[at, :, cols]), head) * scale
        for branch, grad in ((0, d_v), (1, d_q)):
            old = slice(branch * width + pair * 2 * head, branch * width + (pair + 1) * 2 * head)
            new = slice(old.start + width, old.stop + width)
            dpre_ref[here, new] = (grad * slope_ref[at, :, old].astype(f32)).astype(bf16)
        for j in range(2):
            mine = slice((2 * pair + j) * head, (2 * pair + j + 1) * head)
            d_k = dot_nn(q_t_ref[at, mine], d_s[j]) * scale
            dk_ref[mine, here] = (d_k * slope_t_ref[at, mine].astype(f32)).astype(bf16)


def owner_kernel(*refs):
    n_in, n_out = 15, 6
    sources, outs, refs = refs[:n_in], refs[n_in : n_in + n_out], refs[n_in + n_out :]
    held, refs = refs[:n_in], refs[n_in:]
    (
        recv_ref, enc_ref, wout_ref, normed_ref, nu_ref, gi_ref, v_ref, k_ref, q_t_ref,
        attn_t_ref, grad_ref, slope_ref, slope_t_ref, mt_ref, xt_ref,
    ) = held
    grouped_ref, turned_ref, dmix_ref, dq_ref, denc_ref, dpre_ref, dk_ref, keep_ref, send_ref, sem_in, sem_out = refs
    dq_hbm, denc_hbm, dpre_hbm, dk_hbm, keep_hbm, send_hbm = outs
    hist, seq, width = enc_ref.shape
    slots, padded = recv_ref.shape[0], grouped_ref.shape[0]
    kept = keep_ref.shape[0]

    def load(i, n, at=None):
        source, dest = (sources[i], held[i]) if at is None else (sources[i].at[at], held[i].at[at])
        return pltpu.make_async_copy(source, dest, sem_in.at[n])

    first = [load(i, i) for i in range(6)]
    by_history = [[load(i, i + 7 * at, at) for i in range(6, 13)] for at in range(hist)]
    last = [load(i, 7 * hist + i - 7) for i in (13, 14)]
    for copy in first + sum(by_history, []) + last:
        copy.start()
    grouped_ref[...] = jnp.zeros_like(grouped_ref)
    turned_ref[...] = jnp.zeros_like(turned_ref)
    first[0].wait()
    dest, dest_row, starts, tiles = group_slots(recv_ref, hist)
    first[1].wait()

    def one_tile(tile, carry):
        target_tile(tile, starts, dest_row, recv_ref, enc_ref, grouped_ref, turned_ref)
        return carry

    lax.fori_loop(0, tiles, one_tile, 0)
    for h in range(hist):
        denc_ref[h] = jnp.transpose(turned_ref[h]).astype(bf16)
    back = (dest == iota((slots, padded), 1)).astype(f32).astype(bf16)
    dq_ref[...] = dot_nn(back, grouped_ref[...]).astype(bf16)
    stores = []

    def store(source, dest):
        copy = pltpu.make_async_copy(source, dest, sem_out.at[len(stores)])
        copy.start()
        stores.append(copy)

    store(denc_ref, denc_hbm)
    store(dq_ref, dq_hbm)
    for copy in first[2:]:
        copy.wait()
    norm_backward(denc_ref, wout_ref, normed_ref, nu_ref, gi_ref, dmix_ref, dpre_ref)
    for at in range(hist):
        for copy in by_history[at]:
            copy.wait()
        attention_backward(
            at, dmix_ref, v_ref, k_ref, q_t_ref, attn_t_ref, grad_ref, slope_ref, slope_t_ref,
            dpre_ref, dk_ref,
        )
        here = pl.ds(at * seq, seq)
        store(dpre_ref.at[here, :], dpre_hbm.at[here, :])
        store(dk_ref.at[:, here], dk_hbm.at[:, here])
    for copy in last:
        copy.wait()
    for block in range(5):
        cols = slice(block * width, (block + 1) * width)
        if block == 0:
            part = dot_nn(mt_ref[...], denc_ref[...].reshape(hist * seq, width))
        elif block == 4:
            part = dot_nt(xt_ref[...], dk_ref[...])
        else:
            part = dot_nn(xt_ref[...], dpre_ref[:, (block - 1) * width : block * width])
        keep_ref[:, cols] = part[:kept].astype(bf16)
        send_ref[:, cols] = part[kept:].astype(bf16)
        store(keep_ref.at[:, cols], keep_hbm.at[:, cols])
        store(send_ref.at[:, cols], send_hbm.at[:, cols])
    for copy in stores:
        copy.wait()


def owner_backward(recv, enc, w_out, state, mt, xt, kept):
    hist, seq, width = enc.shape
    slots = recv.shape[0]
    rows = hist * seq
    padded = ((slots - hist) // TILE + hist) * TILE
    operands = (recv, enc, w_out) + state + (mt, xt)
    raw = pl.BlockSpec(memory_space=pl.ANY)
    outs = [
        jax.ShapeDtypeStruct((slots, width), bf16),
        jax.ShapeDtypeStruct(enc.shape, bf16),
        jax.ShapeDtypeStruct((rows, 3 * width), bf16),
        jax.ShapeDtypeStruct((width, rows), bf16),
        jax.ShapeDtypeStruct((kept, 5 * width), bf16),
        jax.ShapeDtypeStruct((width - kept, 5 * width), bf16),
    ]
    return pl.pallas_call(
        owner_kernel,
        grid=(1,),
        in_specs=[raw] * len(operands),
        out_specs=[raw] * len(outs),
        out_shape=outs,
        scratch_shapes=[pltpu.VMEM(a.shape, a.dtype) for a in operands]
        + [
            pltpu.VMEM((padded, width), bf16),
            pltpu.VMEM((hist, width, seq), f32),
            pltpu.VMEM((hist, seq, width), bf16),
        ]
        + [pltpu.VMEM(a.shape, a.dtype) for a in outs]
        + [
            pltpu.SemaphoreType.DMA((7 * hist + 8,)),
            pltpu.SemaphoreType.DMA((2 * hist + 12,)),
        ],
        compiler_params=params(60),
        cost_estimate=cost(30e9, 30e6),
        name="owner_backward",
    )(*operands)


def input_kernel(denc_ref, win_ref, dpre_ref, dk_ref, out_ref):
    width = denc_ref.shape[2]
    total = denc_ref[0].astype(f32) + dot_nt(dpre_ref[...], win_ref[:, : 3 * width])
    total = total + dot_nt(jnp.transpose(dk_ref[...]), win_ref[:, 3 * width :])
    out_ref[0] = total.astype(bf16)


def input_backward(denc, w_in, dpre, dk):
    hist, seq, width = denc.shape
    block = lambda a: pl.BlockSpec((1,) + a.shape[1:], lambda i: (i, 0, 0))
    return pl.pallas_call(
        input_kernel,
        grid=(hist,),
        in_specs=[
            block(denc),
            whole(w_in.shape),
            pl.BlockSpec((seq, 3 * width), lambda i: (i, 0)),
            pl.BlockSpec((width, seq), lambda i: (0, i)),
        ],
        out_specs=block(denc),
        out_shape=jax.ShapeDtypeStruct(denc.shape, bf16),
        compiler_params=params(60),
        cost_estimate=cost(6e9, 8e6),
        name="input_backward",
    )(denc, w_in, dpre, dk)


def owner_order(width):
    n_y, n_core, n_z, n_x = (lax.axis_size(a) for a in AXES)
    rows = width // (n_y * n_core * n_z * n_x)
    place = jnp.arange(width, dtype=jnp.int32)
    inner = place % rows
    place = place // rows
    z, place = place % n_z, place // n_z
    x, place = place % n_x, place // n_x
    y, d_core = place % n_y, place // n_y
    core = (lax.axis_index(AXES[1]) + d_core) % n_core
    y, x = (lax.axis_index(AXES[0]) + y) % n_y, (lax.axis_index(AXES[3]) + x) % n_x
    z = (lax.axis_index(AXES[2]) + z) % n_z
    source = (((y * n_core + core) * n_z + z) * n_x + x) * rows + inner
    return (source[:, None] == jnp.arange(width, dtype=jnp.int32)[None, :]).astype(bf16)


def return_orders(capacity):
    sizes = n_y, n_core, n_z, n_x = tuple(lax.axis_size(a) for a in AXES)
    slots = n_y * n_core * n_z * n_x * capacity
    place = jnp.arange(slots, dtype=jnp.int32)
    inner, block = place % capacity, place // capacity
    plane = n_y * n_x
    orders = []
    for sign, (d_core, d_z, d_plane) in (
        (1, (block // (plane * n_z), block // plane % n_z, block % plane)),
        (-1, (block % n_core, block // n_core % n_z, block // (n_core * n_z))),
    ):
        y, core, z, x = (
            (lax.axis_index(a) + sign * d + n) % n
            for a, d, n in zip(AXES, (d_plane // n_x, d_core, d_z, d_plane % n_x), sizes)
        )
        source = (((y * n_core + core) * n_z + z) * n_x + x) * capacity + inner
        orders.append((source[:, None] == place[None, :]).astype(bf16))
    return orders


def add_up(blocks):
    total = blocks[0].astype(f32)
    for block in blocks[1:]:
        total = total + block.astype(f32)
    return total


def core_stage(keep, send):
    return add_up(send_blocks([keep] + cut_rows(send, lax.axis_size(AXES[1]) - 1), AXES[1:2])).astype(bf16)


def send_blocks(blocks, axes):
    count = len(blocks)
    sizes = [lax.axis_size(a) for a in axes]
    parts = [blocks[0]]
    for d in range(1, count):
        pairs = []
        for c in range(count):
            there, stride, rest_c, rest_d = 0, 1, c, d
            for n in reversed(sizes):
                there += (rest_c + rest_d) % n * stride
                stride, rest_c, rest_d = stride * n, rest_c // n, rest_d // n
            pairs.append((c, there))
        parts.append(lax.ppermute(blocks[d], axes, pairs))
    return parts


def cut_rows(rows, count):
    step = rows.shape[0] // count
    return [rows[i * step : (i + 1) * step] for i in range(count)]


def local(histories, weight_in, weight_out, candidates, cotangent, owner_ids, hist_slot, lengths):
    devices = lax.axis_size(AXES)
    imp_rows, width = candidates.shape
    capacity = max(2, 2 * imp_rows // devices)
    slots = devices * capacity
    kept = width // lax.axis_size(AXES[1])
    after = lax.optimization_barrier

    n_y, n_core, n_z, n_x = (lax.axis_size(a) for a in AXES)
    core, line, plane = AXES[1:2], AXES[2:3], (AXES[0], AXES[3])
    send, pick = route(owner_ids, hist_slot, lengths, candidates, cotangent, devices, capacity)
    shaped = send.reshape(devices, capacity, send.shape[1])
    recv = lax.all_to_all(shaped, AXES, split_axis=0, concat_axis=0, tiled=True)
    recv = recv.reshape(slots, send.shape[1])
    perm = owner_order(width)
    leaving, arriving = return_orders(capacity)
    pick = dot_nn(arriving, pick).astype(bf16)
    enc, slope, slope_t, v, q, k, q_t, attn_t, grad, normed, nu, gi, xt, mt = layer_forward(
        histories, weight_in, weight_out, perm
    )
    state = (normed, nu, gi, v, k, q_t, attn_t, grad, slope, slope_t)
    d_query, d_enc, dpre, dk, keep, send = owner_backward(recv, enc, weight_out, state, mt, xt, kept)
    d_query = dot_nn(leaving, d_query).astype(bf16)
    rows = core_stage(keep, send)
    d_enc, rows, d_query = after((d_enc, rows, d_query))
    back = [cut_rows(b, n_z) for b in send_blocks(cut_rows(d_query, n_core), core)]
    back = [jnp.concatenate([b[d] for b in back], axis=0) for d in range(n_z)]
    d_inputs = input_backward(d_enc, weight_in, dpre, dk)
    back = send_blocks(back, line)
    parts = send_blocks(cut_rows(rows, n_y * n_x), plane)
    back, parts, d_inputs = after((back, parts, d_inputs))
    parts = send_blocks(cut_rows(add_up(parts).astype(bf16), n_z), line)
    back = [b.reshape(n_core, n_y * n_x, capacity, width) for b in back]
    back = [
        jnp.concatenate([b[:, i].reshape(n_core * capacity, width) for b in back], axis=0)
        for i in range(n_y * n_x)
    ]
    returned = jnp.concatenate(send_blocks(back, plane), axis=0)
    candidate_grad = lax.dot_general(
        pick, returned, (((0,), (0,)), ((), ())), preferred_element_type=f32
    ).astype(bf16)
    w_in_grad = add_up([p[:, width:] for p in parts])
    w_out_grad = add_up([p[:, :width] for p in parts])
    return d_inputs, candidate_grad, w_in_grad, w_out_grad


def solution(mesh):
    n_hash, n_dp = mesh.devices.shape
    fine = jax.sharding.Mesh(mesh.devices.reshape(n_hash // 2, 2, n_dp // 2, 2), AXES)
    return jax.shard_map(
        local,
        mesh=fine,
        in_specs=(
            P(AXES, None, None),
            P(),
            P(),
            P(AXES, None),
            P(AXES, None),
            P(AXES, None),
            P(AXES),
            P(AXES),
        ),
        out_specs=(
            P(AXES, None, None),
            P(AXES, None),
            P(AXES, None),
            P(AXES, None),
        ),
        check_vma=False,
    )
```

```python
import functools

import jax
import jax.numpy as jnp
from jax import lax
from jax.experimental import pallas as pl
from jax.experimental.pallas import tpu as pltpu
from jax.sharding import PartitionSpec as P

HEADS = 8
TILE = 128
META = 128
AXES = ("hash_hi", "core", "dp_hi", "dp_lo")
norm_eps = 1e-05
f32 = jnp.float32
bf16 = jnp.bfloat16
MIB = 1024 * 1024


def dot_nn(a, b):
    return lax.dot_general(a, b, (((1,), (0,)), ((), ())), preferred_element_type=f32)


def dot_nt(a, b):
    return lax.dot_general(a, b, (((1,), (1,)), ((), ())), preferred_element_type=f32)


def dot_tn(a, b):
    return lax.dot_general(a, b, (((0,), (0,)), ((), ())), preferred_element_type=f32)


def iota(shape, axis):
    return lax.broadcasted_iota(jnp.int32, shape, axis)


def silu_pair(half):
    t = jnp.tanh(half)
    u = 1.0 + t
    act = half * u
    return act, u + act * (1.0 - t)


def lane_masks(width, part):
    lane = iota((1, width), 1)
    return [((lane >= j * part) & (lane < (j + 1) * part)).astype(bf16) for j in range(width // part)]


def both_heads(pair, masks):
    return jnp.concatenate([pair * m for m in masks], axis=0)


def pick_lanes(stacked, head):
    rows = stacked.shape[0] // 2
    lane = iota((1, 2 * head), 1)
    return jnp.where(lane < head, stacked[:rows], stacked[rows:])


def params(mib):
    return pltpu.CompilerParams(dimension_semantics=("arbitrary",), vmem_limit_bytes=mib * MIB)


def whole(shape):
    return pl.BlockSpec(shape, lambda i: (0,) * len(shape))


def cost(flops, nbytes, trans=0):
    return pl.CostEstimate(flops=int(flops), bytes_accessed=int(nbytes), transcendentals=int(trans))


def route_kernel(devices, capacity, own_ref, slot_ref, len_ref, cand_ref, cot_ref, send_ref, pick_ref):
    rows, width = cand_ref.shape
    slots = devices * capacity
    own = own_ref[...]
    hot = (own == iota((devices, rows), 0)).astype(f32)
    before = (iota((rows, rows), 0) < iota((rows, rows), 1)).astype(f32).astype(bf16)
    earlier = dot_nn(hot.astype(bf16), before)
    position = jnp.sum(earlier * hot, axis=0, keepdims=True).astype(jnp.int32)
    target = own * capacity + position
    pick = (target == iota((slots, rows), 0)).astype(f32).astype(bf16)
    pick_ref[...] = pick
    send_ref[:, :width] = dot_nn(pick, cand_ref[...]).astype(bf16)
    send_ref[:, width : 2 * width] = dot_nn(pick, cot_ref[...]).astype(bf16)
    line = iota((META, rows), 0)
    meta = jnp.where(line == 0, slot_ref[...], jnp.where(line == 1, len_ref[...], 0))
    send_ref[:, 2 * width :] = dot_nt(pick, meta.astype(f32).astype(bf16)).astype(bf16)


def route(own, slot, length, cand, cot, devices, capacity):
    rows, width = cand.shape
    slots = devices * capacity
    line = whole((1, rows))
    return pl.pallas_call(
        functools.partial(route_kernel, devices, capacity),
        grid=(1,),
        in_specs=[line, line, line, whole(cand.shape), whole(cot.shape)],
        out_specs=[whole((slots, 2 * width + META)), whole((slots, rows))],
        out_shape=(
            jax.ShapeDtypeStruct((slots, 2 * width + META), bf16),
            jax.ShapeDtypeStruct((slots, rows), bf16),
        ),
        compiler_params=params(60),
        cost_estimate=cost(2e9, 4 * rows * width * 4),
        name="route",
    )(own.reshape(1, rows), slot.reshape(1, rows), length.reshape(1, rows), cand, cot)


def forward_kernel(
    x_ref, win_ref, wout_ref, perm_ref,
    enc_ref, slope_ref, slope_t_ref, v_ref, q_ref, k_ref, q_t_ref, attn_t_ref, grad_ref,
    normed_ref, nu_ref, gi_ref, xt_ref, mt_ref,
    gate_ref, mixed_ref, slope_u_ref,
):
    seq, width = x_ref.shape[1:]
    head = width // HEADS
    half_seq = seq // 2
    x = x_ref[0]
    for branch in range(4):
        cols = slice(branch * width, (branch + 1) * width)
        act, slope = silu_pair(0.5 * dot_nn(x, win_ref[:, cols]))
        if branch == 3:
            slope_t_ref[0] = jnp.transpose(0.5 * slope).astype(bf16)
        elif branch > 0:
            slope_ref[0, :, (branch - 1) * width : branch * width] = (0.5 * slope).astype(bf16)
        if branch == 0:
            gate_ref[...] = act
            slope_u_ref[...] = 0.5 * slope
        else:
            (v_ref, q_ref, k_ref)[branch - 1][0] = act.astype(bf16)
        if branch == 2:
            q_t_ref[0] = jnp.transpose(act).astype(bf16)
    masks = lane_masks(2 * head, head)
    scale = 0.5 * head**-0.5
    tri = iota((half_seq, half_seq), 0) >= iota((half_seq, half_seq), 1)
    zero = jnp.zeros((half_seq, half_seq), f32)
    for pair in range(HEADS // 2):
        cols = slice(pair * 2 * head, (pair + 1) * 2 * head)
        q_p = q_ref[0, :, cols] * jnp.asarray(scale, bf16)
        half = dot_nt(both_heads(q_p, masks), k_ref[0, :, cols])
        stack = []
        for j in range(2):
            h = 2 * pair + j
            top = silu_pair(half[j * seq : j * seq + half_seq, :half_seq])
            bot = silu_pair(half[j * seq + half_seq : (j + 1) * seq])
            full = []
            for a, b in zip(top, bot):
                a = jnp.concatenate([jnp.where(tri, a, 0.0), zero], axis=1)
                b = jnp.concatenate([b[:, :half_seq], jnp.where(tri, b[:, half_seq:], 0.0)], axis=1)
                full.append(jnp.concatenate([a, b], axis=0))
            stack.append(full[0].astype(bf16))
            attn_t_ref[0, h] = jnp.transpose(full[0]).astype(bf16)
            grad_ref[0, h] = full[1].astype(bf16)
        mixed = dot_nn(jnp.concatenate(stack, axis=0), v_ref[0, :, cols])
        mixed_ref[:, cols] = pick_lanes(mixed, head) * (1.0 / seq)
    mixed = mixed_ref[...]
    centred = mixed - jnp.mean(mixed, axis=1, keepdims=True)
    inv_std = lax.rsqrt(jnp.mean(centred * centred, axis=1, keepdims=True) + norm_eps)
    normed = centred * inv_std
    gate = gate_ref[...]
    merged = (normed * gate).astype(bf16)
    normed_ref[0] = normed.astype(bf16)
    nu_ref[0] = (normed * slope_u_ref[...]).astype(bf16)
    gi_ref[0] = (gate * inv_std).astype(bf16)
    enc_ref[0] = (x.astype(f32) + dot_nn(merged, wout_ref[...])).astype(bf16)
    perm = perm_ref[...]
    xt_ref[...] = dot_nt(perm, x).astype(bf16)
    mt_ref[...] = dot_nt(perm, merged).astype(bf16)


def layer_forward(x, w_in, w_out, perm):
    hist, seq, width = x.shape
    row = pl.BlockSpec((1, seq, width), lambda i: (i, 0, 0))
    wide = pl.BlockSpec((1, seq, 2 * width), lambda i: (i, 0, 0))
    column = pl.BlockSpec((1, width, seq), lambda i: (i, 0, 0))
    square = pl.BlockSpec((1, HEADS, seq, seq), lambda i: (i, 0, 0, 0))
    turned = pl.BlockSpec((width, seq), lambda i: (0, i))
    row_s = jax.ShapeDtypeStruct((hist, seq, width), bf16)
    column_s = jax.ShapeDtypeStruct((hist, width, seq), bf16)
    square_s = jax.ShapeDtypeStruct((hist, HEADS, seq, seq), bf16)
    turned_s = jax.ShapeDtypeStruct((width, hist * seq), bf16)
    return pl.pallas_call(
        forward_kernel,
        grid=(hist,),
        in_specs=[row, whole(w_in.shape), whole(w_out.shape), whole(perm.shape)],
        out_specs=[
            row, wide, column, row, row, row, column, square, square, row, row, row, turned, turned,
        ],
        out_shape=[
            row_s, jax.ShapeDtypeStruct((hist, seq, 2 * width), bf16), column_s, row_s, row_s, row_s,
            column_s, square_s, square_s, row_s, row_s, row_s, turned_s, turned_s,
        ],
        scratch_shapes=[pltpu.VMEM((seq, width), f32)] * 3,
        compiler_params=params(60),
        cost_estimate=cost(18e9, 24e6),
        name="forward",
    )(x, w_in, w_out, perm)


def group_slots(recv_ref, hist):
    slots, width = recv_ref.shape
    meta = recv_ref[:, width - META :].astype(f32)
    slot_h = meta[:, 0:1]
    valid = meta[:, 1:2] > 0.0
    lane = iota((slots, META), 1).astype(f32)
    hot = jnp.where(valid & (slot_h == lane), 1.0, 0.0)
    lower = (iota((slots, slots), 0) > iota((slots, slots), 1)).astype(f32).astype(bf16)
    rank = jnp.sum(dot_nn(lower, hot.astype(bf16)) * hot, axis=1, keepdims=True)
    starts, start = [], jnp.int32(0)
    begin = jnp.zeros((slots, 1), f32)
    for h in range(hist):
        starts.append(start)
        begin = jnp.where(slot_h == float(h), (start * TILE).astype(f32), begin)
        count = jnp.sum(hot[:, h : h + 1]).astype(jnp.int32)
        start = start + (count + (TILE - 1)) // TILE
    dest = jnp.where(valid, begin + rank, -1.0)
    eye = iota((slots, slots), 0) == iota((slots, slots), 1)
    dest_row = jnp.sum(jnp.where(eye, dest, 0.0), axis=0, keepdims=True).astype(jnp.int32)
    return dest.astype(jnp.int32), dest_row, starts, start


def target_tile(tile, starts, dest_row, recv_ref, enc_ref, grouped_ref, turned_ref):
    seq, width = enc_ref.shape[1:]
    head = width // HEADS
    masks = lane_masks(2 * head, head)
    scale = 0.5 * head**-0.5
    base = pl.multiple_of(tile * TILE, TILE)
    hist = jnp.int32(0)
    for start in starts[1:]:
        hist = hist + (tile >= start).astype(jnp.int32)
    choose = (iota((TILE, dest_row.shape[1]), 0) + base == dest_row).astype(f32).astype(bf16)
    rows = dot_nn(choose, recv_ref[...])
    q_all = rows[:, :width] * scale
    g_all = rows[:, width : 2 * width]
    q_t = jnp.transpose(q_all).astype(bf16)
    g_t = jnp.transpose(g_all).astype(bf16)
    q_all = q_all.astype(bf16)
    g_all = g_all.astype(bf16)
    length = rows[:, 2 * width + 1 : 2 * width + 2]
    positions = iota((TILE, seq), 1).astype(f32)
    weight = jnp.where(positions < length, 1.0 / jnp.maximum(length, 1.0), 0.0)
    for pair in range(HEADS // 2):
        cols = slice(pair * 2 * head, (pair + 1) * 2 * head)
        k_p = enc_ref[hist, :, cols]
        both = dot_nt(
            jnp.concatenate(
                [both_heads(q_all[:, cols], masks), both_heads(g_all[:, cols], masks)], axis=0
            ),
            k_p,
        )
        slopes = []
        for j in range(2):
            h = 2 * pair + j
            mine = slice(h * head, (h + 1) * head)
            act, slope = silu_pair(both[j * TILE : (j + 1) * TILE])
            d_attn = both[(2 + j) * TILE : (3 + j) * TILE]
            attn = (act * weight).astype(bf16)
            d_s = (d_attn * weight * slope).astype(bf16)
            turned_ref[hist, mine, :] += dot_nn(
                jnp.concatenate([g_t[mine], q_t[mine]], axis=1),
                jnp.concatenate([attn, d_s], axis=0),
            )
            slopes.append(d_s)
        d_q = pick_lanes(dot_nn(jnp.concatenate(slopes, axis=0), k_p), head)
        grouped_ref[pl.ds(base, TILE), cols] = (d_q * scale).astype(bf16)


def norm_backward(denc_ref, wout_ref, normed_ref, nu_ref, gi_ref, dmix_ref, dpre_ref):
    hist, seq, width = denc_ref.shape
    d_merged_all = dot_nt(denc_ref[...].reshape(hist * seq, width), wout_ref[...])
    for at in range(hist):
        here = slice(at * seq, (at + 1) * seq)
        d_merged = d_merged_all[here]
        dpre_ref[here, :width] = (d_merged * nu_ref[at].astype(f32)).astype(bf16)
        normed = normed_ref[at].astype(f32)
        d_norm = d_merged * gi_ref[at].astype(f32)
        d_mix = (
            d_norm
            - jnp.mean(d_norm, axis=1, keepdims=True)
            - normed * jnp.mean(d_norm * normed, axis=1, keepdims=True)
        )
        dmix_ref[at] = d_mix.astype(bf16)


def attention_backward(
    at, dmix_ref, v_ref, k_ref, q_t_ref, attn_t_ref, grad_ref, slope_ref, slope_t_ref, dpre_ref, dk_ref
):
    seq, width = dmix_ref.shape[1:]
    head = width // HEADS
    half_seq = seq // 2
    zero = jnp.zeros((half_seq, half_seq), bf16)
    here = slice(at * seq, (at + 1) * seq)
    masks = lane_masks(2 * head, head)
    scale = 0.5 * head**-0.5 / seq
    for pair in range(HEADS // 2):
        cols = slice(pair * 2 * head, (pair + 1) * 2 * head)
        d_p = dmix_ref[at, :, cols]
        v_p = v_ref[at, :, cols]
        top = dot_nt(both_heads(d_p[:half_seq], masks), v_p[:half_seq])
        bot = dot_nt(both_heads(d_p[half_seq:], masks), v_p)
        d_s = []
        for j in range(2):
            part = slice(j * half_seq, (j + 1) * half_seq)
            grad = grad_ref[at, 2 * pair + j]
            d_top = (top[part] * grad[:half_seq, :half_seq].astype(f32)).astype(bf16)
            d_bot = (bot[part] * grad[half_seq:].astype(f32)).astype(bf16)
            d_s.append(jnp.concatenate([jnp.concatenate([d_top, zero], axis=1), d_bot], axis=0))
        attn_t = jnp.concatenate([attn_t_ref[at, 2 * pair], attn_t_ref[at, 2 * pair + 1]], axis=0)
        d_v = pick_lanes(dot_nn(attn_t, d_p), head) * (1.0 / seq)
        d_q = pick_lanes(dot_nn(jnp.concatenate(d_s, axis=0), k_ref[at, :, cols]), head) * scale
        for branch, grad in ((0, d_v), (1, d_q)):
            old = slice(branch * width + pair * 2 * head, branch * width + (pair + 1) * 2 * head)
            new = slice(old.start + width, old.stop + width)
            dpre_ref[here, new] = (grad * slope_ref[at, :, old].astype(f32)).astype(bf16)
        for j in range(2):
            mine = slice((2 * pair + j) * head, (2 * pair + j + 1) * head)
            d_k = dot_nn(q_t_ref[at, mine], d_s[j]) * scale
            dk_ref[mine, here] = (d_k * slope_t_ref[at, mine].astype(f32)).astype(bf16)


def owner_kernel(*refs):
    n_in, n_out = 15, 6
    sources, outs, refs = refs[:n_in], refs[n_in : n_in + n_out], refs[n_in + n_out :]
    held, refs = refs[:n_in], refs[n_in:]
    (
        recv_ref, enc_ref, wout_ref, normed_ref, nu_ref, gi_ref, v_ref, k_ref, q_t_ref,
        attn_t_ref, grad_ref, slope_ref, slope_t_ref, mt_ref, xt_ref,
    ) = held
    grouped_ref, turned_ref, dmix_ref, dq_ref, denc_ref, dpre_ref, dk_ref, keep_ref, send_ref, sem_in, sem_out = refs
    dq_hbm, denc_hbm, dpre_hbm, dk_hbm, keep_hbm, send_hbm = outs
    hist, seq, width = enc_ref.shape
    slots, padded = recv_ref.shape[0], grouped_ref.shape[0]
    kept = keep_ref.shape[0]

    def load(i, n, at=None):
        source, dest = (sources[i], held[i]) if at is None else (sources[i].at[at], held[i].at[at])
        return pltpu.make_async_copy(source, dest, sem_in.at[n])

    first = [load(i, i) for i in range(6)]
    by_history = [[load(i, i + 7 * at, at) for i in range(6, 13)] for at in range(hist)]
    last = [load(i, 7 * hist + i - 7) for i in (13, 14)]
    for copy in first + sum(by_history, []) + last:
        copy.start()
    grouped_ref[...] = jnp.zeros_like(grouped_ref)
    turned_ref[...] = jnp.zeros_like(turned_ref)
    first[0].wait()
    dest, dest_row, starts, tiles = group_slots(recv_ref, hist)
    first[1].wait()

    def one_tile(tile, carry):
        target_tile(tile, starts, dest_row, recv_ref, enc_ref, grouped_ref, turned_ref)
        return carry

    lax.fori_loop(0, tiles, one_tile, 0)
    for h in range(hist):
        denc_ref[h] = jnp.transpose(turned_ref[h].astype(bf16))
    back = (dest == iota((slots, padded), 1)).astype(f32).astype(bf16)
    dq_ref[...] = dot_nn(back, grouped_ref[...]).astype(bf16)
    stores = []

    def store(source, dest):
        copy = pltpu.make_async_copy(source, dest, sem_out.at[len(stores)])
        copy.start()
        stores.append(copy)

    store(denc_ref, denc_hbm)
    store(dq_ref, dq_hbm)
    for copy in first[2:]:
        copy.wait()
    norm_backward(denc_ref, wout_ref, normed_ref, nu_ref, gi_ref, dmix_ref, dpre_ref)
    for at in range(hist):
        for copy in by_history[at]:
            copy.wait()
        attention_backward(
            at, dmix_ref, v_ref, k_ref, q_t_ref, attn_t_ref, grad_ref, slope_ref, slope_t_ref,
            dpre_ref, dk_ref,
        )
        here = pl.ds(at * seq, seq)
        store(dpre_ref.at[here, :], dpre_hbm.at[here, :])
        store(dk_ref.at[:, here], dk_hbm.at[:, here])
    for copy in last:
        copy.wait()
    for block in range(5):
        cols = slice(block * width, (block + 1) * width)
        if block == 0:
            part = dot_nn(mt_ref[...], denc_ref[...].reshape(hist * seq, width))
        elif block == 4:
            part = dot_nt(xt_ref[...], dk_ref[...])
        else:
            part = dot_nn(xt_ref[...], dpre_ref[:, (block - 1) * width : block * width])
        keep_ref[:, cols] = part[:kept].astype(bf16)
        send_ref[:, cols] = part[kept:].astype(bf16)
        store(keep_ref.at[:, cols], keep_hbm.at[:, cols])
        store(send_ref.at[:, cols], send_hbm.at[:, cols])
    for copy in stores:
        copy.wait()


def owner_backward(recv, enc, w_out, state, mt, xt, kept):
    hist, seq, width = enc.shape
    slots = recv.shape[0]
    rows = hist * seq
    padded = ((slots - hist) // TILE + hist) * TILE
    operands = (recv, enc, w_out) + state + (mt, xt)
    raw = pl.BlockSpec(memory_space=pl.ANY)
    outs = [
        jax.ShapeDtypeStruct((slots, width), bf16),
        jax.ShapeDtypeStruct(enc.shape, bf16),
        jax.ShapeDtypeStruct((rows, 3 * width), bf16),
        jax.ShapeDtypeStruct((width, rows), bf16),
        jax.ShapeDtypeStruct((kept, 5 * width), bf16),
        jax.ShapeDtypeStruct((width - kept, 5 * width), bf16),
    ]
    return pl.pallas_call(
        owner_kernel,
        grid=(1,),
        in_specs=[raw] * len(operands),
        out_specs=[raw] * len(outs),
        out_shape=outs,
        scratch_shapes=[pltpu.VMEM(a.shape, a.dtype) for a in operands]
        + [
            pltpu.VMEM((padded, width), bf16),
            pltpu.VMEM((hist, width, seq), f32),
            pltpu.VMEM((hist, seq, width), bf16),
        ]
        + [pltpu.VMEM(a.shape, a.dtype) for a in outs]
        + [
            pltpu.SemaphoreType.DMA((7 * hist + 8,)),
            pltpu.SemaphoreType.DMA((2 * hist + 12,)),
        ],
        compiler_params=params(60),
        cost_estimate=cost(30e9, 30e6),
        name="owner_backward",
    )(*operands)


def input_kernel(denc_ref, win_ref, dpre_ref, dk_ref, out_ref):
    width = denc_ref.shape[2]
    total = denc_ref[0].astype(f32) + dot_nt(dpre_ref[...], win_ref[:, : 3 * width])
    total = total + dot_nt(jnp.transpose(dk_ref[...]), win_ref[:, 3 * width :])
    out_ref[0] = total.astype(bf16)


def input_backward(denc, w_in, dpre, dk):
    hist, seq, width = denc.shape
    block = lambda a: pl.BlockSpec((1,) + a.shape[1:], lambda i: (i, 0, 0))
    return pl.pallas_call(
        input_kernel,
        grid=(hist,),
        in_specs=[
            block(denc),
            whole(w_in.shape),
            pl.BlockSpec((seq, 3 * width), lambda i: (i, 0)),
            pl.BlockSpec((width, seq), lambda i: (0, i)),
        ],
        out_specs=block(denc),
        out_shape=jax.ShapeDtypeStruct(denc.shape, bf16),
        compiler_params=params(60),
        cost_estimate=cost(6e9, 8e6),
        name="input_backward",
    )(denc, w_in, dpre, dk)


def owner_order(width):
    n_y, n_core, n_z, n_x = (lax.axis_size(a) for a in AXES)
    rows = width // (n_y * n_core * n_z * n_x)
    place = jnp.arange(width, dtype=jnp.int32)
    inner = place % rows
    place = place // rows
    z, place = place % n_z, place // n_z
    x, place = place % n_x, place // n_x
    y, d_core = place % n_y, place // n_y
    core = (lax.axis_index(AXES[1]) + d_core) % n_core
    y, x = (lax.axis_index(AXES[0]) + y) % n_y, (lax.axis_index(AXES[3]) + x) % n_x
    z = (lax.axis_index(AXES[2]) + z) % n_z
    source = (((y * n_core + core) * n_z + z) * n_x + x) * rows + inner
    return (source[:, None] == jnp.arange(width, dtype=jnp.int32)[None, :]).astype(bf16)


def return_orders(capacity):
    sizes = n_y, n_core, n_z, n_x = tuple(lax.axis_size(a) for a in AXES)
    slots = n_y * n_core * n_z * n_x * capacity
    place = jnp.arange(slots, dtype=jnp.int32)
    inner, block = place % capacity, place // capacity
    plane = n_y * n_x
    orders = []
    for sign, (d_core, d_z, d_plane) in (
        (1, (block // (plane * n_z), block // plane % n_z, block % plane)),
        (-1, (block % n_core, block // n_core % n_z, block // (n_core * n_z))),
    ):
        y, core, z, x = (
            (lax.axis_index(a) + sign * d + n) % n
            for a, d, n in zip(AXES, (d_plane // n_x, d_core, d_z, d_plane % n_x), sizes)
        )
        source = (((y * n_core + core) * n_z + z) * n_x + x) * capacity + inner
        orders.append((source[:, None] == place[None, :]).astype(bf16))
    return orders


def add_up(blocks):
    total = blocks[0].astype(f32)
    for block in blocks[1:]:
        total = total + block.astype(f32)
    return total


def core_stage(keep, send):
    return add_up(send_blocks([keep] + cut_rows(send, lax.axis_size(AXES[1]) - 1), AXES[1:2])).astype(bf16)


def send_blocks(blocks, axes):
    count = len(blocks)
    sizes = [lax.axis_size(a) for a in axes]
    parts = [blocks[0]]
    for d in range(1, count):
        pairs = []
        for c in range(count):
            there, stride, rest_c, rest_d = 0, 1, c, d
            for n in reversed(sizes):
                there += (rest_c + rest_d) % n * stride
                stride, rest_c, rest_d = stride * n, rest_c // n, rest_d // n
            pairs.append((c, there))
        parts.append(lax.ppermute(blocks[d], axes, pairs))
    return parts


def cut_rows(rows, count):
    step = rows.shape[0] // count
    return [rows[i * step : (i + 1) * step] for i in range(count)]


def local(histories, weight_in, weight_out, candidates, cotangent, owner_ids, hist_slot, lengths):
    devices = lax.axis_size(AXES)
    imp_rows, width = candidates.shape
    capacity = max(2, 2 * imp_rows // devices)
    slots = devices * capacity
    kept = width // lax.axis_size(AXES[1])
    after = lax.optimization_barrier

    n_y, n_core, n_z, n_x = (lax.axis_size(a) for a in AXES)
    core, line, plane = AXES[1:2], AXES[2:3], (AXES[0], AXES[3])
    send, pick = route(owner_ids, hist_slot, lengths, candidates, cotangent, devices, capacity)
    shaped = send.reshape(devices, capacity, send.shape[1])
    recv = lax.all_to_all(shaped, AXES, split_axis=0, concat_axis=0, tiled=True)
    recv = recv.reshape(slots, send.shape[1])
    perm = owner_order(width)
    leaving, arriving = return_orders(capacity)
    pick = dot_nn(arriving, pick).astype(bf16)
    enc, slope, slope_t, v, q, k, q_t, attn_t, grad, normed, nu, gi, xt, mt = layer_forward(
        histories, weight_in, weight_out, perm
    )
    state = (normed, nu, gi, v, k, q_t, attn_t, grad, slope, slope_t)
    d_query, d_enc, dpre, dk, keep, send = owner_backward(recv, enc, weight_out, state, mt, xt, kept)
    d_query = dot_nn(leaving, d_query).astype(bf16)
    rows = core_stage(keep, send)
    d_enc, rows, d_query = after((d_enc, rows, d_query))
    back = [cut_rows(b, n_z) for b in send_blocks(cut_rows(d_query, n_core), core)]
    back = [jnp.concatenate([b[d] for b in back], axis=0) for d in range(n_z)]
    d_inputs = input_backward(d_enc, weight_in, dpre, dk)
    back = send_blocks(back, line)
    parts = send_blocks(cut_rows(rows, n_y * n_x), plane)
    back, parts, d_inputs = after((back, parts, d_inputs))
    parts = send_blocks(cut_rows(add_up(parts).astype(bf16), n_z), line)
    back = [b.reshape(n_core, n_y * n_x, capacity, width) for b in back]
    back = [
        jnp.concatenate([b[:, i].reshape(n_core * capacity, width) for b in back], axis=0)
        for i in range(n_y * n_x)
    ]
    returned = jnp.concatenate(send_blocks(back, plane), axis=0)
    candidate_grad = lax.dot_general(
        pick, returned, (((0,), (0,)), ((), ())), preferred_element_type=f32
    ).astype(bf16)
    w_in_grad = add_up([p[:, width:] for p in parts])
    w_out_grad = add_up([p[:, :width] for p in parts])
    return d_inputs, candidate_grad, w_in_grad, w_out_grad


def solution(mesh):
    n_hash, n_dp = mesh.devices.shape
    fine = jax.sharding.Mesh(mesh.devices.reshape(n_hash // 2, 2, n_dp // 2, 2), AXES)
    return jax.shard_map(
        local,
        mesh=fine,
        in_specs=(
            P(AXES, None, None),
            P(),
            P(),
            P(AXES, None),
            P(AXES, None),
            P(AXES, None),
            P(AXES),
            P(AXES),
        ),
        out_specs=(
            P(AXES, None, None),
            P(AXES, None),
            P(AXES, None),
            P(AXES, None),
        ),
        check_vma=False,
    )
```
